32 devices in a mesh: dp: 8 (over y, x, core), seq: 4 (over z).
Axes of the slice: x: 2, y: 2, z: 4, core: 2. Of those that a mesh axis runs over, the one named last changes fastest.
Arguments:
- hidden_in: bfloat16 [16384, 2048], P(('dp', 'seq')), may hold values from -6 to 6
- out_grad: bfloat16 [16384, 2048], P(('dp', 'seq')), may hold values from -6 to 6
- seq_lengths: int32 [8, 2], P('dp'), may hold values from 0 to 2048, as said below
- seq_counts: int32 [8], P('dp'), may hold values from 1 to 2, as said below
- segment_ids: int32 [8, 2048], P('dp'), may hold values from 0 to 1, as said below
- qkv_weight: float32 [2048, 2560], P(('dp', 'seq')), may hold values from -0.125 to 0.125
- qkv_m: float32 [2048, 2560], P(('dp', 'seq'))
- qkv_v: float32 [2048, 2560], P(('dp', 'seq'))
- out_weight: float32 [2048, 2048], P(('dp', 'seq')), may hold values from -1 to 1
- out_m: float32 [2048, 2048], P(('dp', 'seq'))
- out_v: float32 [2048, 2048], P(('dp', 'seq'))
- gate_up_weight: float32 [2048, 11264], P(('dp', 'seq')), may hold values from -0.125 to 0.125
- gate_up_m: float32 [2048, 11264], P(('dp', 'seq'))
- gate_up_v: float32 [2048, 11264], P(('dp', 'seq'))
- down_weight: float32 [5632, 2048], P(('dp', 'seq')), may hold values from -0.078125 to 0.078125
- down_m: float32 [5632, 2048], P(('dp', 'seq'))
- down_v: float32 [5632, 2048], P(('dp', 'seq'))
- norm_gains: float32 [2, 2048], P(None, ('dp', 'seq')), may hold values from 0.4 to 3.2, as said below
- gain_m: float32 [2, 2048], P(None, ('dp', 'seq'))
- gain_v: float32 [2, 2048], P(None, ('dp', 'seq'))
Outputs:
- block_out: bfloat16 [16384, 2048], P(('dp', 'seq'))
- input_grad: float32 [16384, 2048], P(('dp', 'seq'))
- grad_norm: float32 [], replicated
- new_qkv: float32 [2048, 2560], P(('dp', 'seq'))
- new_qkv_m: float32 [2048, 2560], P(('dp', 'seq'))
- new_qkv_v: float32 [2048, 2560], P(('dp', 'seq'))
- new_out: float32 [2048, 2048], P(('dp', 'seq'))
- new_out_m: float32 [2048, 2048], P(('dp', 'seq'))
- new_out_v: float32 [2048, 2048], P(('dp', 'seq'))
- new_gate_up: float32 [2048, 11264], P(('dp', 'seq'))
- new_gate_up_m: float32 [2048, 11264], P(('dp', 'seq'))
- new_gate_up_v: float32 [2048, 11264], P(('dp', 'seq'))
- new_down: float32 [5632, 2048], P(('dp', 'seq'))
- new_down_m: float32 [5632, 2048], P(('dp', 'seq'))
- new_down_v: float32 [5632, 2048], P(('dp', 'seq'))
- new_gains: float32 [2, 2048], P(None, ('dp', 'seq'))
- new_gain_m: float32 [2, 2048], P(None, ('dp', 'seq'))
- new_gain_v: float32 [2, 2048], P(None, ('dp', 'seq'))
The draws below stay inside these ranges and needn't reach their ends.
Inputs may be any that keep to these rules, and one draw needn't show every extreme that they name: `seq_lengths`: row g is (1024, 1024) for a group of two sequences and (2048, 0) for a group of one; every draw has groups of both kinds. `seq_counts`: agrees with seq_lengths: the number of its nonzero entries. `segment_ids`: agrees with seq_lengths: token t of group g lies in sequence j where the sum of seq_lengths[g, i] over i < j is at most t and t is below that sum plus seq_lengths[g, j]. `norm_gains`: Positive.
All inputs are finite; a program needn't handle non-finite values.
Results may differ from the reference program's by a relative error of at most 0.014.
The reference program's roundings to bfloat16 on the way count: a program that leaves them out, or rounds other values in their place, can miss the bound.
Values may be sent and summed in bfloat16 or wider, within the bound.
A program may use at most 448 MiB of HBM per device.

```python
import math
import jax
import jax.numpy as jnp
from jax import lax

D = 2048
HEADS = 32
KV_HEADS = 4
HD = 64
FF = 5632
SEQ_MIN = 1024
STEP = 10
QD = 2048
QKV = 2560
GROUP_TOK = 2048
GROUPS = 8
TOK_DEV = 512
TOKENS = 16384


CLIP_NORM = 1.0


BETA_ONE = 0.9


BETA_TWO = 0.999


def group_layout(key):
    first_key, second_key, third_key = jax.random.split(key, 3)
    counts = 1 + jax.random.randint(first_key, (GROUPS,), 0, 2)
    single = jax.random.randint(second_key, (), 0, GROUPS)
    double = (single + 1 + jax.random.randint(third_key, (), 0, GROUPS - 1)) % GROUPS
    group_idx = jnp.arange(GROUPS, dtype=jnp.int32)
    counts = jnp.where(group_idx == single, 1, jnp.where(group_idx == double, 2, counts)).astype(jnp.int32)
    lengths = jnp.stack([jnp.where(counts == 1, 2 * SEQ_MIN, SEQ_MIN), jnp.where(counts == 1, 0, SEQ_MIN)], -1).astype(jnp.int32)
    tokens = jnp.arange(GROUP_TOK, dtype=jnp.int32)
    segments = jnp.where((counts[:, None] == 2) & (tokens[None, :] >= SEQ_MIN), 1, 0).astype(jnp.int32)
    return (lengths, counts, segments)


def draw_seq_lengths(key, part):
    lengths, counts, segments = group_layout(key)
    return lengths


def draw_seq_counts(key, part):
    lengths, counts, segments = group_layout(key)
    return counts


def draw_segment_ids(key, part):
    lengths, counts, segments = group_layout(key)
    return segments


def grad_units():
    q_width = HEADS * HD
    kv_width = KV_HEADS * HD
    length_mean = 1.5 * SEQ_MIN
    spread_share = math.sqrt(2.7 * math.log(length_mean) / length_mean)
    out_fan = max(4, 16 * q_width // SEQ_MIN)
    back_size = 1.2 * math.sqrt(D / out_fan)
    query_size = back_size * spread_share
    keyval_size = query_size * math.sqrt(HEADS / KV_HEADS)
    attended_size = 1.2 * spread_share
    gated_size = 0.36
    down_size = 0.6
    normed_size = math.sqrt(q_width / D * query_size ** 2 + 2 * kv_width / D * keyval_size ** 2)
    total_size = D * (q_width * query_size ** 2 + 2 * kv_width * keyval_size ** 2) + q_width * D * attended_size ** 2 + 2 * D * FF * gated_size ** 2 + FF * D * down_size ** 2 + D * (normed_size ** 2 + 1.0)
    unit_size = CLIP_NORM / math.sqrt(total_size)
    return (unit_size, query_size, keyval_size, attended_size, gated_size, down_size, normed_size)


def first_moment(key, scales):
    noise_vals = jax.random.normal(key, scales.shape, jnp.float32)
    return noise_vals * scales * ((1.0 - BETA_ONE) / BETA_ONE)


def second_moment(key, scales):
    factor = jnp.exp(jax.random.uniform(key, scales.shape, jnp.float32, math.log(0.5), math.log(8.0)))
    return factor * scales * scales * ((1.0 - BETA_TWO) / BETA_TWO)


def qkv_scales():
    unit_size, query_size, keyval_size, attended_size, gated_size, down_size, normed_size = grad_units()
    columns = jnp.arange(QKV, dtype=jnp.int32)
    per_column = jnp.where(columns < QD, query_size, keyval_size) * unit_size
    return jnp.broadcast_to(per_column[None, :], (D, QKV)).astype(jnp.float32)


def plain_scales(shape, which):
    sizes = grad_units()
    return jnp.full(shape, sizes[0] * sizes[which], jnp.float32)


def gain_scales():
    sizes = grad_units()
    per_row = jnp.array([sizes[6], 1.0], jnp.float32) * sizes[0]
    return jnp.broadcast_to(per_row[:, None], (2, D)).astype(jnp.float32)


def draw_qkv_m(key, part):
    key = jax.random.fold_in(key, 21)
    return first_moment(key, qkv_scales())


def draw_qkv_v(key, part):
    key = jax.random.fold_in(key, 22)
    return second_moment(key, qkv_scales())


def draw_out_m(key, part):
    key = jax.random.fold_in(key, 23)
    return first_moment(key, plain_scales((QD, D), 3))


def draw_out_v(key, part):
    key = jax.random.fold_in(key, 24)
    return second_moment(key, plain_scales((QD, D), 3))


def draw_gate_up_m(key, part):
    key = jax.random.fold_in(key, 25)
    return first_moment(key, plain_scales((D, 2 * FF), 4))


def draw_gate_up_v(key, part):
    key = jax.random.fold_in(key, 26)
    return second_moment(key, plain_scales((D, 2 * FF), 4))


def draw_down_m(key, part):
    key = jax.random.fold_in(key, 27)
    return first_moment(key, plain_scales((FF, D), 5))


def draw_down_v(key, part):
    key = jax.random.fold_in(key, 28)
    return second_moment(key, plain_scales((FF, D), 5))


def draw_gain_m(key, part):
    key = jax.random.fold_in(key, 29)
    return first_moment(key, gain_scales())


def draw_gain_v(key, part):
    key = jax.random.fold_in(key, 30)
    return second_moment(key, gain_scales())


def draw_norm_gains(key, part):
    key = jax.random.fold_in(key, 11)
    seq_devices = GROUP_TOK // TOK_DEV
    all_devices = GROUPS * seq_devices
    feature = jnp.arange(D, dtype=jnp.int32)
    shard_rank = feature // (D // all_devices)
    seq_place = (shard_rank % seq_devices).astype(jnp.float32) / max(seq_devices - 1, 1)
    dp_place = (shard_rank // seq_devices).astype(jnp.float32) / max(GROUPS - 1, 1)
    rise_log = math.log(3.0)
    base_level = 0.6
    baseline = base_level * jnp.exp(0.5 * rise_log * (seq_place + dp_place))
    roughness = jnp.exp(jax.random.uniform(key, (2, D), jnp.float32, math.log(0.8), math.log(1.25)))
    return baseline[None, :] * roughness


def spiked(values, own_key, source, target, blocks, factor):
    owner, partner = [(jnp.arange(values.shape[axis_at]) // (values.shape[axis_at] // blocks)).reshape([-1 if axis == axis_at else 1 for axis in range(values.ndim)]) for axis_at in (source, target)]
    chosen = jax.random.permutation(own_key, blocks)[partner]
    strong = (owner == chosen) | (owner == (partner + blocks // 2) % blocks)
    return jnp.where(strong, factor * values, values)


def shard_levels(key, extent, shards, least, high):
    loudness = 1.0
    for axis_at, blocks in shards:
        draws = jax.random.uniform(jax.random.fold_in(jax.random.fold_in(key, 6), axis_at), (blocks,), jnp.float32, least / len(shards), high / len(shards))
        loudness = loudness * jnp.repeat(jnp.exp(draws), extent[axis_at] // blocks).reshape((-1,) + (1,) * (len(extent) - 1 - axis_at))
    return loudness


def noise(own_key, dims, width, most, shards=(), held_as=jnp.bfloat16):
    values = jax.random.normal(own_key, dims, jnp.float32) * width
    if len(shards) > 0:
        values = shard_levels(own_key, dims, shards, -0.22, 0.18) * values
    return jnp.clip(values, min=-most, max=most).astype(held_as)


def bell_draw_with(own_key, dims, deviation, reach, pieces, heavy, held_as=jnp.bfloat16):
    values = deviation * jax.random.normal(own_key, dims, jnp.float32)
    if pieces:
        values = values * shard_levels(own_key, dims, pieces, -0.22, 0.18)
    return jnp.clip(spiked(values, jax.random.fold_in(own_key, 3), *heavy), -reach, reach).astype(held_as)


def setup_inputs(seed: int = 0) -> dict:
    key_of = jax.random.split(jax.random.key(seed), 21)
    hidden_in = bell_draw_with(key_of[0], (TOKENS, D), 1.0, 6.0, ((0, 32),), (0, 1, 32, 2.75))
    out_grad = noise(key_of[1], (TOKENS, D), 1.0, 6.0, ((0, 32),))
    seq_lengths = draw_seq_lengths(jax.random.fold_in(key_of[20], 71), 0)
    seq_counts = draw_seq_counts(jax.random.fold_in(key_of[20], 71), 0)
    segment_ids = draw_segment_ids(jax.random.fold_in(key_of[20], 71), 0)
    qkv_weight = noise(key_of[5], (D, QKV), D ** -0.5, 0.125, ((0, 32),), jnp.float32)
    qkv_m = draw_qkv_m(jax.random.fold_in(key_of[20], 71), 0)
    qkv_v = draw_qkv_v(jax.random.fold_in(key_of[20], 71), 0)
    out_weight = noise(key_of[8], (QD, D), (max(4, 16 * QD // SEQ_MIN)) ** -0.5, 1.0, ((0, 32),), jnp.float32)
    out_m = draw_out_m(jax.random.fold_in(key_of[20], 71), 0)
    out_v = draw_out_v(jax.random.fold_in(key_of[20], 71), 0)
    gate_up_weight = noise(key_of[11], (D, 2 * FF), D ** -0.5, 0.125, ((0, 32),), jnp.float32)
    gate_up_m = draw_gate_up_m(jax.random.fold_in(key_of[20], 71), 0)
    gate_up_v = draw_gate_up_v(jax.random.fold_in(key_of[20], 71), 0)
    down_weight = noise(key_of[14], (FF, D), FF ** -0.5, 0.078125, ((0, 32),), jnp.float32)
    down_m = draw_down_m(jax.random.fold_in(key_of[20], 71), 0)
    down_v = draw_down_v(jax.random.fold_in(key_of[20], 71), 0)
    norm_gains = draw_norm_gains(jax.random.fold_in(key_of[20], 71), 0)
    gain_m = draw_gain_m(jax.random.fold_in(key_of[20], 71), 0)
    gain_v = draw_gain_v(jax.random.fold_in(key_of[20], 71), 0)
    return dict(hidden_in=hidden_in, out_grad=out_grad, seq_lengths=seq_lengths, seq_counts=seq_counts, segment_ids=segment_ids, qkv_weight=qkv_weight, qkv_m=qkv_m, qkv_v=qkv_v, out_weight=out_weight, out_m=out_m, out_v=out_v, gate_up_weight=gate_up_weight, gate_up_m=gate_up_m, gate_up_v=gate_up_v, down_weight=down_weight, down_m=down_m, down_v=down_v, norm_gains=norm_gains, gain_m=gain_m, gain_v=gain_v)


@jax.custom_vjp
def low(v):
    return lax.optimization_barrier(v.astype(jnp.bfloat16)).astype(jnp.float32)

@jax.custom_vjp
def low_back(v):
    return v

def low_keep(v):
    return (low(v), None)

def low_pass(kept, grad):
    return (grad,)

def back_keep(v):
    return (v, None)

def back_low(kept, grad):
    return (low(grad),)
low.defvjp(low_keep, low_pass)
low_back.defvjp(back_keep, back_low)
NORM_EPS = 1e-05
ROPE_BASE = 10000.0
CLIP_NORM = 1.0
BETA_ONE = 0.9
BETA_TWO = 0.999
ADAM_EPS = 1e-08
WEIGHT_DECAY = 0.1
MASKED = -1e+30

def exact_dot(left, right):
    return jnp.dot(left, right, precision=lax.Precision.HIGHEST, preferred_element_type=jnp.float32)

def rope_tables(positions):
    half_dim = HD // 2
    inverse = jnp.exp(-(2.0 * jnp.arange(half_dim, dtype=jnp.float32) / HD) * jnp.log(ROPE_BASE))
    angles = positions.astype(jnp.float32)[:, None] * inverse[None, :]
    return (jnp.cos(angles)[:, None, :], jnp.sin(angles)[:, None, :])

def rotate(vector, cos_table, sin_table):
    half_dim = vector.shape[-1] // 2
    first_half, second_half = (vector[..., :half_dim], vector[..., half_dim:])
    return jnp.concatenate([first_half * cos_table - second_half * sin_table, second_half * cos_table + first_half * sin_table], -1)

def allowed_mask(row_ids, seg_rows, seg_all, seq_count):
    col_ids = jnp.arange(seg_all.shape[0], dtype=jnp.int32)
    earlier = (col_ids[None, :] < row_ids[:, None]) & (seg_all[None, :] == seg_rows[:, None]) & (seg_all[None, :] < seq_count)
    return earlier | (col_ids[None, :] == row_ids[:, None])

def attend_head(query_one, key_one, value_one, allowed):
    scores = low_back(exact_dot(query_one, key_one.T)) * HD ** (-0.5)
    scores = jnp.where(allowed, scores, MASKED)
    row_max = lax.optimization_barrier(jnp.max(scores, -1, keepdims=True))
    exp_vals = jnp.exp(scores - row_max)
    probability = exp_vals / lax.optimization_barrier(jnp.sum(exp_vals, -1, keepdims=True))
    return exact_dot(low(probability), value_one)

def block_forward(rows_in, masters, cos_table, sin_table, allowed):
    w_qkv, w_out, w_gu, w_down, w_gain = [low(weight_in) for weight_in in masters]
    q_width = HEADS * HD
    kv_width = KV_HEADS * HD
    inv_rms = lax.rsqrt(lax.optimization_barrier(jnp.mean(rows_in * rows_in, -1, keepdims=True)) + NORM_EPS)
    normed = low(rows_in * inv_rms * w_gain[0])
    qkv_out = exact_dot(normed, w_qkv)
    query_raw = low_back(qkv_out[:, :q_width])
    key_raw = low_back(qkv_out[:, q_width:q_width + kv_width])
    value_raw = low_back(qkv_out[:, q_width + kv_width:])
    query_rot = low(rotate(query_raw.reshape(GROUP_TOK, HEADS, HD), cos_table, sin_table))
    key_rot = low(rotate(key_raw.reshape(GROUP_TOK, KV_HEADS, HD), cos_table, sin_table))
    value_rows = low(value_raw.reshape(GROUP_TOK, KV_HEADS, HD))
    head_share = HEADS // KV_HEADS
    query_heads = jnp.moveaxis(query_rot, 1, 0)
    key_heads = jnp.repeat(jnp.moveaxis(key_rot, 1, 0), head_share, axis=0)
    value_heads = jnp.repeat(jnp.moveaxis(value_rows, 1, 0), head_share, axis=0)

    def one_head(query_one, key_one, value_one):
        return attend_head(query_one, key_one, value_one, allowed)
    checked = jax.checkpoint(one_head)
    head_outs = lax.map(lambda group_item: checked(group_item[0], group_item[1], group_item[2]), (query_heads, key_heads, value_heads))
    attended = jnp.moveaxis(head_outs, 0, 1).reshape(GROUP_TOK, q_width)
    attended = low(low_back(attended))
    mid_rows = rows_in + low_back(exact_dot(attended, w_out))
    inv_two = lax.rsqrt(lax.optimization_barrier(jnp.mean(mid_rows * mid_rows, -1, keepdims=True)) + NORM_EPS)
    inner_rows = low(mid_rows * inv_two * w_gain[1])
    gate_up = exact_dot(inner_rows, w_gu)
    gate_vals = low_back(gate_up[:, :FF])
    up_vals = low_back(gate_up[:, FF:])
    hidden = low(jax.nn.silu(gate_vals) * up_vals)
    return mid_rows + low_back(exact_dot(hidden, w_down))

def adam_update(weight, first_mom, second_mom, gradient, clip_factor, rate, decay):
    step_grad = gradient * clip_factor
    first_new = BETA_ONE * first_mom + (1.0 - BETA_ONE) * step_grad
    second_new = BETA_TWO * second_mom + (1.0 - BETA_TWO) * step_grad * step_grad
    mean_hat = first_new / (1.0 - BETA_ONE ** STEP)
    square_hat = second_new / (1.0 - BETA_TWO ** STEP)
    weight_new = weight - rate * (mean_hat / (jnp.sqrt(square_hat) + ADAM_EPS) + decay * weight)
    return (weight_new, first_new, second_new)

def reference(hidden_in, out_grad, seq_lengths, seq_counts, segment_ids, qkv_weight, qkv_m, qkv_v, out_weight, out_m, out_v, gate_up_weight, gate_up_m, gate_up_v, down_weight, down_m, down_v, norm_gains, gain_m, gain_v):
    masters = (qkv_weight, out_weight, gate_up_weight, down_weight, norm_gains)
    x_groups = hidden_in.astype(jnp.float32).reshape(GROUPS, GROUP_TOK, D)
    c_groups = out_grad.astype(jnp.float32).reshape(GROUPS, GROUP_TOK, D)

    def per_group(carry, group_item):
        rows_in, cotangent, lengths, seq_count, segments = group_item
        starts = jnp.cumsum(lengths, dtype=jnp.int32) - lengths
        positions = jnp.arange(GROUP_TOK, dtype=jnp.int32) - starts[segments]
        cos_table, sin_table = rope_tables(positions)
        token_ids = jnp.arange(GROUP_TOK, dtype=jnp.int32)
        allowed = allowed_mask(token_ids, segments, segments, seq_count)

        def forward(rows_x, *weights):
            return block_forward(rows_x, weights, cos_table, sin_table, allowed)
        result, pull = jax.vjp(forward, rows_in, *masters)
        grads = pull(cotangent)
        carry = tuple((acc + new_grad for acc, new_grad in zip(carry, grads[1:])))
        return (carry, (result.astype(jnp.bfloat16), grads[0]))
    zero_sums = tuple((jnp.zeros(weight_in.shape, jnp.float32) for weight_in in masters))
    totals, (group_outs, group_grads) = lax.scan(per_group, zero_sums, (x_groups, c_groups, seq_lengths, seq_counts, segment_ids))
    g_qkv, g_out, g_gu, g_down, g_gains = totals
    total_sq = jnp.sum(g_qkv * g_qkv) + jnp.sum(g_out * g_out) + jnp.sum(g_gu * g_gu) + jnp.sum(g_down * g_down) + jnp.sum(g_gains * g_gains)
    grad_norm = jnp.sqrt(total_sq)
    clip_factor = jnp.minimum(1.0, CLIP_NORM / (grad_norm + 1e-06))
    new_qkv, new_qkv_m, new_qkv_v = adam_update(qkv_weight, qkv_m, qkv_v, g_qkv, clip_factor, 0.06, WEIGHT_DECAY)
    new_out, new_out_m, new_out_v = adam_update(out_weight, out_m, out_v, g_out, clip_factor, 0.4, WEIGHT_DECAY)
    new_gu, new_gu_m, new_gu_v = adam_update(gate_up_weight, gate_up_m, gate_up_v, g_gu, clip_factor, 0.06, WEIGHT_DECAY)
    new_down, new_down_m, new_down_v = adam_update(down_weight, down_m, down_v, g_down, clip_factor, 0.06, WEIGHT_DECAY)
    new_gains, new_gain_m, new_gain_v = adam_update(norm_gains, gain_m, gain_v, g_gains, clip_factor, 0.6, 0.0)
    block_out = group_outs.reshape(TOKENS, D)
    input_grad = group_grads.reshape(TOKENS, D)
    return (block_out, input_grad, grad_norm, new_qkv, new_qkv_m, new_qkv_v, new_out, new_out_m, new_out_v, new_gu, new_gu_m, new_gu_v, new_down, new_down_m, new_down_v, new_gains, new_gain_m, new_gain_v)
```

```python
import jax
import jax.numpy as jnp
from jax import lax
from jax.experimental import pallas as pl
from jax.experimental.pallas import tpu as pltpu
from jax.sharding import PartitionSpec as P

HEADS = 32
KV_HEADS = 4
HD = 64
FF = 5632
STEP = 10


NORM_EPS = 1e-05
ROPE_BASE = 10000.0
CLIP_NORM = 1.0
BETA_ONE = 0.9
BETA_TWO = 0.999
ADAM_EPS = 1e-08
WEIGHT_DECAY = 0.1
MASKED = -1e30


def matmul(left, right):
    return jnp.dot(left, right, preferred_element_type=jnp.float32)


def contract(left, right, left_dim, right_dim):
    return lax.dot_general(
        left, right, (((left_dim,), (right_dim,)), ((), ())), preferred_element_type=jnp.float32
    )


def rope_tables(positions):
    half_dim = HD // 2
    inverse = jnp.exp(-(2.0 * jnp.arange(half_dim, dtype=jnp.float32) / HD) * jnp.log(ROPE_BASE))
    angles = inverse[:, None] * positions.astype(jnp.float32)[None, :]
    return (jnp.cos(angles), jnp.sin(angles))


def rotate(rows, cos_table, sin_table):
    tokens = rows.shape[1]
    split = rows.reshape(-1, 2, HD // 2, tokens)
    first, second = (split[:, 0], split[:, 1])
    return jnp.stack(
        [first * cos_table - second * sin_table, second * cos_table + first * sin_table], 1
    ).reshape(rows.shape)


def norm_forward(rows_in, gain_row):
    inv_rms = lax.rsqrt(jnp.mean(rows_in * rows_in, axis=-1, keepdims=True) + NORM_EPS)
    return (inv_rms, rows_in * inv_rms * gain_row)


def norm_backward(rows_in, inv_rms, gain_row, gradient):
    weighted = gain_row * gradient
    back_rows = inv_rms * weighted - rows_in * inv_rms**3 * jnp.mean(
        weighted * rows_in, axis=-1, keepdims=True
    )
    return (back_rows, jnp.sum(gradient * rows_in * inv_rms, axis=0))


LOG2E = 1.4426950408889634
SCORE_SCALE = HD ** (-0.5)


def transposed(block):
    return block.astype(jnp.float32).T.astype(block.dtype)


def causal(tokens, valid):
    key_ids = lax.broadcasted_iota(jnp.int32, (tokens, tokens), 0)
    row_ids = lax.broadcasted_iota(jnp.int32, (tokens, tokens), 1)
    return (key_ids == row_ids) | ((key_ids < row_ids) & (valid > 0))


def forward_kernel(info, q_ref, k_ref, v_ref, o_ref, full_ref, lse_ref, k_rows):
    tokens = q_ref.shape[1]
    share = HEADS // KV_HEADS
    blocks, valid = (info[0], info[1])

    @pl.when(pl.program_id(0) % share == 0)
    def _():
        @pl.loop(0, blocks)
        def _(dist):
            k_rows[dist] = transposed(k_ref[dist])

    query = q_ref[...]

    def scores_of(dist):
        return matmul(k_rows[dist], query) * (SCORE_SCALE * LOG2E)

    scores = jnp.where(causal(tokens, valid), scores_of(0), MASKED)
    top = jnp.max(scores, 0, keepdims=True)
    weights = jnp.exp2(scores - top)
    total = jnp.sum(weights, 0, keepdims=True)
    acc = matmul(v_ref[0], weights.astype(jnp.bfloat16))

    def step(dist, carry):
        top, total, acc = carry
        scores = scores_of(dist)
        new_top = jnp.maximum(top, jnp.max(scores, 0, keepdims=True))
        weights = jnp.exp2(scores - new_top)
        fade = jnp.exp2(top - new_top)
        total = total * fade + jnp.sum(weights, 0, keepdims=True)
        acc = acc * fade + matmul(v_ref[dist], weights.astype(jnp.bfloat16))
        return (new_top, total, acc)

    top, total, acc = lax.fori_loop(1, blocks, step, (top, total, acc))
    out = acc / total
    o_ref[...] = out.astype(jnp.bfloat16)
    full_ref[...] = out
    lse_ref[0] = top + jnp.log2(total)


def backward_kernel(
    info, q_ref, k_ref, v_ref, full_ref, lse_ref, do_ref, dq_ref, dk_ref, dv_ref,
    k_rows, v_rows, dk_acc, dv_acc,
):
    tokens = q_ref.shape[1]
    share = HEADS // KV_HEADS
    blocks, valid = (info[0], info[1])

    @pl.when(pl.program_id(0) % share == 0)
    def _():
        dk_acc[...] = jnp.zeros_like(dk_acc)
        dv_acc[...] = jnp.zeros_like(dv_acc)

        @pl.loop(0, blocks)
        def _(dist):
            k_rows[dist] = transposed(k_ref[dist])
            v_rows[dist] = transposed(v_ref[dist])

    query, grad = (q_ref[...], do_ref[...])
    query_rows, grad_rows = (transposed(query), transposed(grad))
    lse = lse_ref[0]
    centre = jnp.sum(grad.astype(jnp.float32) * full_ref[...], 0, keepdims=True)

    def block(dist, mask):
        scores = matmul(k_rows[dist], query) * (SCORE_SCALE * LOG2E)
        prob = jnp.exp2(scores - lse)
        if mask is not None:
            prob = jnp.where(mask, prob, 0.0)
        d_prob = matmul(v_rows[dist], grad)
        d_score = (prob * (d_prob - centre) * SCORE_SCALE).astype(jnp.bfloat16)
        dv_acc[dist] += matmul(prob.astype(jnp.bfloat16), grad_rows)
        dk_acc[dist] += matmul(d_score, query_rows)
        return matmul(k_ref[dist], d_score)

    d_query = block(0, causal(tokens, valid))
    dq_ref[...] = lax.fori_loop(1, blocks, lambda dist, acc: acc + block(dist, None), d_query)

    @pl.when(pl.program_id(0) % share == share - 1)
    def _():
        @pl.loop(0, dk_acc.shape[0])
        def _(dist):
            dk_ref[dist] = dk_acc[dist].T
            dv_ref[dist] = dv_acc[dist].T


def head_block(tokens):
    return pl.BlockSpec((HD, tokens), lambda head, info: (head, 0))


def kv_block(reach, tokens):
    share = HEADS // KV_HEADS
    return pl.BlockSpec((reach, HD, tokens), lambda head, info: (0, head // share, 0))


def row_block(tokens):
    return pl.BlockSpec((1, 1, tokens), lambda head, info: (head, 0, 0))


def attend_forward(info, query, keys, values):
    tokens, reach = (query.shape[1], keys.shape[0])
    return pl.pallas_call(
        forward_kernel,
        grid_spec=pltpu.PrefetchScalarGridSpec(
            num_scalar_prefetch=1,
            grid=(HEADS,),
            in_specs=[head_block(tokens), kv_block(reach, tokens), kv_block(reach, tokens)],
            out_specs=[head_block(tokens), head_block(tokens), row_block(tokens)],
            scratch_shapes=[pltpu.VMEM((reach, tokens, HD), jnp.bfloat16)],
        ),
        out_shape=[
            jax.ShapeDtypeStruct(query.shape, jnp.bfloat16),
            jax.ShapeDtypeStruct(query.shape, jnp.float32),
            jax.ShapeDtypeStruct((HEADS, 1, tokens), jnp.float32),
        ],
        compiler_params=pltpu.CompilerParams(vmem_limit_bytes=40 * 2**20),
        cost_estimate=pl.CostEstimate(
            flops=HEADS * reach * tokens * tokens * 256 * 4,
            bytes_accessed=query.size * 8,
            transcendentals=HEADS * reach * tokens * tokens,
        ),
        name="attend_forward",
    )(info, query, keys, values)


def attend_backward(info, query, keys, values, full, lse, grad):
    tokens, reach = (query.shape[1], keys.shape[0])
    return pl.pallas_call(
        backward_kernel,
        grid_spec=pltpu.PrefetchScalarGridSpec(
            num_scalar_prefetch=1,
            grid=(HEADS,),
            in_specs=[
                head_block(tokens),
                kv_block(reach, tokens),
                kv_block(reach, tokens),
                head_block(tokens),
                row_block(tokens),
                head_block(tokens),
            ],
            out_specs=[head_block(tokens), kv_block(reach, tokens), kv_block(reach, tokens)],
            scratch_shapes=[
                pltpu.VMEM((reach, tokens, HD), jnp.bfloat16),
                pltpu.VMEM((reach, tokens, HD), jnp.bfloat16),
                pltpu.VMEM((reach, tokens, HD), jnp.float32),
                pltpu.VMEM((reach, tokens, HD), jnp.float32),
            ],
        ),
        out_shape=[
            jax.ShapeDtypeStruct(query.shape, jnp.float32),
            jax.ShapeDtypeStruct(keys.shape, jnp.float32),
            jax.ShapeDtypeStruct(keys.shape, jnp.float32),
        ],
        compiler_params=pltpu.CompilerParams(vmem_limit_bytes=40 * 2**20),
        cost_estimate=pl.CostEstimate(
            flops=HEADS * reach * tokens * tokens * 256 * 10,
            bytes_accessed=query.size * 14,
            transcendentals=HEADS * reach * tokens * tokens,
        ),
        name="attend_backward",
    )(info, query, keys, values, full, lse, grad)


def gather_earlier(block):
    size = lax.axis_size("seq")
    held = [block]
    for step in range(1, size):
        held.append(lax.ppermute(held[-1], "seq", [(i, i + 1) for i in range(step - 1, size - 1)]))
    return jnp.stack(held, 0)


def sum_to_owner(parts):
    size = lax.axis_size("seq")
    total = parts[size - 1]
    for step in range(size - 1, 0, -1):
        total = parts[step - 1] + lax.ppermute(
            total.astype(jnp.bfloat16), "seq", [(i, i - 1) for i in range(step, size)]
        ).astype(jnp.float32)
    return total


def adam_update(weight, first_mom, second_mom, gradient, clip_factor, rate, decay):
    step_grad = gradient * clip_factor
    first_new = BETA_ONE * first_mom + (1.0 - BETA_ONE) * step_grad
    second_new = BETA_TWO * second_mom + (1.0 - BETA_TWO) * step_grad * step_grad
    mean_hat = first_new / (1.0 - BETA_ONE**STEP)
    square_hat = second_new / (1.0 - BETA_TWO**STEP)
    weight_new = weight - rate * (mean_hat / (jnp.sqrt(square_hat) + ADAM_EPS) + decay * weight)
    return (weight_new, first_new, second_new)


def gathered(shard):
    return lax.all_gather(shard.astype(jnp.bfloat16), ("dp", "seq"), axis=0, tiled=True)


def scattered(partial):
    part = lax.psum_scatter(
        partial.astype(jnp.bfloat16), "dp", scatter_dimension=0, tiled=True
    )
    return lax.psum_scatter(part, "seq", scatter_dimension=0, tiled=True).astype(jnp.float32)


def per_device(
    hidden_in,
    out_grad,
    seq_lengths,
    seq_counts,
    segment_ids,
    qkv_weight,
    qkv_m,
    qkv_v,
    out_weight,
    out_m,
    out_v,
    gate_up_weight,
    gate_up_m,
    gate_up_v,
    down_weight,
    down_m,
    down_v,
    norm_gains,
    gain_m,
    gain_v,
):
    tok_dev = hidden_in.shape[0]
    q_width = HEADS * HD
    kv_width = KV_HEADS * HD
    seg_all = segment_ids[0]
    lengths = seq_lengths[0]
    seq_index = lax.axis_index("seq")
    offset = seq_index * tok_dev
    seg_local = lax.dynamic_slice_in_dim(seg_all, offset, tok_dev, 0)
    starts = jnp.cumsum(lengths, dtype=jnp.int32) - lengths
    slot_ids = jnp.arange(lengths.shape[0], dtype=jnp.int32)
    seq_start = jnp.sum(
        jnp.where(seg_local[:, None] == slot_ids[None, :], starts[None, :], 0),
        axis=1,
        dtype=jnp.int32,
    )
    positions = offset + jnp.arange(tok_dev, dtype=jnp.int32) - seq_start
    cos_table, sin_table = rope_tables(positions)
    valid = (seg_local[0] < seq_counts[0]).astype(jnp.int32)
    reach = jnp.where(valid > 0, seq_index - seq_start[0] // tok_dev + 1, 1)
    info = jnp.stack([reach, valid]).astype(jnp.int32)

    w_qkv = gathered(qkv_weight)
    w_gain = lax.all_gather(norm_gains.astype(jnp.bfloat16), ("dp", "seq"), axis=1, tiled=True)
    w_out = gathered(out_weight)
    w_down = gathered(down_weight)
    w_gu = gathered(gate_up_weight)
    gain_attn = w_gain[0].astype(jnp.float32)
    gain_mlp = w_gain[1].astype(jnp.float32)
    residual = hidden_in.astype(jnp.float32)
    inv_one, normed = norm_forward(residual, gain_attn)
    normed_low = normed.astype(jnp.bfloat16)
    qkv_out = contract(w_qkv, normed_low, 0, 1)
    query = rotate(qkv_out[:q_width], cos_table, sin_table).astype(jnp.bfloat16)
    key = rotate(qkv_out[q_width : q_width + kv_width], cos_table, sin_table).astype(jnp.bfloat16)
    value = qkv_out[q_width + kv_width :].astype(jnp.bfloat16)
    kv_all = gather_earlier(jnp.concatenate([key, value], 0))
    keys, values = (kv_all[:, :kv_width], kv_all[:, kv_width:])
    attended, attended_full, lse = attend_forward(info, query, keys, values)
    mid_rows = residual + contract(attended, w_out, 0, 0)
    inv_two, normed_two = norm_forward(mid_rows, gain_mlp)
    inner_rows = normed_two.astype(jnp.bfloat16)
    gate_up = matmul(inner_rows, w_gu)
    gate_vals, up_vals = (gate_up[:, :FF], gate_up[:, FF:])
    sigmoid_gate = jax.nn.sigmoid(gate_vals)
    hidden = (gate_vals * sigmoid_gate * up_vals).astype(jnp.bfloat16)
    block_out = (mid_rows + matmul(hidden, w_down)).astype(jnp.bfloat16)
    d_hidden = contract(out_grad, w_down, 1, 1)
    g_down = contract(hidden, out_grad, 0, 0)
    d_gate = d_hidden * up_vals * sigmoid_gate * (1.0 + gate_vals * (1.0 - sigmoid_gate))
    d_up = d_hidden * gate_vals * sigmoid_gate
    d_gu = jnp.concatenate([d_gate, d_up], -1).astype(jnp.bfloat16)
    d_inner = contract(d_gu, w_gu, 1, 1)
    g_gu = contract(inner_rows, d_gu, 0, 0)
    back_two, g_gain_two = norm_backward(mid_rows, inv_two, gain_mlp, d_inner)
    d_mid = out_grad.astype(jnp.float32) + back_two
    g_down_own = scattered(g_down)
    g_gu_own = scattered(g_gu)
    d_branch = d_mid.astype(jnp.bfloat16)
    g_out = matmul(attended, d_branch)
    g_out_own = scattered(g_out)
    d_attended = contract(w_out, d_branch, 1, 1).astype(jnp.bfloat16)
    d_query, d_keys, d_values = attend_backward(
        info, query, keys, values, attended_full, lse, d_attended
    )
    d_kv = sum_to_owner(jnp.concatenate([d_keys, d_values], 1))
    d_qkv = jnp.concatenate(
        [
            rotate(d_query, cos_table, -sin_table),
            rotate(d_kv[:kv_width], cos_table, -sin_table),
            d_kv[kv_width:],
        ],
        0,
    ).astype(jnp.bfloat16)
    d_normed = contract(d_qkv, w_qkv, 0, 1)
    g_qkv = contract(normed_low, d_qkv, 0, 1)
    back_one, g_gain_one = norm_backward(residual, inv_one, gain_attn, d_normed)
    input_grad = d_mid + back_one
    g_gains = jnp.stack([g_gain_one, g_gain_two], 0)
    g_qkv_own = scattered(g_qkv)
    g_gains_own = lax.psum_scatter(g_gains, ("dp", "seq"), scatter_dimension=1, tiled=True)
    local_sq = (
        jnp.sum(g_qkv_own * g_qkv_own)
        + jnp.sum(g_out_own * g_out_own)
        + jnp.sum(g_gu_own * g_gu_own)
        + jnp.sum(g_down_own * g_down_own)
        + jnp.sum(g_gains_own * g_gains_own)
    )
    total_sq = lax.psum(local_sq, ("dp", "seq"))
    grad_norm = jnp.sqrt(total_sq)
    clip_factor = jnp.minimum(1.0, CLIP_NORM / (grad_norm + 1e-06))
    new_qkv, new_qkv_m, new_qkv_v = adam_update(
        qkv_weight, qkv_m, qkv_v, g_qkv_own, clip_factor, 0.06, WEIGHT_DECAY
    )
    new_out, new_out_m, new_out_v = adam_update(
        out_weight, out_m, out_v, g_out_own, clip_factor, 0.4, WEIGHT_DECAY
    )
    new_gu, new_gu_m, new_gu_v = adam_update(
        gate_up_weight, gate_up_m, gate_up_v, g_gu_own, clip_factor, 0.06, WEIGHT_DECAY
    )
    new_down, new_down_m, new_down_v = adam_update(
        down_weight, down_m, down_v, g_down_own, clip_factor, 0.06, WEIGHT_DECAY
    )
    new_gains, new_gain_m, new_gain_v = adam_update(
        norm_gains, gain_m, gain_v, g_gains_own, clip_factor, 0.6, 0.0
    )
    return (
        block_out,
        input_grad,
        grad_norm,
        new_qkv,
        new_qkv_m,
        new_qkv_v,
        new_out,
        new_out_m,
        new_out_v,
        new_gu,
        new_gu_m,
        new_gu_v,
        new_down,
        new_down_m,
        new_down_v,
        new_gains,
        new_gain_m,
        new_gain_v,
    )


def solution(mesh):
    in_specs = (
        P(("dp", "seq"), None),
        P(("dp", "seq"), None),
        P("dp", None),
        P("dp"),
        P("dp", None),
        P(("dp", "seq"), None),
        P(("dp", "seq"), None),
        P(("dp", "seq"), None),
        P(("dp", "seq"), None),
        P(("dp", "seq"), None),
        P(("dp", "seq"), None),
        P(("dp", "seq"), None),
        P(("dp", "seq"), None),
        P(("dp", "seq"), None),
        P(("dp", "seq"), None),
        P(("dp", "seq"), None),
        P(("dp", "seq"), None),
        P(None, ("dp", "seq")),
        P(None, ("dp", "seq")),
        P(None, ("dp", "seq")),
    )
    out_specs = (
        P(("dp", "seq"), None),
        P(("dp", "seq"), None),
        P(),
        P(("dp", "seq"), None),
        P(("dp", "seq"), None),
        P(("dp", "seq"), None),
        P(("dp", "seq"), None),
        P(("dp", "seq"), None),
        P(("dp", "seq"), None),
        P(("dp", "seq"), None),
        P(("dp", "seq"), None),
        P(("dp", "seq"), None),
        P(("dp", "seq"), None),
        P(("dp", "seq"), None),
        P(("dp", "seq"), None),
        P(None, ("dp", "seq")),
        P(None, ("dp", "seq")),
        P(None, ("dp", "seq")),
    )
    return jax.shard_map(
        per_device, mesh=mesh, in_specs=in_specs, out_specs=out_specs, check_vma=False
    )
```

```python
import functools

import jax
import jax.numpy as jnp
from jax import lax
from jax.experimental import pallas as pl
from jax.experimental.pallas import tpu as pltpu
from jax.sharding import PartitionSpec as P

HEADS = 32
KV_HEADS = 4
HD = 64
FF = 5632
STEP = 10


NORM_EPS = 1e-05
ROPE_BASE = 10000.0
CLIP_NORM = 1.0
BETA_ONE = 0.9
BETA_TWO = 0.999
ADAM_EPS = 1e-08
WEIGHT_DECAY = 0.1
MASKED = -1e30


def matmul(left, right):
    return jnp.dot(left, right, preferred_element_type=jnp.float32)


def contract(left, right, left_dim, right_dim):
    return lax.dot_general(
        left, right, (((left_dim,), (right_dim,)), ((), ())), preferred_element_type=jnp.float32
    )


def rope_tables(positions):
    half_dim = HD // 2
    inverse = jnp.exp(-(2.0 * jnp.arange(half_dim, dtype=jnp.float32) / HD) * jnp.log(ROPE_BASE))
    angles = inverse[:, None] * positions.astype(jnp.float32)[None, :]
    return (jnp.cos(angles), jnp.sin(angles))


def rotate(rows, cos_table, sin_table):
    tokens = rows.shape[1]
    split = rows.reshape(-1, 2, HD // 2, tokens)
    first, second = (split[:, 0], split[:, 1])
    return jnp.stack(
        [first * cos_table - second * sin_table, second * cos_table + first * sin_table], 1
    ).reshape(rows.shape)


def norm_forward(rows_in, gain_row):
    inv_rms = lax.rsqrt(jnp.mean(rows_in * rows_in, axis=-1, keepdims=True) + NORM_EPS)
    return (inv_rms, rows_in * inv_rms * gain_row)


def norm_backward(rows_in, inv_rms, gain_row, gradient):
    weighted = gain_row * gradient
    back_rows = inv_rms * weighted - rows_in * inv_rms**3 * jnp.mean(
        weighted * rows_in, axis=-1, keepdims=True
    )
    return (back_rows, jnp.sum(gradient * rows_in * inv_rms, axis=0))


LOG2E = 1.4426950408889634
SCORE_SCALE = HD ** (-0.5)
SHARE = HEADS // KV_HEADS


def transposed(block):
    return block.astype(jnp.float32).T.astype(block.dtype)


def causal(tokens, valid):
    key_ids = lax.broadcasted_iota(jnp.int32, (tokens, tokens), 0)
    row_ids = lax.broadcasted_iota(jnp.int32, (tokens, tokens), 1)
    return (key_ids == row_ids) | ((key_ids < row_ids) & (valid > 0))


def attend_head(head, blocks, reach, valid, q_ref, kv_ref, group, k_rows, o_ref, full_ref, lse_ref):
    tokens = q_ref.shape[1]
    rows = pl.ds(pl.multiple_of(head * HD, HD), HD)
    query = q_ref[rows, :]

    def scores_of(dist):
        return matmul(k_rows[dist], query) * (SCORE_SCALE * LOG2E)

    def values_of(dist):
        return kv_ref[dist, group, HD:, :]

    scores = jnp.where(causal(tokens, valid), scores_of(0), MASKED)
    top = jnp.max(scores, 0, keepdims=True)
    weights = jnp.exp2(scores - top)
    total = jnp.sum(weights, 0, keepdims=True)
    acc = matmul(values_of(0), weights.astype(jnp.bfloat16))

    def step(dist, carry):
        top, total, acc = carry
        scores = jnp.where(dist < reach, scores_of(dist), MASKED)
        new_top = jnp.maximum(top, jnp.max(scores, 0, keepdims=True))
        weights = jnp.exp2(scores - new_top)
        fade = jnp.exp2(top - new_top)
        total = total * fade + jnp.sum(weights, 0, keepdims=True)
        acc = acc * fade + matmul(values_of(dist), weights.astype(jnp.bfloat16))
        return (new_top, total, acc)

    top, total, acc = lax.fori_loop(1, blocks, step, (top, total, acc))
    out = acc / total
    o_ref[rows, :] = out.astype(jnp.bfloat16)
    full_ref[rows, :] = out
    lse_ref[head] = top + jnp.log2(total)


def backward_kernel(
    info, q_ref, kv_ref, full_ref, lse_ref, do_ref, dq_ref, dkv_ref, k_rows, v_rows, dk_acc, dv_acc
):
    tokens = q_ref.shape[1]
    blocks, valid = (info[0], info[1])

    @pl.when(pl.program_id(0) % SHARE == 0)
    def _():
        dk_acc[...] = jnp.zeros_like(dk_acc)
        dv_acc[...] = jnp.zeros_like(dv_acc)

        @pl.loop(0, blocks)
        def _(dist):
            k_rows[dist] = transposed(kv_ref[dist, 0, :HD, :])
            v_rows[dist] = transposed(kv_ref[dist, 0, HD:, :])

    query, grad = (q_ref[...], do_ref[...])
    query_rows, grad_rows = (transposed(query), transposed(grad))
    lse = lse_ref[0]
    centre = jnp.sum(grad.astype(jnp.float32) * full_ref[...], 0, keepdims=True)

    def block(dist, mask):
        scores = matmul(k_rows[dist], query) * (SCORE_SCALE * LOG2E)
        prob = jnp.exp2(scores - lse)
        if mask is not None:
            prob = jnp.where(mask, prob, 0.0)
        d_prob = matmul(v_rows[dist], grad)
        d_score = (prob * (d_prob - centre) * SCORE_SCALE).astype(jnp.bfloat16)
        dv_acc[dist] += matmul(prob.astype(jnp.bfloat16), grad_rows)
        dk_acc[dist] += matmul(d_score, query_rows)
        return matmul(kv_ref[dist, 0, :HD, :], d_score)

    d_query = block(0, causal(tokens, valid))
    dq_ref[...] = lax.fori_loop(1, blocks, lambda dist, acc: acc + block(dist, None), d_query)

    @pl.when(pl.program_id(0) % SHARE == SHARE - 1)
    def _():
        @pl.loop(0, dk_acc.shape[0])
        def _(dist):
            dkv_ref[dist, 0, :HD, :] = dk_acc[dist].T
            dkv_ref[dist, 0, HD:, :] = dv_acc[dist].T


def attend_backward(info, query, kv, full, lse, grad, first, heads):
    tokens, reach = (query.shape[1], kv.shape[0])

    def head_block():
        return pl.BlockSpec((HD, tokens), lambda head, info: (head + first, 0))

    def row_block():
        return pl.BlockSpec((1, 1, tokens), lambda head, info: (head + first, 0, 0))

    return pl.pallas_call(
        backward_kernel,
        grid_spec=pltpu.PrefetchScalarGridSpec(
            num_scalar_prefetch=1,
            grid=(heads,),
            in_specs=[
                head_block(),
                pl.BlockSpec(
                    (reach, 1, 2 * HD, tokens),
                    lambda head, info: (0, (head + first) // SHARE, 0, 0),
                ),
                head_block(),
                row_block(),
                head_block(),
            ],
            out_specs=[
                pl.BlockSpec((HD, tokens), lambda head, info: (head, 0)),
                pl.BlockSpec(
                    (reach, 1, 2 * HD, tokens), lambda head, info: (0, head // SHARE, 0, 0)
                ),
            ],
            scratch_shapes=[
                pltpu.VMEM((reach, tokens, HD), jnp.bfloat16),
                pltpu.VMEM((reach, tokens, HD), jnp.bfloat16),
                pltpu.VMEM((reach, tokens, HD), jnp.float32),
                pltpu.VMEM((reach, tokens, HD), jnp.float32),
            ],
        ),
        out_shape=[
            jax.ShapeDtypeStruct((heads * HD, tokens), jnp.float32),
            jax.ShapeDtypeStruct((reach, heads // SHARE, 2 * HD, tokens), jnp.float32),
        ],
        compiler_params=pltpu.CompilerParams(vmem_limit_bytes=40 * 2**20),
        cost_estimate=pl.CostEstimate(
            flops=heads * reach * tokens * tokens * 256 * 10,
            bytes_accessed=query.size * 14,
            transcendentals=heads * reach * tokens * tokens,
        ),
        name="attend_backward",
    )(info, query, kv, full, lse, grad)


def sum_to_owner(parts):
    size = lax.axis_size("seq")
    total = parts[size - 1]
    for step in range(size - 1, 0, -1):
        total = parts[step - 1] + lax.ppermute(
            total.astype(jnp.bfloat16), "seq", [(i, i - 1) for i in range(step, size)]
        ).astype(jnp.float32)
    return total


def adam_update(weight, first_mom, second_mom, gradient, clip_factor, rate, decay):
    step_grad = gradient * clip_factor
    first_new = BETA_ONE * first_mom + (1.0 - BETA_ONE) * step_grad
    second_new = BETA_TWO * second_mom + (1.0 - BETA_TWO) * step_grad * step_grad
    mean_hat = first_new / (1.0 - BETA_ONE**STEP)
    square_hat = second_new / (1.0 - BETA_TWO**STEP)
    weight_new = weight - rate * (mean_hat / (jnp.sqrt(square_hat) + ADAM_EPS) + decay * weight)
    return (weight_new, first_new, second_new)


MESH = pl.DeviceIdType.MESH


def flipped(index, bit):
    return index + (1 << bit) * (1 - 2 * ((index // (1 << bit)) % 2))


WHOLE, ROWS, BLOCKS = range(3)


class Gather:
    ahead = 3

    def __init__(self, kinds, pieces, shards, fulls, local_sems, send_sems, recv_sems):
        self.kinds, self.pieces, self.shards, self.fulls = (kinds, pieces, shards, fulls)
        self.local_sems, self.send_sems, self.recv_sems = (local_sems, send_sems, recv_sems)
        self.dp, self.seq = (lax.axis_index("dp"), lax.axis_index("seq"))
        self.dp_size, self.seq_size = (lax.axis_size("dp"), lax.axis_size("seq"))
        self.bits = self.dp_size.bit_length() - 1
        up = list(range(1, self.bits))
        self.orders = (up + [0], up[::-1] + [0])
        self.started = []
        self.local = {}
        self.done = set()

    def along(self, step):
        return {"seq": lax.rem(self.seq + step, self.seq_size)}

    def across(self, bit):
        return {"dp": flipped(self.dp, bit)}

    def barrier(self):
        barrier = pltpu.get_barrier_semaphore()
        others = [self.along(step) for step in range(1, self.seq_size)]
        others += [self.across(bit) for bit in range(self.bits)]
        for other in others:
            pl.semaphore_signal(barrier, inc=1, device_id=other, device_id_type=MESH)
        pl.semaphore_wait(barrier, len(others))

    def columns(self, piece, side):
        _, low, middle, high = self.pieces[piece]
        return (pl.ds(low, middle - low), pl.ds(middle, high - middle))[side]

    def sides(self, piece):
        return (0, 1) if self.pieces[piece][3] > self.pieces[piece][2] else (0,)

    def own_rows(self, weight):
        depth = self.shards[weight].shape[0]
        index = {
            WHOLE: self.dp * self.seq_size + self.seq, ROWS: self.seq, BLOCKS: self.dp
        }[self.kinds[weight]]
        return pl.ds(pl.multiple_of(index * depth, depth), depth)

    def seq_copy(self, piece, side, step):
        weight = self.pieces[piece][0]
        cols = self.columns(piece, side)
        return pltpu.make_async_remote_copy(
            src_ref=self.shards[weight].at[:, cols],
            dst_ref=self.fulls[weight].at[self.own_rows(weight), cols],
            send_sem=self.send_sems.at[piece, side, self.dp_size + step],
            recv_sem=self.recv_sems.at[piece, side, self.dp_size + step],
            device_id=self.along(step),
            device_id_type=MESH,
        )

    def block_copy(self, piece, side, held, bit):
        weight = self.pieces[piece][0]
        depth = self.fulls[weight].shape[0] // self.dp_size
        owner = self.dp
        for position in range(self.bits):
            if held >> position & 1:
                owner = flipped(owner, position)
        window = (pl.ds(pl.multiple_of(owner * depth, depth), depth), self.columns(piece, side))
        source = self.fulls[weight].at[window]
        if not held and self.kinds[weight] == BLOCKS:
            source = self.shards[weight].at[:, self.columns(piece, side)]
        return pltpu.make_async_remote_copy(
            src_ref=source,
            dst_ref=self.fulls[weight].at[window],
            send_sem=self.send_sems.at[piece, side, held | 1 << bit],
            recv_sem=self.recv_sems.at[piece, side, held | 1 << bit],
            device_id=self.across(bit),
            device_id_type=MESH,
        )

    def start(self, copy):
        copy.start()
        self.started.append(copy)

    def begin(self):
        for weight, shard in enumerate(self.shards):
            self.local[weight] = pltpu.make_async_copy(
                shard, self.fulls[weight].at[self.own_rows(weight)], self.local_sems.at[weight]
            )
            self.local[weight].start()
        for piece in range(min(self.ahead, len(self.pieces))):
            self.send_rows(piece)

    def send_rows(self, piece):
        if self.kinds[self.pieces[piece][0]] == BLOCKS:
            return
        for step in range(1, self.seq_size):
            for side in self.sides(piece):
                self.start(self.seq_copy(piece, side, step))

    def advance(self, piece, stage):
        if (piece, stage) in self.done:
            return
        self.done.add((piece, stage))
        weight = self.pieces[piece][0]
        kind = self.kinds[weight]
        if stage and kind == ROWS:
            return
        if stage == 0 and kind == WHOLE and weight in self.local:
            self.local.pop(weight).wait()
        for side in self.sides(piece):
            order = self.orders[side] if kind != ROWS else []
            if stage == 0:
                if kind != BLOCKS:
                    for step in range(1, self.seq_size):
                        self.seq_copy(piece, side, step).wait_recv()
                held = [0]
            else:
                reached = [0]
                for bit in order[: stage - 1]:
                    reached += [block | 1 << bit for block in reached]
                held = [block | 1 << order[stage - 1] for block in reached]
                for block in reached:
                    self.block_copy(piece, side, block, order[stage - 1]).wait_recv()
            for bit in order[stage:]:
                for block in held:
                    self.start(self.block_copy(piece, side, block, bit))
        if stage == 0 and piece + self.ahead < len(self.pieces):
            self.send_rows(piece + self.ahead)

    def finish(self):
        for turn in range(len(self.pieces) + self.bits):
            for piece in range(len(self.pieces)):
                if 0 <= turn - piece <= self.bits:
                    self.advance(piece, turn - piece)
        for copy in self.local.values():
            copy.wait()
        for copy in self.started:
            copy.wait_send()


def gather_scratch(count, pieces):
    slots = lax.axis_size("dp") + lax.axis_size("seq")
    return [
        pltpu.SemaphoreType.DMA((count,)),
        pltpu.SemaphoreType.DMA((pieces, 2, slots)),
        pltpu.SemaphoreType.DMA((pieces, 2, slots)),
    ]


def gather_shapes(kinds, shards):
    dp_size, seq_size = (lax.axis_size("dp"), lax.axis_size("seq"))
    factor = {WHOLE: dp_size * seq_size, ROWS: seq_size, BLOCKS: dp_size}
    return [
        jax.ShapeDtypeStruct((s.shape[0] * factor[kind], s.shape[1]), s.dtype)
        for kind, s in zip(kinds, shards)
    ]


def gather_kernel(kinds, pieces, *refs):
    count = len(kinds)
    gather = Gather(kinds, pieces, refs[:count], refs[count : 2 * count], *refs[2 * count :])
    gather.barrier()
    gather.begin()
    gather.finish()


def gather_all(kinds, shards, pieces, collective_id):
    count = len(shards)
    return pl.pallas_call(
        functools.partial(gather_kernel, kinds, pieces),
        out_shape=gather_shapes(kinds, shards),
        in_specs=[pl.BlockSpec(memory_space=pl.ANY)] * count,
        out_specs=[pl.BlockSpec(memory_space=pl.ANY)] * count,
        scratch_shapes=gather_scratch(count, len(pieces)),
        compiler_params=pltpu.CompilerParams(collective_id=collective_id, has_side_effects=True),
        name="gather",
    )(*shards)


def attend_kernel(kinds, pieces, info, q_ref, kv_ref, *refs):
    count = len(kinds)
    shards = refs[:count]
    o_ref, full_ref, lse_ref, kv_all_ref = refs[count : count + 4]
    fulls = refs[count + 4 : 2 * count + 4]
    k_rows, slots, kv_send, kv_recv = refs[2 * count + 4 : 2 * count + 8]
    gather = Gather(kinds, pieces, shards, fulls, *refs[2 * count + 8 :])
    seq, seq_size = (gather.seq, gather.seq_size)
    reach, valid = (info[0], info[1])
    gather.barrier()

    def kv_copy(group, step):
        return pltpu.make_async_remote_copy(
            src_ref=kv_ref.at[group],
            dst_ref=slots.at[step, group],
            send_sem=kv_send.at[step, group],
            recv_sem=kv_recv.at[step, group],
            device_id=gather.along(step),
            device_id_type=MESH,
        )

    for group in range(KV_HEADS):
        for step in range(1, seq_size):

            @pl.when(seq + step < seq_size)
            def _():
                kv_copy(group, step).start()

    gather.begin()
    gather.advance(0, 0)
    slots[0] = kv_ref[...]
    beside = {1: [(0, 1)], 3: [(0, 2)], 5: [(1, 0)], 7: [(0, 3), (1, 1), (2, 0)]}
    for group in range(KV_HEADS):
        k_rows[0] = transposed(kv_ref[group, :HD, :])
        for step in range(1, seq_size):

            @pl.when(seq >= step)
            def _():
                kv_copy(group, step).wait_recv()
                k_rows[step] = transposed(slots[step, group, :HD, :])

        for part in range(2):

            @pl.loop(group * SHARE + part * SHARE // 2, group * SHARE + (part + 1) * SHARE // 2)
            def _(head):
                attend_head(
                    head, seq + 1, reach, valid, q_ref, slots, group, k_rows, o_ref, full_ref, lse_ref
                )

            for event in beside.get(group * 2 + part, []):
                gather.advance(*event)
    for step in range(seq_size):

        @pl.when(seq >= step)
        def _():
            kv_all_ref[step] = slots[step]

        @pl.when(seq < step)
        def _():
            kv_all_ref[step] = jnp.zeros_like(kv_ref)

    for group in range(KV_HEADS):
        for step in range(1, seq_size):

            @pl.when(seq + step < seq_size)
            def _():
                kv_copy(group, step).wait_send()

    gather.finish()


def attend_forward(info, query, kv, kinds, shards, pieces, collective_id):
    tokens = query.shape[1]
    seq_size = lax.axis_size("seq")
    count = len(shards)
    vmem = pl.BlockSpec(memory_space=pltpu.VMEM)
    hbm = pl.BlockSpec(memory_space=pl.ANY)
    out = pl.pallas_call(
        functools.partial(attend_kernel, kinds, pieces),
        out_shape=[
            jax.ShapeDtypeStruct(query.shape, jnp.bfloat16),
            jax.ShapeDtypeStruct(query.shape, jnp.float32),
            jax.ShapeDtypeStruct((HEADS, 1, tokens), jnp.float32),
            jax.ShapeDtypeStruct((seq_size, *kv.shape), kv.dtype),
            *gather_shapes(kinds, shards),
        ],
        in_specs=[pl.BlockSpec(memory_space=pltpu.SMEM), vmem, vmem] + [hbm] * count,
        out_specs=[vmem] * 4 + [hbm] * count,
        scratch_shapes=[
            pltpu.VMEM((seq_size, tokens, HD), jnp.bfloat16),
            pltpu.VMEM((seq_size, *kv.shape), kv.dtype),
            pltpu.SemaphoreType.DMA((seq_size, KV_HEADS)),
            pltpu.SemaphoreType.DMA((seq_size, KV_HEADS)),
            *gather_scratch(count, len(pieces)),
        ],
        compiler_params=pltpu.CompilerParams(
            collective_id=collective_id, has_side_effects=True, vmem_limit_bytes=48 * 2**20
        ),
        name="attend_forward",
    )(info, query, kv, *shards)
    return (out[:4], out[4:])


def total_kernel(x_ref, o_ref, slots, send_sems, recv_sems):
    dp, seq = (lax.axis_index("dp"), lax.axis_index("seq"))
    dp_size, seq_size = (lax.axis_size("dp"), lax.axis_size("seq"))
    devices = dp_size * seq_size
    me = dp * seq_size + seq

    def device(step):
        other = lax.rem(me + step, devices)
        return (other // seq_size, lax.rem(other, seq_size))

    def copy(step):
        return pltpu.make_async_remote_copy(
            src_ref=x_ref,
            dst_ref=slots.at[step],
            send_sem=send_sems.at[step],
            recv_sem=recv_sems.at[step],
            device_id=device(step),
            device_id_type=MESH,
        )

    barrier = pltpu.get_barrier_semaphore()

    @pl.loop(1, devices)
    def _(step):
        pl.semaphore_signal(barrier, inc=1, device_id=device(step), device_id_type=MESH)

    pl.semaphore_wait(barrier, devices - 1)

    @pl.loop(1, devices)
    def _(step):
        copy(step).start()

    @pl.loop(1, devices)
    def _(step):
        copy(step).wait()

    o_ref[...] = x_ref[...] + jnp.sum(slots[1:], 0)


def total_of(value, collective_id):
    devices = lax.axis_size("dp") * lax.axis_size("seq")
    return pl.pallas_call(
        total_kernel,
        out_shape=jax.ShapeDtypeStruct((8, 128), jnp.float32),
        in_specs=[pl.BlockSpec(memory_space=pltpu.VMEM)],
        out_specs=pl.BlockSpec(memory_space=pltpu.VMEM),
        scratch_shapes=[
            pltpu.VMEM((devices, 8, 128), jnp.float32),
            pltpu.SemaphoreType.DMA((devices,)),
            pltpu.SemaphoreType.DMA((devices,)),
        ],
        compiler_params=pltpu.CompilerParams(collective_id=collective_id, has_side_effects=True),
        name="total",
    )(jnp.full((8, 128), value, jnp.float32))[0, 0]


PARTS = 4


def swapped(block, axis, mask):
    return lax.ppermute(block, axis, [(i, i ^ mask) for i in range(lax.axis_size(axis))])


def by_distance(rows):
    size = lax.axis_size("dp")
    index = lax.axis_index("dp")
    depth = rows.shape[0] // size
    pick = lambda j: lax.dynamic_slice_in_dim(rows, (index ^ j) * depth, depth, 0)
    return (
        jnp.concatenate([pick(j) for j in range(0, size, 2)], 0),
        jnp.concatenate([pick(j) for j in range(1, size, 2)], 0),
    )


def owner_sum(total, split, dtype=jnp.bfloat16):
    size = total.shape[0]
    depth = total.shape[1]
    low, high = (total[..., :split], total[..., split:])
    bits = size.bit_length() - 1

    def plus(kept, got):
        return (kept.astype(jnp.float32) + got.astype(jnp.float32)).astype(dtype)

    for step in range(bits):
        half = low.shape[0] // 2
        low_pair = low.reshape(half, 2, depth, low.shape[-1])
        low_got, high_got = yield [
            ("dp", 2 << step, low_pair[:, 1].reshape(half * depth, -1)),
            ("dp", 1 << (bits - step), high[half:].reshape(half * depth, -1)),
        ]
        low = plus(low_pair[:, 0], low_got.reshape(half, depth, -1))
        high = plus(high[:half], high_got.reshape(half, depth, -1))
    total = jnp.concatenate([low[0], high[0]], -1)
    index = lax.axis_index("seq")
    mask = lax.axis_size("seq") // 2
    while mask:
        half = total.shape[0] // 2
        upper = ((index // mask) % 2) * half
        send = lax.dynamic_slice_in_dim(total, half - upper, half, 0)
        (got,) = yield [("seq", mask, send)]
        kept = lax.dynamic_slice_in_dim(total, upper, half, 0)
        mask //= 2
        total = plus(kept, got) if mask else kept.astype(jnp.float32) + got.astype(jnp.float32)
    return total


class Sums:
    def __init__(self):
        self.results = []
        self.ready = []
        self.arrived = []

    def step(self, place, generator, answer):
        try:
            self.ready.append((place, generator, generator.send(answer)))
        except StopIteration as stop:
            self.results[place] = stop.value

    def add(self, total, split, dtype=jnp.bfloat16):
        self.results.append(None)
        self.step(len(self.results) - 1, owner_sum(total, split, dtype), None)

    def absorb(self):
        arrived, self.arrived = (self.arrived, [])
        for place, generator, answer in arrived:
            self.step(place, generator, answer)

    def round(self, work, inputs, prompt=True):
        if prompt:
            self.absorb()
        sending, self.ready = (self.ready, [])
        blocks = [[block for _, _, block in wanted] for _, _, wanted in sending]
        came = [answer for _, _, answer in self.arrived]
        inputs, blocks, came = lax.optimization_barrier((inputs, blocks, came))
        self.arrived = [(p, g, a) for (p, g, _), a in zip(self.arrived, came)]
        self.absorb()
        answers = [
            [swapped(block, axis, mask) for (axis, mask, _), block in zip(wanted, group)]
            for (_, _, wanted), group in zip(sending, blocks)
        ]
        outputs = work(*inputs)
        later = [[block for _, _, block in wanted] for _, _, wanted in self.ready]
        outputs, answers, later = lax.optimization_barrier((outputs, answers, later))
        self.ready = [
            (p, g, [(axis, mask, block) for (axis, mask, _), block in zip(wanted, group)])
            for (p, g, wanted), group in zip(self.ready, later)
        ]
        self.arrived = [(p, g, a) for (p, g, _), a in zip(sending, answers)]
        return outputs


def weight_gradient(left, right, right_dim):
    left_own, left_other = left
    other = contract(left_other, right, 1, right_dim).astype(jnp.bfloat16)
    got = swapped(other, "dp", 1)
    total = contract(left_own, right, 1, right_dim) + got.astype(jnp.float32)
    size = lax.axis_size("dp") // 2
    return total.astype(jnp.bfloat16).reshape(size, total.shape[0] // size, total.shape[1])


def per_device(
    hidden_in,
    out_grad,
    seq_lengths,
    seq_counts,
    segment_ids,
    qkv_weight,
    qkv_m,
    qkv_v,
    out_weight,
    out_m,
    out_v,
    gate_up_weight,
    gate_up_m,
    gate_up_v,
    down_weight,
    down_m,
    down_v,
    norm_gains,
    gain_m,
    gain_v,
):
    tok_dev = hidden_in.shape[0]
    q_width = HEADS * HD
    kv_width = KV_HEADS * HD
    seg_all = segment_ids[0]
    lengths = seq_lengths[0]
    seq_index = lax.axis_index("seq")
    offset = seq_index * tok_dev
    seg_local = lax.dynamic_slice_in_dim(seg_all, offset, tok_dev, 0)
    starts = jnp.cumsum(lengths, dtype=jnp.int32) - lengths
    slot_ids = jnp.arange(lengths.shape[0], dtype=jnp.int32)
    seq_start = jnp.sum(
        jnp.where(seg_local[:, None] == slot_ids[None, :], starts[None, :], 0),
        axis=1,
        dtype=jnp.int32,
    )
    positions = offset + jnp.arange(tok_dev, dtype=jnp.int32) - seq_start
    cos_table, sin_table = rope_tables(positions)
    valid = (seg_local[0] < seq_counts[0]).astype(jnp.int32)
    reach = jnp.where(valid > 0, seq_index - seq_start[0] // tok_dev + 1, 1)
    info = jnp.stack([reach, valid]).astype(jnp.int32)

    devices = lax.axis_size("dp") * lax.axis_size("seq")
    own = norm_gains.shape[1]
    gain_rows = jnp.pad(norm_gains.astype(jnp.bfloat16), ((0, 14), (0, 128 - own)))
    width = qkv_weight.shape[1] // 4
    part = FF // PARTS
    gu_shards = [
        jnp.concatenate(
            [
                gate_up_weight[:, p * part : (p + 1) * part],
                gate_up_weight[:, FF + p * part : FF + (p + 1) * part],
            ],
            1,
        ).astype(jnp.bfloat16)
        for p in range(PARTS)
    ]
    w_qkv, gain_rows, gu_shards[0] = gather_all(
        [WHOLE, WHOLE, ROWS],
        [qkv_weight.astype(jnp.bfloat16), gain_rows, gu_shards[0]],
        [
            (1, 0, 128, 128),
            (0, 0, width, 2 * width),
            (0, 2 * width, 3 * width, 4 * width),
            (2, 0, part, 2 * part),
        ],
        1,
    )
    w_gain = jnp.moveaxis(gain_rows.reshape(devices, 16, 128)[:, :2, :own], 1, 0).reshape(2, -1)
    gain_attn = w_gain[0].astype(jnp.float32)
    gain_mlp = w_gain[1].astype(jnp.float32)
    residual = hidden_in.astype(jnp.float32)
    inv_one, normed = norm_forward(residual, gain_attn)
    normed_low = normed.astype(jnp.bfloat16)
    qkv_out = contract(w_qkv, normed_low, 0, 1)
    query = rotate(qkv_out[:q_width], cos_table, sin_table).astype(jnp.bfloat16)
    key = rotate(qkv_out[q_width : q_width + kv_width], cos_table, sin_table).astype(jnp.bfloat16)
    value = qkv_out[q_width + kv_width :].astype(jnp.bfloat16)
    kv_own = jnp.concatenate(
        [key.reshape(KV_HEADS, HD, tok_dev), value.reshape(KV_HEADS, HD, tok_dev)], 1
    )
    down_depth = down_weight.shape[0]
    spare = -down_depth % 16
    shards = [
        out_weight.astype(jnp.bfloat16),
        jnp.pad(down_weight.astype(jnp.bfloat16), ((0, spare), (0, 0))),
        *gu_shards,
    ]
    kinds = [WHOLE, WHOLE, BLOCKS] + [WHOLE] * (PARTS - 1)
    model = out_weight.shape[1]
    near = part // 256 * 128 + 128
    pieces = [(2, 0, part, 2 * part), (0, 0, model // 2, model)]
    pieces += [(1, low, low + model // 4, low + model // 2) for low in (0, model // 2)]
    pieces += [(2 + p, 0, part, 2 * part) for p in range(1, PARTS - 1)]
    pieces += [(1 + PARTS, 0, near, part), (1 + PARTS, part, 2 * part - near, 2 * part)]
    (attended, attended_full, lse, kv_all), (w_out, w_down, *w_gu) = attend_forward(
        info, query, kv_own, kinds, shards, pieces, 2
    )
    if spare:
        w_down = w_down.reshape(devices, -1, model)[:, :down_depth].reshape(-1, model)
    mid_rows = residual + contract(attended, w_out, 0, 0)
    inv_two, normed_two = norm_forward(mid_rows, gain_mlp)
    inner_rows = normed_two.astype(jnp.bfloat16)

    inner_blocks = by_distance(inner_rows.T)

    def mlp_part(inner_rows, inner_blocks, out_grad, w_gu_part, w_down_part):
        gate_up = matmul(inner_rows, w_gu_part)
        gate_vals, up_vals = (gate_up[:, :part], gate_up[:, part:])
        d_hidden = contract(out_grad, w_down_part, 1, 1)
        sigmoid_gate = jax.nn.sigmoid(gate_vals)
        hidden = (gate_vals * sigmoid_gate * up_vals).astype(jnp.bfloat16)
        d_gate = d_hidden * up_vals * sigmoid_gate * (1.0 + gate_vals * (1.0 - sigmoid_gate))
        d_up = d_hidden * gate_vals * sigmoid_gate
        d_gu = jnp.concatenate([d_gate, d_up], -1).astype(jnp.bfloat16)
        return (hidden, d_gu, weight_gradient(inner_blocks, d_gu, 0))

    def down_rows(p):
        return w_down[p * part : (p + 1) * part]

    sums = Sums()
    hidden_parts, d_gu_parts = ([], [])
    out = mlp_part(inner_rows, inner_blocks, out_grad, w_gu[0], down_rows(0))
    for p in range(1, PARTS + 1):
        hidden_parts.append(out[0])
        d_gu_parts.append(out[1])
        sums.add(out[2], part)
        if p < PARTS:
            out = sums.round(
                mlp_part, (inner_rows, inner_blocks, out_grad, w_gu[p], down_rows(p)), prompt=False
            )

    half = out_grad.shape[1] // 2

    def finish_mlp(hidden_parts, d_gu_parts, w_gu, out_grad, mid_rows, w_out):
        hidden = jnp.concatenate(hidden_parts, -1)
        d_inner = sum(contract(d, w, 1, 1) for d, w in zip(d_gu_parts, w_gu))
        back_two, g_gain_two = norm_backward(mid_rows, inv_two, gain_mlp, d_inner)
        d_mid = out_grad.astype(jnp.float32) + back_two
        d_branch = d_mid.astype(jnp.bfloat16)
        d_attended = contract(w_out, d_branch, 1, 1).astype(jnp.bfloat16)
        hidden_blocks = by_distance(hidden.T)
        g_down = weight_gradient(hidden_blocks, out_grad[:, :half], 0)
        return (hidden, hidden_blocks, g_gain_two, d_mid, d_branch, d_attended, g_down)

    hidden, hidden_blocks, g_gain_two, d_mid, d_branch, d_attended, g_down = sums.round(
        finish_mlp, (hidden_parts, d_gu_parts, w_gu, out_grad, mid_rows, w_out)
    )
    sums.add(g_down, half // 2)

    def attention_part(first):
        def work(d_attended, hidden_blocks, right):
            grads = attend_backward(
                info, query, kv_all, attended_full, lse, d_attended, first, HEADS // 2
            )
            return (grads, weight_gradient(hidden_blocks, right, 0))

        return work

    early, g_down = sums.round(
        attention_part(0), (d_attended, hidden_blocks, out_grad[:, half:])
    )
    sums.add(g_down, half // 2)
    late, g_out = sums.round(
        attention_part(HEADS // 2), (d_attended, by_distance(attended), d_branch)
    )
    sums.add(g_out, half)

    def finish_attention(early, late, normed_low):
        d_query = jnp.concatenate([early[0], late[0]], 0)
        d_kv = sum_to_owner(jnp.concatenate([early[1], late[1]], 1))
        d_qkv = jnp.concatenate(
            [
                rotate(d_query, cos_table, -sin_table),
                rotate(d_kv[:, :HD].reshape(kv_width, tok_dev), cos_table, -sin_table),
                d_kv[:, HD:].reshape(kv_width, tok_dev),
            ],
            0,
        ).astype(jnp.bfloat16)
        d_normed = contract(d_qkv, w_qkv, 0, 1)
        g_qkv = weight_gradient(by_distance(normed_low.T), d_qkv, 1)
        g_gain_one = jnp.sum(d_normed * residual * inv_one, axis=0)
        g_gains = jnp.stack([g_gain_one, g_gain_two], 0).reshape(2, devices, own)
        g_gains = by_distance(jnp.moveaxis(g_gains, 0, 1).reshape(devices, 2 * own))
        g_gains = (g_gains[0] + swapped(g_gains[1], "dp", 1)).reshape(
            lax.axis_size("dp") // 2, -1, 2 * own
        )
        return (d_normed, g_qkv, g_gains)

    d_normed, g_qkv, g_gains = sums.round(finish_attention, (early, late, normed_low))
    sums.add(g_qkv, g_qkv.shape[-1] // 2)
    sums.add(g_gains, own, jnp.float32)

    (input_grad,) = sums.round(
        lambda d_normed, d_mid: (
            d_mid + norm_backward(residual, inv_one, gain_attn, d_normed)[0],
        ),
        (d_normed, d_mid),
    )
    (block_out,) = sums.round(
        lambda hidden, mid_rows: ((mid_rows + matmul(hidden, w_down)).astype(jnp.bfloat16),),
        (hidden, mid_rows),
    )
    while sums.ready or sums.arrived:
        sums.round(lambda: (), ())
    summed = sums.results
    g_gu_own = jnp.concatenate(
        [s[:, :part] for s in summed[:PARTS]] + [s[:, part:] for s in summed[:PARTS]], 1
    )
    g_down_own = jnp.concatenate(summed[PARTS : PARTS + 2], 1)
    g_out_own, g_qkv_own, g_gains_own = summed[PARTS + 2 :]
    g_gains_own = g_gains_own.reshape(2, own)
    local_sq = (
        jnp.sum(g_qkv_own * g_qkv_own)
        + jnp.sum(g_out_own * g_out_own)
        + jnp.sum(g_gu_own * g_gu_own)
        + jnp.sum(g_down_own * g_down_own)
        + jnp.sum(g_gains_own * g_gains_own)
    )
    total_sq = total_of(local_sq, 3)
    grad_norm = jnp.sqrt(total_sq)
    clip_factor = jnp.minimum(1.0, CLIP_NORM / (grad_norm + 1e-06))
    new_qkv, new_qkv_m, new_qkv_v = adam_update(
        qkv_weight, qkv_m, qkv_v, g_qkv_own, clip_factor, 0.06, WEIGHT_DECAY
    )
    new_out, new_out_m, new_out_v = adam_update(
        out_weight, out_m, out_v, g_out_own, clip_factor, 0.4, WEIGHT_DECAY
    )
    new_gu, new_gu_m, new_gu_v = adam_update(
        gate_up_weight, gate_up_m, gate_up_v, g_gu_own, clip_factor, 0.06, WEIGHT_DECAY
    )
    new_down, new_down_m, new_down_v = adam_update(
        down_weight, down_m, down_v, g_down_own, clip_factor, 0.06, WEIGHT_DECAY
    )
    new_gains, new_gain_m, new_gain_v = adam_update(
        norm_gains, gain_m, gain_v, g_gains_own, clip_factor, 0.6, 0.0
    )
    return (
        block_out,
        input_grad,
        grad_norm,
        new_qkv,
        new_qkv_m,
        new_qkv_v,
        new_out,
        new_out_m,
        new_out_v,
        new_gu,
        new_gu_m,
        new_gu_v,
        new_down,
        new_down_m,
        new_down_v,
        new_gains,
        new_gain_m,
        new_gain_v,
    )


def solution(mesh):
    in_specs = (
        P(("dp", "seq"), None),
        P(("dp", "seq"), None),
        P("dp", None),
        P("dp"),
        P("dp", None),
        P(("dp", "seq"), None),
        P(("dp", "seq"), None),
        P(("dp", "seq"), None),
        P(("dp", "seq"), None),
        P(("dp", "seq"), None),
        P(("dp", "seq"), None),
        P(("dp", "seq"), None),
        P(("dp", "seq"), None),
        P(("dp", "seq"), None),
        P(("dp", "seq"), None),
        P(("dp", "seq"), None),
        P(("dp", "seq"), None),
        P(None, ("dp", "seq")),
        P(None, ("dp", "seq")),
        P(None, ("dp", "seq")),
    )
    out_specs = (
        P(("dp", "seq"), None),
        P(("dp", "seq"), None),
        P(),
        P(("dp", "seq"), None),
        P(("dp", "seq"), None),
        P(("dp", "seq"), None),
        P(("dp", "seq"), None),
        P(("dp", "seq"), None),
        P(("dp", "seq"), None),
        P(("dp", "seq"), None),
        P(("dp", "seq"), None),
        P(("dp", "seq"), None),
        P(("dp", "seq"), None),
        P(("dp", "seq"), None),
        P(("dp", "seq"), None),
        P(None, ("dp", "seq")),
        P(None, ("dp", "seq")),
        P(None, ("dp", "seq")),
    )
    return jax.shard_map(
        per_device, mesh=mesh, in_specs=in_specs, out_specs=out_specs, check_vma=False
    )
```

```python
import functools

import jax
import jax.numpy as jnp
from jax import lax
from jax.experimental import pallas as pl
from jax.experimental.pallas import tpu as pltpu
from jax.sharding import PartitionSpec as P

HEADS = 32
KV_HEADS = 4
HD = 64
FF = 5632
STEP = 10


NORM_EPS = 1e-05
ROPE_BASE = 10000.0
CLIP_NORM = 1.0
BETA_ONE = 0.9
BETA_TWO = 0.999
ADAM_EPS = 1e-08
WEIGHT_DECAY = 0.1
MASKED = -1e30


def matmul(left, right):
    return jnp.dot(left, right, preferred_element_type=jnp.float32)


def contract(left, right, left_dim, right_dim):
    return lax.dot_general(
        left, right, (((left_dim,), (right_dim,)), ((), ())), preferred_element_type=jnp.float32
    )


def rope_tables(positions):
    half_dim = HD // 2
    inverse = jnp.exp(-(2.0 * jnp.arange(half_dim, dtype=jnp.float32) / HD) * jnp.log(ROPE_BASE))
    angles = inverse[:, None] * positions.astype(jnp.float32)[None, :]
    return (jnp.cos(angles), jnp.sin(angles))


def rotate(rows, cos_table, sin_table):
    tokens = rows.shape[1]
    split = rows.reshape(-1, 2, HD // 2, tokens)
    first, second = (split[:, 0], split[:, 1])
    return jnp.stack(
        [first * cos_table - second * sin_table, second * cos_table + first * sin_table], 1
    ).reshape(rows.shape)


def norm_forward(rows_in, gain_row):
    inv_rms = lax.rsqrt(jnp.mean(rows_in * rows_in, axis=-1, keepdims=True) + NORM_EPS)
    return (inv_rms, rows_in * inv_rms * gain_row)


def norm_backward(rows_in, inv_rms, gain_row, gradient):
    weighted = gain_row * gradient
    back_rows = inv_rms * weighted - rows_in * inv_rms**3 * jnp.mean(
        weighted * rows_in, axis=-1, keepdims=True
    )
    return (back_rows, jnp.sum(gradient * rows_in * inv_rms, axis=0))


LOG2E = 1.4426950408889634
SCORE_SCALE = HD ** (-0.5)
SHARE = HEADS // KV_HEADS


def transposed(block):
    return block.astype(jnp.float32).T.astype(block.dtype)


def causal(tokens, valid):
    key_ids = lax.broadcasted_iota(jnp.int32, (tokens, tokens), 0)
    row_ids = lax.broadcasted_iota(jnp.int32, (tokens, tokens), 1)
    return (key_ids == row_ids) | ((key_ids < row_ids) & (valid > 0))


def attend_head(head, blocks, reach, valid, q_ref, kv_ref, group, k_rows, o_ref, full_ref, lse_ref):
    tokens = q_ref.shape[1]
    rows = pl.ds(pl.multiple_of(head * HD, HD), HD)
    query = q_ref[rows, :]

    def scores_of(dist):
        return matmul(k_rows[dist], query) * (SCORE_SCALE * LOG2E)

    def values_of(dist):
        return kv_ref[dist, group, HD:, :]

    scores = jnp.where(causal(tokens, valid), scores_of(0), MASKED)
    top = jnp.max(scores, 0, keepdims=True)
    weights = jnp.exp2(scores - top)
    total = jnp.sum(weights, 0, keepdims=True)
    acc = matmul(values_of(0), weights.astype(jnp.bfloat16))

    def step(dist, carry):
        top, total, acc = carry
        scores = jnp.where(dist < reach, scores_of(dist), MASKED)
        new_top = jnp.maximum(top, jnp.max(scores, 0, keepdims=True))
        weights = jnp.exp2(scores - new_top)
        fade = jnp.exp2(top - new_top)
        total = total * fade + jnp.sum(weights, 0, keepdims=True)
        acc = acc * fade + matmul(values_of(dist), weights.astype(jnp.bfloat16))
        return (new_top, total, acc)

    top, total, acc = lax.fori_loop(1, blocks, step, (top, total, acc))
    out = acc / total
    o_ref[rows, :] = out.astype(jnp.bfloat16)
    full_ref[rows, :] = out
    lse_ref[head] = top + jnp.log2(total)


def sum_to_owner(parts):
    size = lax.axis_size("seq")
    total = parts[size - 1]
    for step in range(size - 1, 0, -1):
        total = parts[step - 1] + lax.ppermute(
            total.astype(jnp.bfloat16), "seq", [(i, i - 1) for i in range(step, size)]
        ).astype(jnp.float32)
    return total


def adam_update(weight, first_mom, second_mom, gradient, clip_factor, rate, decay):
    step_grad = gradient * clip_factor
    first_new = BETA_ONE * first_mom + (1.0 - BETA_ONE) * step_grad
    second_new = BETA_TWO * second_mom + (1.0 - BETA_TWO) * step_grad * step_grad
    mean_hat = first_new / (1.0 - BETA_ONE**STEP)
    square_hat = second_new / (1.0 - BETA_TWO**STEP)
    weight_new = weight - rate * (mean_hat / (jnp.sqrt(square_hat) + ADAM_EPS) + decay * weight)
    return (weight_new, first_new, second_new)


MESH = pl.DeviceIdType.MESH


def flipped(index, bit):
    return index + (1 << bit) * (1 - 2 * ((index // (1 << bit)) % 2))


WHOLE, ROWS, BLOCKS = range(3)


class Gather:
    ahead = 3

    def __init__(self, kinds, pieces, shards, fulls, local_sems, send_sems, recv_sems):
        self.kinds, self.pieces, self.shards, self.fulls = (kinds, pieces, shards, fulls)
        self.local_sems, self.send_sems, self.recv_sems = (local_sems, send_sems, recv_sems)
        self.dp, self.seq = (lax.axis_index("dp"), lax.axis_index("seq"))
        self.dp_size, self.seq_size = (lax.axis_size("dp"), lax.axis_size("seq"))
        self.bits = self.dp_size.bit_length() - 1
        up = list(range(1, self.bits))
        self.orders = (up + [0], up[::-1] + [0])
        self.started = []
        self.done = set()

    def along(self, step):
        return {"seq": lax.rem(self.seq + step, self.seq_size)}

    def across(self, bit):
        return {"dp": flipped(self.dp, bit)}

    def sides(self, piece):
        return range(len(self.pieces[piece][2]))

    def kind(self, piece):
        return self.kinds[self.pieces[piece][0]]

    def source(self, piece, side):
        shard, _, sides = self.pieces[piece]
        return self.shards[shard].at[:, pl.ds(sides[side][0], sides[side][2])]

    def target(self, piece, side, index, depth):
        _, result, sides = self.pieces[piece]
        rows = pl.ds(pl.multiple_of(index * depth, depth), depth)
        return self.fulls[result].at[rows, pl.ds(sides[side][1], sides[side][2])]

    def own_target(self, piece, side):
        index = {
            WHOLE: self.dp * self.seq_size + self.seq, ROWS: self.seq, BLOCKS: self.dp
        }[self.kind(piece)]
        return self.target(piece, side, index, self.shards[self.pieces[piece][0]].shape[0])

    def local_copy(self, piece, side):
        return pltpu.make_async_copy(
            self.source(piece, side), self.own_target(piece, side), self.local_sems.at[piece, side]
        )

    def seq_copy(self, piece, side, step):
        return pltpu.make_async_remote_copy(
            src_ref=self.source(piece, side),
            dst_ref=self.own_target(piece, side),
            send_sem=self.send_sems.at[piece, side, self.dp_size + step],
            recv_sem=self.recv_sems.at[piece, side, self.dp_size + step],
            device_id=self.along(step),
            device_id_type=MESH,
        )

    def block_copy(self, piece, side, held, bit):
        depth = self.fulls[self.pieces[piece][1]].shape[0] // self.dp_size
        owner = self.dp
        for position in range(self.bits):
            if held >> position & 1:
                owner = flipped(owner, position)
        target = self.target(piece, side, owner, depth)
        early = not held and self.kind(piece) == BLOCKS
        return pltpu.make_async_remote_copy(
            src_ref=self.source(piece, side) if early else target,
            dst_ref=target,
            send_sem=self.send_sems.at[piece, side, held | 1 << bit],
            recv_sem=self.recv_sems.at[piece, side, held | 1 << bit],
            device_id=self.across(bit),
            device_id_type=MESH,
        )

    def start(self, copy):
        copy.start()
        self.started.append(copy)

    def begin(self):
        for piece in range(len(self.pieces)):
            for side in self.sides(piece):
                self.local_copy(piece, side).start()
        for piece in range(min(self.ahead, len(self.pieces))):
            self.send_rows(piece)

    def send_rows(self, piece):
        if self.kind(piece) == BLOCKS:
            return
        for step in range(1, self.seq_size):
            for side in self.sides(piece):
                self.start(self.seq_copy(piece, side, step))

    def advance(self, piece, stage):
        if (piece, stage) in self.done:
            return
        self.done.add((piece, stage))
        kind = self.kind(piece)
        if stage and kind == ROWS:
            return
        for side in self.sides(piece):
            order = self.orders[side] if kind != ROWS else []
            if stage == 0:
                if kind == WHOLE:
                    self.local_copy(piece, side).wait()
                if kind != BLOCKS:
                    for step in range(1, self.seq_size):
                        self.seq_copy(piece, side, step).wait_recv()
                held = [0]
            else:
                reached = [0]
                for bit in order[: stage - 1]:
                    reached += [block | 1 << bit for block in reached]
                held = [block | 1 << order[stage - 1] for block in reached]
                for block in reached:
                    self.block_copy(piece, side, block, order[stage - 1]).wait_recv()
            for bit in order[stage:]:
                for block in held:
                    self.start(self.block_copy(piece, side, block, bit))
        if stage == 0 and piece + self.ahead < len(self.pieces):
            self.send_rows(piece + self.ahead)

    def finish(self):
        for turn in range(len(self.pieces) + self.bits):
            for piece in range(len(self.pieces)):
                if 0 <= turn - piece <= self.bits:
                    self.advance(piece, turn - piece)
        for piece in range(len(self.pieces)):
            if self.kind(piece) != WHOLE:
                for side in self.sides(piece):
                    self.local_copy(piece, side).wait()
        for copy in self.started:
            copy.wait_send()


def gather_scratch(pieces):
    slots = lax.axis_size("dp") + lax.axis_size("seq")
    return [
        pltpu.SemaphoreType.DMA((pieces, 2)),
        pltpu.SemaphoreType.DMA((pieces, 2, slots)),
        pltpu.SemaphoreType.DMA((pieces, 2, slots)),
    ]


def gather_kernel(kinds, pieces, *refs):
    count, sems = (len(kinds), len(refs) - 3)
    gather = Gather(kinds, pieces, refs[:count], refs[count:sems], *refs[sems:])
    greet()
    gather.begin()
    gather.finish()


def gather_all(kinds, shards, shapes, pieces, collective_id):
    hbm = pl.BlockSpec(memory_space=pl.ANY)
    return pl.pallas_call(
        functools.partial(gather_kernel, kinds, pieces),
        out_shape=[jax.ShapeDtypeStruct(shape, jnp.bfloat16) for shape in shapes],
        in_specs=[hbm] * len(shards),
        out_specs=[hbm] * len(shapes),
        scratch_shapes=gather_scratch(len(pieces)),
        compiler_params=pltpu.CompilerParams(collective_id=collective_id, has_side_effects=True),
        name="gather",
    )(*shards)


def attend_kernel(kinds, pieces, info, q_ref, kv_ref, *refs):
    count = len(kinds)
    shards = refs[:count]
    o_ref, full_ref, lse_ref, kv_all_ref = refs[count : count + 4]
    fulls = refs[count + 4 : -7]
    k_rows, slots, kv_send, kv_recv = refs[-7:-3]
    gather = Gather(kinds, pieces, shards, fulls, *refs[-3:])
    seq, seq_size = (gather.seq, gather.seq_size)
    reach, valid = (info[0], info[1])
    greet()

    def kv_copy(group, step):
        return pltpu.make_async_remote_copy(
            src_ref=kv_ref.at[group],
            dst_ref=slots.at[step, group],
            send_sem=kv_send.at[step, group],
            recv_sem=kv_recv.at[step, group],
            device_id=gather.along(step),
            device_id_type=MESH,
        )

    for group in range(KV_HEADS):
        for step in range(1, seq_size):

            @pl.when(seq + step < seq_size)
            def _():
                kv_copy(group, step).start()

    gather.begin()
    gather.advance(0, 0)
    slots[0] = kv_ref[...]
    beside = {1: [(0, 1)], 3: [(0, 2)], 5: [(1, 0)], 7: [(0, 3), (1, 1), (2, 0)]}
    for group in range(KV_HEADS):
        k_rows[0] = transposed(kv_ref[group, :HD, :])
        for step in range(1, seq_size):

            @pl.when(seq >= step)
            def _():
                kv_copy(group, step).wait_recv()
                k_rows[step] = transposed(slots[step, group, :HD, :])

        for part in range(2):

            @pl.loop(group * SHARE + part * SHARE // 2, group * SHARE + (part + 1) * SHARE // 2)
            def _(head):
                attend_head(
                    head, seq + 1, reach, valid, q_ref, slots, group, k_rows, o_ref, full_ref, lse_ref
                )

            for event in beside.get(group * 2 + part, []):
                gather.advance(*event)
    for step in range(seq_size):

        @pl.when(seq >= step)
        def _():
            kv_all_ref[step] = slots[step]

        @pl.when(seq < step)
        def _():
            kv_all_ref[step] = jnp.zeros_like(kv_ref)

    for group in range(KV_HEADS):
        for step in range(1, seq_size):

            @pl.when(seq + step < seq_size)
            def _():
                kv_copy(group, step).wait_send()

    gather.finish()


def attend_forward(info, query, kv, kinds, shards, shapes, pieces, collective_id):
    tokens = query.shape[1]
    seq_size = lax.axis_size("seq")
    count = len(shards)
    vmem = pl.BlockSpec(memory_space=pltpu.VMEM)
    hbm = pl.BlockSpec(memory_space=pl.ANY)
    out = pl.pallas_call(
        functools.partial(attend_kernel, kinds, pieces),
        out_shape=[
            jax.ShapeDtypeStruct(query.shape, jnp.bfloat16),
            jax.ShapeDtypeStruct(query.shape, jnp.float32),
            jax.ShapeDtypeStruct((HEADS, 1, tokens), jnp.float32),
            jax.ShapeDtypeStruct((seq_size, *kv.shape), kv.dtype),
            *[jax.ShapeDtypeStruct(shape, jnp.bfloat16) for shape in shapes],
        ],
        in_specs=[pl.BlockSpec(memory_space=pltpu.SMEM), vmem, vmem] + [hbm] * count,
        out_specs=[vmem] * 4 + [hbm] * len(shapes),
        scratch_shapes=[
            pltpu.VMEM((seq_size, tokens, HD), jnp.bfloat16),
            pltpu.VMEM((seq_size, *kv.shape), kv.dtype),
            pltpu.SemaphoreType.DMA((seq_size, KV_HEADS)),
            pltpu.SemaphoreType.DMA((seq_size, KV_HEADS)),
            *gather_scratch(len(pieces)),
        ],
        compiler_params=pltpu.CompilerParams(
            collective_id=collective_id, has_side_effects=True, vmem_limit_bytes=48 * 2**20
        ),
        name="attend_forward",
    )(info, query, kv, *shards)
    return (out[:4], out[4:])


def squares_of(value):
    return jnp.sum((value * value).reshape(-1, 8, 128), 0)


def apart(index, distance, bits):
    return sum(
        lax.rem(index // (1 << bit) + distance // (1 << bit), 2) * (1 << bit) for bit in range(bits)
    )


class Scatter:
    def __init__(self, tiles, shape, refs, deliver):
        self.tiles, (self.size, self.depth, self.columns) = (tiles, shape)
        self.half = self.columns // 2
        self.deliver = deliver
        self.dp, self.seq = (lax.axis_index("dp"), lax.axis_index("seq"))
        self.dp_size, self.seq_size = (lax.axis_size("dp"), lax.axis_size("seq"))
        self.hops = self.size.bit_length() - 1
        refs = list(refs)
        self.own, self.other, self.came = (refs.pop(0), refs.pop(0), refs.pop(0))
        self.sent, self.got, self.kept = ([None], [None], [None])
        for _ in range(self.hops):
            self.sent.append(refs.pop(0))
            self.got.append(refs.pop(0))
            self.kept.append(refs.pop(0))
        self.rows, self.rows_got, self.send_sems, self.recv_sems = refs
        self.steps = tiles + self.hops + 2

    @staticmethod
    def scratch(shape):
        size, depth, columns = shape
        half = columns // 2
        hops = size.bit_length() - 1
        seq_size = lax.axis_size("seq")
        low = jnp.bfloat16
        shapes = [
            pltpu.VMEM((size, depth, columns), low),
            pltpu.VMEM((size, depth, columns), low),
            pltpu.VMEM((2, size, depth, columns), low),
        ]
        for hop in range(1, hops + 1):
            shapes.append(pltpu.VMEM((2, 2, size >> hop, depth, half), low))
            shapes.append(pltpu.VMEM((2, 2, size >> hop, depth, half), low))
            shapes.append(pltpu.VMEM((2, size >> hop, depth, half), low))
        shapes.append(pltpu.VMEM((2, 2, depth, half), low))
        shapes.append(pltpu.VMEM((2, seq_size - 1, 2, depth // seq_size, half), low))
        lanes = max(2, seq_size - 1)
        shapes.append(pltpu.SemaphoreType.DMA((hops + 2, 2, lanes)))
        shapes.append(pltpu.SemaphoreType.DMA((hops + 2, 2, lanes)))
        return shapes

    def bit(self, hop, side):
        return hop if side == 0 else self.hops + 1 - hop

    def copy(self, kind, slot, lane, src, dst, device):
        return pltpu.make_async_remote_copy(
            src_ref=src,
            dst_ref=dst,
            send_sem=self.send_sems.at[kind, slot, lane],
            recv_sem=self.recv_sems.at[kind, slot, lane],
            device_id=device,
            device_id_type=MESH,
        )

    def copies(self, kind, slot):
        if kind == 0:
            return [
                self.copy(0, slot, 0, self.other, self.came.at[slot], {"dp": flipped(self.dp, 0)})
            ]
        if kind <= self.hops:
            return [
                self.copy(
                    kind,
                    slot,
                    side,
                    self.sent[kind].at[slot, side],
                    self.got[kind].at[slot, side],
                    {"dp": flipped(self.dp, self.bit(kind, side))},
                )
                for side in range(2)
            ]
        own = self.depth // self.seq_size
        result = []
        for step in range(1, self.seq_size):
            there = lax.rem(self.seq + step, self.seq_size)
            window = pl.ds(pl.multiple_of(there * own, own), own)
            result.append(
                self.copy(
                    kind,
                    slot,
                    step - 1,
                    self.rows.at[slot, :, window, :],
                    self.rows_got.at[slot, step - 1],
                    {"seq": there},
                )
            )
        return result

    def send(self, kind, tile):
        for copy in self.copies(kind, lax.rem(tile, 2)):
            copy.start()

    def sent_before(self, kind, tile, back):
        @pl.when(tile >= back)
        def _():
            for copy in self.copies(kind, lax.rem(tile + 2 - back, 2)):
                copy.wait_send()

    def plus(self, into, one, two):
        rows = 64 if self.depth % 64 == 0 else 16

        @pl.loop(0, self.depth // rows)
        def _(chunk):
            part = pl.ds(pl.multiple_of(chunk * rows, rows), rows)
            into[part, :] = one[part, :] + two[part, :]

    def stage(self, kind, tile):
        slot = lax.rem(tile, 2)
        for copy in self.copies(kind, slot):
            copy.wait_recv()
        if kind == self.hops + 1:
            own = self.depth // self.seq_size
            window = pl.ds(pl.multiple_of(self.seq * own, own), own)
            for side in range(2):
                total = self.rows[slot, side, window, :].astype(jnp.float32)
                for step in range(self.seq_size - 1):
                    total = total + self.rows_got[slot, step, side].astype(jnp.float32)
                self.deliver(tile, side, total)
            return
        self.sent_before(kind + 1, tile, 2)
        size = self.size >> kind
        for side in range(2):
            columns = pl.ds(side * self.half, self.half)
            for block in range(size):
                if kind == 0:
                    one, two = (self.own.at[block, :, columns], self.came.at[slot, block, :, columns])
                else:
                    one, two = (self.kept[kind].at[side, block], self.got[kind].at[slot, side, block])
                if kind == self.hops:
                    into = self.rows.at[slot, side]
                elif side == 0:
                    place = self.sent if block % 2 else self.kept
                    index = (block // 2,)
                    into = place[kind + 1].at[((slot, 0) if block % 2 else (0,)) + index]
                else:
                    away = block >= size // 2
                    place = self.sent if away else self.kept
                    index = (block - size // 2 if away else block,)
                    into = place[kind + 1].at[((slot, 1) if away else (1,)) + index]
                self.plus(into, one, two)
        self.send(kind + 1, tile)

    def step(self, now, begin):
        for kind in range(self.hops + 1, -1, -1):
            tile = now - kind - 1

            @pl.when((tile >= 0) & (tile < self.tiles))
            def _():
                self.stage(kind, tile)

        @pl.when((now >= 0) & (now < self.tiles))
        def _():
            self.sent_before(0, now, 1)
            begin(now)

    def finish(self):
        for kind in range(self.hops + 2):
            for tile in range(max(0, self.tiles - (1 if kind == 0 else 2)), self.tiles):
                for copy in self.copies(kind, tile % 2):
                    copy.wait_send()


def greet():
    dp, seq = (lax.axis_index("dp"), lax.axis_index("seq"))
    dp_size, seq_size = (lax.axis_size("dp"), lax.axis_size("seq"))
    barrier = pltpu.get_barrier_semaphore()
    others = [{"seq": lax.rem(seq + step, seq_size)} for step in range(1, seq_size)]
    others += [{"dp": flipped(dp, bit)} for bit in range(dp_size.bit_length() - 1)]
    for other in others:
        pl.semaphore_signal(barrier, inc=1, device_id=other, device_id_type=MESH)
    pl.semaphore_wait(barrier, len(others))


TILE = 512


def mlp_kernel(
    rows_ref, turned_ref, grad_hbm, gu_ref, down_ref,
    down_grad, inner_hbm, out_hbm, sum_ref,
    grad_ref, gu_buf, down_buf, hidden, d_gu, product, inner_ref, out_ref,
    load_sems, store_sems, *scratch
):
    tokens, model = rows_ref.shape
    tiles = FF // TILE
    size, depth, columns = scratch[0].shape

    def deliver(tile, side, total):
        sum_ref[:, pl.ds(pl.multiple_of(side * FF + tile * TILE, TILE), TILE)] = total

    scatter = Scatter(tiles, (size, depth, columns), scratch, deliver)
    bits = scatter.hops + 1

    def loads(tile, slot):
        start = pl.multiple_of(tile * TILE, TILE)
        return [
            pltpu.make_async_copy(
                gu_ref.at[:, pl.ds(start, TILE)], gu_buf.at[slot, 0], load_sems.at[slot, 0]
            ),
            pltpu.make_async_copy(
                gu_ref.at[:, pl.ds(pl.multiple_of(FF + start, TILE), TILE)],
                gu_buf.at[slot, 1],
                load_sems.at[slot, 1],
            ),
            pltpu.make_async_copy(
                down_ref.at[pl.ds(start, TILE), :], down_buf.at[slot], load_sems.at[slot, 2]
            ),
        ]

    def store(tile):
        start = pl.multiple_of(tile * TILE, TILE)
        return pltpu.make_async_copy(
            product, down_grad.at[pl.ds(start, TILE), :], store_sems.at[0]
        )

    grad_load = pltpu.make_async_copy(grad_hbm, grad_ref, store_sems.at[1])
    inner_store = pltpu.make_async_copy(inner_ref, inner_hbm, store_sems.at[2])
    out_store = pltpu.make_async_copy(out_ref, out_hbm, store_sems.at[3])
    grad_load.start()
    for copy in loads(0, 0):
        copy.start()
    inner_ref[...] = jnp.zeros_like(inner_ref)
    out_ref[...] = jnp.zeros_like(out_ref)
    greet()
    grad_load.wait()

    def begin(tile):
        slot = lax.rem(tile, 2)
        for copy in loads(tile, slot):
            copy.wait()

        @pl.when(tile + 1 < tiles)
        def _():
            for copy in loads(tile + 1, 1 - slot):
                copy.start()

        chunk_rows = min(256, tokens)

        @pl.loop(0, tokens // chunk_rows)
        def _(chunk):
            part = pl.ds(pl.multiple_of(chunk * chunk_rows, chunk_rows), chunk_rows)
            rows = rows_ref[part, :]
            gate = matmul(rows, gu_buf[slot, 0])
            up = matmul(rows, gu_buf[slot, 1])
            d_hidden = contract(grad_ref[part, :], down_buf[slot], 1, 1)
            sigmoid_gate = 1.0 / (1.0 + jnp.exp(-gate))
            silu = gate * sigmoid_gate
            hidden[part, :] = (silu * up).astype(jnp.bfloat16)
            d_gate = d_hidden * up * sigmoid_gate * (1.0 + gate * (1.0 - sigmoid_gate))
            d_gu[part, :TILE] = d_gate.astype(jnp.bfloat16)
            d_gu[part, TILE:] = (d_hidden * silu).astype(jnp.bfloat16)

        def blocks_of(core, into):
            @pl.loop(0, size)
            def _(block):
                owner = apart(scatter.dp, 2 * block + core, bits)
                part = pl.ds(pl.multiple_of(owner * depth, depth), depth)
                into[block] = matmul(turned_ref[part, :], d_gu[...]).astype(jnp.bfloat16)

        blocks_of(1, scatter.other)
        scatter.send(0, tile)
        blocks_of(0, scatter.own)

        @pl.when(tile >= 1)
        def _():
            store(tile - 1).wait()

        hidden_turned = transposed(hidden[...])

        @pl.loop(0, model // TILE)
        def _(chunk):
            part = pl.ds(pl.multiple_of(chunk * TILE, TILE), TILE)
            inner_ref[:, part] += contract(d_gu[:, :TILE], gu_buf[slot, 0, part, :], 1, 1) + contract(
                d_gu[:, TILE:], gu_buf[slot, 1, part, :], 1, 1
            )
            out_ref[:, part] += matmul(hidden[...], down_buf[slot, :, part])
            product[:, part] = matmul(hidden_turned, grad_ref[:, part]).astype(jnp.bfloat16)

        store(tile).start()

        @pl.when(tile == tiles - 1)
        def _():
            inner_store.start()
            out_store.start()

    @pl.loop(0, scatter.steps)
    def _(now):
        scatter.step(now, begin)

    store(tiles - 1).wait()
    inner_store.wait()
    out_store.wait()
    scatter.finish()


def feed_forward(rows, turned, grad, w_gu, w_down, collective_id):
    tokens, model = rows.shape
    dp_size, seq_size = (lax.axis_size("dp"), lax.axis_size("seq"))
    shape = (dp_size // 2, model // dp_size, 2 * TILE)
    vmem = pl.BlockSpec(memory_space=pltpu.VMEM)
    hbm = pl.BlockSpec(memory_space=pl.ANY)
    return pl.pallas_call(
        mlp_kernel,
        out_shape=[
            jax.ShapeDtypeStruct((FF, model), jnp.bfloat16),
            jax.ShapeDtypeStruct((tokens, model), jnp.float32),
            jax.ShapeDtypeStruct((tokens, model), jnp.float32),
            jax.ShapeDtypeStruct((model // (dp_size * seq_size), 2 * FF), jnp.float32),
        ],
        in_specs=[vmem, vmem, hbm, hbm, hbm],
        out_specs=[hbm, hbm, hbm, vmem],
        scratch_shapes=[
            pltpu.VMEM((tokens, model), jnp.bfloat16),
            pltpu.VMEM((2, 2, model, TILE), jnp.bfloat16),
            pltpu.VMEM((2, TILE, model), jnp.bfloat16),
            pltpu.VMEM((tokens, TILE), jnp.bfloat16),
            pltpu.VMEM((tokens, 2 * TILE), jnp.bfloat16),
            pltpu.VMEM((TILE, model), jnp.bfloat16),
            pltpu.VMEM((tokens, model), jnp.float32),
            pltpu.VMEM((tokens, model), jnp.float32),
            pltpu.SemaphoreType.DMA((2, 3)),
            pltpu.SemaphoreType.DMA((4,)),
            *Scatter.scratch(shape),
        ],
        compiler_params=pltpu.CompilerParams(
            collective_id=collective_id, has_side_effects=True, vmem_limit_bytes=60 * 2**20
        ),
        name="feed_forward",
    )(rows, turned, grad, w_gu, w_down)


def load_tile(scatter, source, load_sems):
    def copies(tile):
        columns = pl.ds(
            pl.multiple_of(tile * scatter.columns, scatter.columns), scatter.columns
        )
        result = []
        for block in range(2 * scatter.size):
            owner = apart(scatter.dp, block, scatter.hops + 1)
            into = scatter.other if block % 2 else scatter.own
            result.append(
                pltpu.make_async_copy(
                    source.at[owner, :, columns], into.at[block // 2], load_sems.at[block]
                )
            )
        return result

    def begin(tile):
        for copy in copies(tile):
            copy.start()

    def complete(now):
        @pl.when((now >= 0) & (now < scatter.tiles))
        def _():
            for copy in copies(now):
                copy.wait()
            scatter.send(0, now)

    return (begin, complete)


def delivered(ref, columns):
    def deliver(tile, side, total):
        start = pl.multiple_of(tile * columns + side * (columns // 2), columns // 2)
        ref[:, pl.ds(start, columns // 2)] = total

    return deliver


def backward_kernel(
    info, q_ref, kv_ref, full_ref, lse_ref, do_ref, down_ref, proj_ref,
    dq_ref, dkv_ref, down_sum, proj_sum,
    k_rows, v_rows, dk_acc, dv_acc, parts, parts_got, part_sends, part_recvs, load_sems, *scratch
):
    tokens = q_ref.shape[1]
    reach, valid = (info[0], info[1])
    count = len(scratch) // 2
    down = Scatter(
        down_ref.shape[2] // scratch[0].shape[2],
        scratch[0].shape,
        scratch[:count],
        delivered(down_sum, scratch[0].shape[2]),
    )
    proj = Scatter(
        proj_ref.shape[2] // scratch[count].shape[2],
        scratch[count].shape,
        scratch[count:],
        delivered(proj_sum, scratch[count].shape[2]),
    )
    seq, seq_size = (down.seq, down.seq_size)
    blocks = seq + 1
    greet()

    def part_copy(group, dist):
        return pltpu.make_async_remote_copy(
            src_ref=parts.at[dist, group],
            dst_ref=parts_got.at[dist, group],
            send_sem=part_sends.at[dist, group],
            recv_sem=part_recvs.at[dist, group],
            device_id={"seq": lax.rem(seq + seq_size - dist, seq_size)},
            device_id_type=MESH,
        )

    def one_head(head):
        group = head // SHARE
        rows = pl.ds(pl.multiple_of(head * HD, HD), HD)

        @pl.when(lax.rem(head, SHARE) == 0)
        def _():
            dk_acc[...] = jnp.zeros_like(dk_acc)
            dv_acc[...] = jnp.zeros_like(dv_acc)

            @pl.loop(0, blocks)
            def _(dist):
                k_rows[dist] = transposed(kv_ref[dist, group, :HD, :])
                v_rows[dist] = transposed(kv_ref[dist, group, HD:, :])

        query, grad = (q_ref[rows, :], do_ref[rows, :])
        query_rows, grad_rows = (transposed(query), transposed(grad))
        lse = lse_ref[head]
        centre = jnp.sum(grad.astype(jnp.float32) * full_ref[rows, :], 0, keepdims=True)

        def block(dist, mask):
            scores = matmul(k_rows[dist], query) * (SCORE_SCALE * LOG2E)
            prob = jnp.where(mask, jnp.exp2(scores - lse), 0.0)
            d_prob = matmul(v_rows[dist], grad)
            d_score = (prob * (d_prob - centre) * SCORE_SCALE).astype(jnp.bfloat16)
            dv_acc[dist] += matmul(prob.astype(jnp.bfloat16), grad_rows)
            dk_acc[dist] += matmul(d_score, query_rows)
            return matmul(kv_ref[dist, group, :HD, :], d_score)

        d_query = block(0, causal(tokens, valid))
        dq_ref[rows, :] = lax.fori_loop(
            1, blocks, lambda dist, acc: acc + block(dist, dist < reach), d_query
        )

        @pl.when(lax.rem(head, SHARE) == SHARE - 1)
        def _():
            dkv_ref[group, :HD, :] = dk_acc[0].T
            dkv_ref[group, HD:, :] = dv_acc[0].T
            for dist in range(1, seq_size):

                @pl.when(seq >= dist)
                def _():
                    parts[dist, group, :HD, :] = dk_acc[dist].T.astype(jnp.bfloat16)
                    parts[dist, group, HD:, :] = dv_acc[dist].T.astype(jnp.bfloat16)
                    part_copy(group, dist).start()

    begin_down, complete_down = load_tile(down, down_ref, load_sems.at[0])
    begin_proj, complete_proj = load_tile(proj, proj_ref, load_sems.at[1])
    steps = down.steps
    lag = steps - proj.steps

    @pl.loop(0, steps)
    def _(now):
        down.step(now, begin_down)
        proj.step(now - lag, begin_proj)
        complete_down(now)
        complete_proj(now - lag)

        @pl.loop(now * HEADS // steps, (now + 1) * HEADS // steps)
        def _(head):
            one_head(head)

    down.finish()
    proj.finish()
    for dist in range(1, seq_size):

        @pl.when(seq + dist < seq_size)
        def _():
            for group in range(KV_HEADS):
                part_copy(group, dist).wait_recv()
            dkv_ref[...] += parts_got[dist].astype(jnp.float32)

        @pl.when(seq >= dist)
        def _():
            for group in range(KV_HEADS):
                part_copy(group, dist).wait_send()


def attend_backward(info, query, kv, full, lse, grad, g_down, g_out, collective_id):
    tokens, reach = (query.shape[1], kv.shape[0])
    seq_size = lax.axis_size("seq")
    vmem = pl.BlockSpec(memory_space=pltpu.VMEM)
    hbm = pl.BlockSpec(memory_space=pl.ANY)
    down_shape = (g_down.shape[0] // 2, g_down.shape[1], 256)
    proj_shape = (g_out.shape[0] // 2, g_out.shape[1], 512)
    return pl.pallas_call(
        backward_kernel,
        out_shape=[
            jax.ShapeDtypeStruct(query.shape, jnp.float32),
            jax.ShapeDtypeStruct((KV_HEADS, 2 * HD, tokens), jnp.float32),
            jax.ShapeDtypeStruct((g_down.shape[1] // seq_size, g_down.shape[2]), jnp.float32),
            jax.ShapeDtypeStruct((g_out.shape[1] // seq_size, g_out.shape[2]), jnp.float32),
        ],
        in_specs=[pl.BlockSpec(memory_space=pltpu.SMEM)] + [vmem] * 5 + [hbm] * 2,
        out_specs=[vmem] * 4,
        scratch_shapes=[
            pltpu.VMEM((reach, tokens, HD), jnp.bfloat16),
            pltpu.VMEM((reach, tokens, HD), jnp.bfloat16),
            pltpu.VMEM((reach, tokens, HD), jnp.float32),
            pltpu.VMEM((reach, tokens, HD), jnp.float32),
            pltpu.VMEM((reach, KV_HEADS, 2 * HD, tokens), jnp.bfloat16),
            pltpu.VMEM((reach, KV_HEADS, 2 * HD, tokens), jnp.bfloat16),
            pltpu.SemaphoreType.DMA((reach, KV_HEADS)),
            pltpu.SemaphoreType.DMA((reach, KV_HEADS)),
            pltpu.SemaphoreType.DMA((2, g_down.shape[0])),
            *Scatter.scratch(down_shape),
            *Scatter.scratch(proj_shape),
        ],
        compiler_params=pltpu.CompilerParams(
            collective_id=collective_id, has_side_effects=True, vmem_limit_bytes=60 * 2**20
        ),
        name="attend_backward",
    )(info, query, kv, full, lse, grad, g_down, g_out)


def everyone():
    seq_size = lax.axis_size("seq")
    devices = lax.axis_size("dp") * seq_size
    me = lax.axis_index("dp") * seq_size + lax.axis_index("seq")

    def device(distance):
        other = lax.rem(me + distance, devices)
        return (other, (other // seq_size, lax.rem(other, seq_size)))

    return (me, devices, device)


def last_kernel(
    source, gains_ref, squares_ref,
    result, gains_sum, total_ref,
    load_sems, gains_got, mine, totals_got, tile_sends, tile_recvs, *scratch
):
    columns = scratch[0].shape[2]
    scatter = Scatter(
        source.shape[2] // columns, scratch[0].shape, scratch, delivered(result, columns)
    )
    me, devices, device = everyone()

    def copy(kind, distance):
        other, place = device(distance)
        return pltpu.make_async_remote_copy(
            src_ref=mine if kind else gains_ref.at[other],
            dst_ref=(totals_got if kind else gains_got).at[distance],
            send_sem=tile_sends.at[kind, distance],
            recv_sem=tile_recvs.at[kind, distance],
            device_id=place,
            device_id_type=MESH,
        )

    barrier = pltpu.get_barrier_semaphore()

    @pl.loop(1, devices)
    def _(distance):
        pl.semaphore_signal(barrier, inc=1, device_id=device(distance)[1], device_id_type=MESH)

    pl.semaphore_wait(barrier, devices - 1)

    @pl.loop(1, devices)
    def _(distance):
        copy(0, distance).start()

    begin, complete = load_tile(scatter, source, load_sems)

    @pl.loop(0, scatter.steps)
    def _(now):
        scatter.step(now, begin)
        complete(now)

    @pl.loop(1, devices)
    def _(distance):
        copy(0, distance).wait()

    gains = gains_ref[me] + jnp.sum(gains_got[1:], 0)
    gains_sum[...] = gains
    lanes = result.shape[1] // 128
    squares = squares_ref[...] + gains * gains
    for lane in range(lanes):
        block = result[:, lane * 128 : (lane + 1) * 128]
        squares = squares + jnp.sum((block * block).reshape(-1, 8, 128), 0)
    mine[...] = squares

    @pl.loop(1, devices)
    def _(distance):
        copy(1, distance).start()

    @pl.loop(1, devices)
    def _(distance):
        copy(1, distance).wait()

    total = jnp.sum(squares + jnp.sum(totals_got[1:], 0))
    total_ref[...] = jnp.full((8, 128), total, jnp.float32)
    scatter.finish()


def last_sums(parts, gains, squares, columns, collective_id):
    devices = gains.shape[0]
    shape = (parts.shape[0] // 2, parts.shape[1], columns)
    vmem = pl.BlockSpec(memory_space=pltpu.VMEM)
    return pl.pallas_call(
        last_kernel,
        out_shape=[
            jax.ShapeDtypeStruct(
                (parts.shape[1] // lax.axis_size("seq"), parts.shape[2]), jnp.float32
            ),
            jax.ShapeDtypeStruct((8, 128), jnp.float32),
            jax.ShapeDtypeStruct((8, 128), jnp.float32),
        ],
        in_specs=[pl.BlockSpec(memory_space=pl.ANY), vmem, vmem],
        out_specs=[vmem] * 3,
        scratch_shapes=[
            pltpu.SemaphoreType.DMA((parts.shape[0],)),
            pltpu.VMEM((devices, 8, 128), jnp.float32),
            pltpu.VMEM((8, 128), jnp.float32),
            pltpu.VMEM((devices, 8, 128), jnp.float32),
            pltpu.SemaphoreType.DMA((2, devices)),
            pltpu.SemaphoreType.DMA((2, devices)),
            *Scatter.scratch(shape),
        ],
        compiler_params=pltpu.CompilerParams(
            collective_id=collective_id, has_side_effects=True, vmem_limit_bytes=48 * 2**20
        ),
        name="last_sums",
    )(parts, gains, squares)


def per_device(
    hidden_in,
    out_grad,
    seq_lengths,
    seq_counts,
    segment_ids,
    qkv_weight,
    qkv_m,
    qkv_v,
    out_weight,
    out_m,
    out_v,
    gate_up_weight,
    gate_up_m,
    gate_up_v,
    down_weight,
    down_m,
    down_v,
    norm_gains,
    gain_m,
    gain_v,
):
    tok_dev = hidden_in.shape[0]
    q_width = HEADS * HD
    kv_width = KV_HEADS * HD
    seg_all = segment_ids[0]
    lengths = seq_lengths[0]
    seq_index = lax.axis_index("seq")
    offset = seq_index * tok_dev
    seg_local = lax.dynamic_slice_in_dim(seg_all, offset, tok_dev, 0)
    starts = jnp.cumsum(lengths, dtype=jnp.int32) - lengths
    slot_ids = jnp.arange(lengths.shape[0], dtype=jnp.int32)
    seq_start = jnp.sum(
        jnp.where(seg_local[:, None] == slot_ids[None, :], starts[None, :], 0),
        axis=1,
        dtype=jnp.int32,
    )
    positions = offset + jnp.arange(tok_dev, dtype=jnp.int32) - seq_start
    cos_table, sin_table = rope_tables(positions)
    valid = (seg_local[0] < seq_counts[0]).astype(jnp.int32)
    reach = jnp.where(valid > 0, seq_index - seq_start[0] // tok_dev + 1, 1)
    info = jnp.stack([reach, valid]).astype(jnp.int32)

    devices = lax.axis_size("dp") * lax.axis_size("seq")
    own = norm_gains.shape[1]
    gain_rows = jnp.pad(norm_gains.astype(jnp.bfloat16), ((0, 14), (0, 128 - own)))
    width = qkv_weight.shape[1] // 4
    model = out_weight.shape[1]
    seq_size = lax.axis_size("seq")
    gu_shard = gate_up_weight.astype(jnp.bfloat16)
    early = 3 * TILE
    w_qkv, gain_rows, gu_block = gather_all(
        [WHOLE, WHOLE, ROWS],
        [qkv_weight.astype(jnp.bfloat16), gain_rows, gu_shard],
        [
            (devices * qkv_weight.shape[0], 4 * width),
            (devices * 16, 128),
            (seq_size * gu_shard.shape[0], 2 * early),
        ],
        [
            (1, 1, ((0, 0, 128),)),
            (0, 0, ((0, 0, width), (width, width, width))),
            (0, 0, ((2 * width, 2 * width, width), (3 * width, 3 * width, width))),
            (2, 2, ((0, 0, early), (FF, early, early))),
        ],
        1,
    )
    w_gain = jnp.moveaxis(gain_rows.reshape(devices, 16, 128)[:, :2, :own], 1, 0).reshape(2, -1)
    gain_attn = w_gain[0].astype(jnp.float32)
    gain_mlp = w_gain[1].astype(jnp.float32)
    residual = hidden_in.astype(jnp.float32)
    inv_one, normed = norm_forward(residual, gain_attn)
    normed_low = normed.astype(jnp.bfloat16)
    qkv_out = contract(w_qkv, normed_low, 0, 1)
    query = rotate(qkv_out[:q_width], cos_table, sin_table).astype(jnp.bfloat16)
    key = rotate(qkv_out[q_width : q_width + kv_width], cos_table, sin_table).astype(jnp.bfloat16)
    value = qkv_out[q_width + kv_width :].astype(jnp.bfloat16)
    kv_own = jnp.concatenate(
        [key.reshape(KV_HEADS, HD, tok_dev), value.reshape(KV_HEADS, HD, tok_dev)], 1
    )
    down_depth = down_weight.shape[0]
    spare = -down_depth % 16
    shards = [
        out_weight.astype(jnp.bfloat16),
        jnp.pad(down_weight.astype(jnp.bfloat16), ((0, spare), (0, 0))),
        gu_shard,
        gu_block,
    ]
    shapes = [(devices * shard.shape[0], shard.shape[1]) for shard in shards[:3]]
    half, quarter = (model // 2, model // 4)
    pieces = [
        (3, 2, ((0, 0, early), (early, FF, early))),
        (0, 0, ((0, 0, half), (half, half, half))),
        (1, 1, ((0, 0, quarter), (quarter, quarter, quarter))),
        (1, 1, ((half, half, quarter), (half + quarter, half + quarter, quarter))),
    ]
    for low, high in ((3, 6), (6, 9), (9, 10), (10, 11)):
        low, high = (low * TILE, high * TILE)
        pieces.append((2, 2, ((low, low, high - low), (FF + low, FF + low, high - low))))
    (attended, attended_full, lse, kv_all), (w_out, w_down, w_gu) = attend_forward(
        info, query, kv_own, [WHOLE, WHOLE, WHOLE, BLOCKS], shards, shapes, pieces, 2
    )
    if spare:
        w_down = w_down.reshape(devices, -1, model)[:, :down_depth].reshape(-1, model)
    mid_rows = residual + contract(attended, w_out, 0, 0)
    inv_two, normed_two = norm_forward(mid_rows, gain_mlp)
    inner_rows = normed_two.astype(jnp.bfloat16)

    g_down, d_inner, out_rows, g_gu_own = feed_forward(
        inner_rows, inner_rows.T, out_grad, w_gu, w_down, 3
    )
    block_out = (mid_rows + out_rows).astype(jnp.bfloat16)
    back_two, g_gain_two = norm_backward(mid_rows, inv_two, gain_mlp, d_inner)
    d_mid = out_grad.astype(jnp.float32) + back_two
    d_branch = d_mid.astype(jnp.bfloat16)
    d_attended = contract(w_out, d_branch, 1, 1).astype(jnp.bfloat16)
    dp_size = lax.axis_size("dp")
    if spare:
        g_down = jnp.pad(
            g_down.reshape(devices, down_depth, model), ((0, 0), (0, spare), (0, 0))
        )
    g_down = g_down.reshape(dp_size, -1, model)
    g_out = matmul(attended, d_branch).astype(jnp.bfloat16).reshape(dp_size, -1, model)
    d_query, d_kv, g_down_own, g_out_own = attend_backward(
        info, query, kv_all, attended_full, lse, d_attended, g_down, g_out, 4
    )
    g_down_own = g_down_own[:down_depth]
    d_qkv = jnp.concatenate(
        [
            rotate(d_query, cos_table, -sin_table),
            rotate(d_kv[:, :HD].reshape(kv_width, tok_dev), cos_table, -sin_table),
            d_kv[:, HD:].reshape(kv_width, tok_dev),
        ],
        0,
    ).astype(jnp.bfloat16)
    d_normed = contract(d_qkv, w_qkv, 0, 1)
    back_one, g_gain_one = norm_backward(residual, inv_one, gain_attn, d_normed)
    input_grad = d_mid + back_one
    g_qkv = contract(normed_low, d_qkv, 0, 1).astype(jnp.bfloat16).reshape(dp_size, -1, 4 * width)
    g_gains = jnp.stack([g_gain_one, g_gain_two], 0).reshape(2, devices, own)
    g_gains = jnp.pad(jnp.moveaxis(g_gains, 0, 1), ((0, 0), (0, 6), (0, 128 - own)))
    squares = squares_of(g_gu_own) + squares_of(g_down_own) + squares_of(g_out_own)
    g_qkv_own, g_gains_own, total_sq = last_sums(g_qkv, g_gains, squares, 512, 5)
    g_gains_own = g_gains_own[:2, :own]
    grad_norm = jnp.sqrt(total_sq[0, 0])
    clip_factor = jnp.minimum(1.0, CLIP_NORM / (grad_norm + 1e-06))
    new_qkv, new_qkv_m, new_qkv_v = adam_update(
        qkv_weight, qkv_m, qkv_v, g_qkv_own, clip_factor, 0.06, WEIGHT_DECAY
    )
    new_out, new_out_m, new_out_v = adam_update(
        out_weight, out_m, out_v, g_out_own, clip_factor, 0.4, WEIGHT_DECAY
    )
    new_gu, new_gu_m, new_gu_v = adam_update(
        gate_up_weight, gate_up_m, gate_up_v, g_gu_own, clip_factor, 0.06, WEIGHT_DECAY
    )
    new_down, new_down_m, new_down_v = adam_update(
        down_weight, down_m, down_v, g_down_own, clip_factor, 0.06, WEIGHT_DECAY
    )
    new_gains, new_gain_m, new_gain_v = adam_update(
        norm_gains, gain_m, gain_v, g_gains_own, clip_factor, 0.6, 0.0
    )
    return (
        block_out,
        input_grad,
        grad_norm,
        new_qkv,
        new_qkv_m,
        new_qkv_v,
        new_out,
        new_out_m,
        new_out_v,
        new_gu,
        new_gu_m,
        new_gu_v,
        new_down,
        new_down_m,
        new_down_v,
        new_gains,
        new_gain_m,
        new_gain_v,
    )


def solution(mesh):
    in_specs = (
        P(("dp", "seq"), None),
        P(("dp", "seq"), None),
        P("dp", None),
        P("dp"),
        P("dp", None),
        P(("dp", "seq"), None),
        P(("dp", "seq"), None),
        P(("dp", "seq"), None),
        P(("dp", "seq"), None),
        P(("dp", "seq"), None),
        P(("dp", "seq"), None),
        P(("dp", "seq"), None),
        P(("dp", "seq"), None),
        P(("dp", "seq"), None),
        P(("dp", "seq"), None),
        P(("dp", "seq"), None),
        P(("dp", "seq"), None),
        P(None, ("dp", "seq")),
        P(None, ("dp", "seq")),
        P(None, ("dp", "seq")),
    )
    out_specs = (
        P(("dp", "seq"), None),
        P(("dp", "seq"), None),
        P(),
        P(("dp", "seq"), None),
        P(("dp", "seq"), None),
        P(("dp", "seq"), None),
        P(("dp", "seq"), None),
        P(("dp", "seq"), None),
        P(("dp", "seq"), None),
        P(("dp", "seq"), None),
        P(("dp", "seq"), None),
        P(("dp", "seq"), None),
        P(("dp", "seq"), None),
        P(("dp", "seq"), None),
        P(("dp", "seq"), None),
        P(None, ("dp", "seq")),
        P(None, ("dp", "seq")),
        P(None, ("dp", "seq")),
    )
    return jax.shard_map(
        per_device, mesh=mesh, in_specs=in_specs, out_specs=out_specs, check_vma=False
    )
```

```python
import functools
import math

import jax
import jax.numpy as jnp
from jax import lax
from jax.experimental import pallas as pl
from jax.experimental.pallas import tpu as pltpu
from jax.sharding import PartitionSpec as P

HEADS = 32
KV_HEADS = 4
HD = 64
FF = 5632
STEP = 10


NORM_EPS = 1e-05
ROPE_BASE = 10000.0
CLIP_NORM = 1.0
BETA_ONE = 0.9
BETA_TWO = 0.999
ADAM_EPS = 1e-08
WEIGHT_DECAY = 0.1
MASKED = -1e30


def matmul(left, right):
    return jnp.dot(left, right, preferred_element_type=jnp.float32)


def contract(left, right, left_dim, right_dim):
    return lax.dot_general(
        left, right, (((left_dim,), (right_dim,)), ((), ())), preferred_element_type=jnp.float32
    )


LOG2E = 1.4426950408889634
SCORE_SCALE = HD ** (-0.5)
SHARE = HEADS // KV_HEADS


def transposed(block):
    return block.astype(jnp.float32).T.astype(block.dtype)


def causal(tokens, valid):
    key_ids = lax.broadcasted_iota(jnp.int32, (tokens, tokens), 0)
    row_ids = lax.broadcasted_iota(jnp.int32, (tokens, tokens), 1)
    return (key_ids == row_ids) | ((key_ids < row_ids) & (valid > 0))


def attend_head(head, blocks, reach, valid, q_ref, kv_ref, group, k_rows, o_ref, full_ref, lse_ref):
    tokens = q_ref.shape[1]
    rows = pl.ds(pl.multiple_of(head * HD, HD), HD)
    query = q_ref[rows, :]

    def scores_of(dist):
        return matmul(k_rows[dist], query) * (SCORE_SCALE * LOG2E)

    def values_of(dist):
        return kv_ref[dist, group, HD:, :]

    scores = jnp.where(causal(tokens, valid), scores_of(0), MASKED)
    top = jnp.max(scores, 0, keepdims=True)
    weights = jnp.exp2(scores - top)
    total = jnp.sum(weights, 0, keepdims=True)
    acc = matmul(values_of(0), weights.astype(jnp.bfloat16))

    def step(dist, carry):
        top, total, acc = carry
        scores = jnp.where(dist < reach, scores_of(dist), MASKED)
        new_top = jnp.maximum(top, jnp.max(scores, 0, keepdims=True))
        weights = jnp.exp2(scores - new_top)
        fade = jnp.exp2(top - new_top)
        total = total * fade + jnp.sum(weights, 0, keepdims=True)
        acc = acc * fade + matmul(values_of(dist), weights.astype(jnp.bfloat16))
        return (new_top, total, acc)

    top, total, acc = lax.fori_loop(1, blocks, step, (top, total, acc))
    out = acc / total
    o_ref[rows, :] = out.astype(jnp.bfloat16)
    full_ref[rows, :] = out
    lse_ref[head] = top + jnp.log2(total)


def adam_update(weight, first_mom, second_mom, gradient, clip_factor, rate, decay):
    step_grad = gradient * clip_factor
    first_new = BETA_ONE * first_mom + (1.0 - BETA_ONE) * step_grad
    second_new = BETA_TWO * second_mom + (1.0 - BETA_TWO) * step_grad * step_grad
    mean_hat = first_new / (1.0 - BETA_ONE**STEP)
    square_hat = second_new / (1.0 - BETA_TWO**STEP)
    weight_new = weight - rate * (mean_hat / (jnp.sqrt(square_hat) + ADAM_EPS) + decay * weight)
    return (weight_new, first_new, second_new)


MESH = pl.DeviceIdType.MESH


def flipped(index, bit):
    return index + (1 << bit) * (1 - 2 * ((index // (1 << bit)) % 2))


WHOLE, ROWS, BLOCKS = range(3)


class Gather:
    ahead = 2

    def __init__(self, kinds, pieces, shards, fulls, local_sems, send_sems, recv_sems):
        self.kinds, self.pieces, self.shards, self.fulls = (kinds, pieces, shards, fulls)
        self.local_sems, self.send_sems, self.recv_sems = (local_sems, send_sems, recv_sems)
        self.dp, self.seq = (lax.axis_index("dp"), lax.axis_index("seq"))
        self.dp_size, self.seq_size = (lax.axis_size("dp"), lax.axis_size("seq"))
        self.bits = self.dp_size.bit_length() - 1
        up = list(range(1, self.bits))
        self.orders = (up + [0], up[::-1] + [0])
        self.started = []
        self.done, self.begun = (set(), set())
        self.hold = False

    def along(self, step):
        return {"seq": lax.rem(self.seq + step, self.seq_size)}

    def across(self, bit):
        return {"dp": flipped(self.dp, bit)}

    def sides(self, piece):
        return range(len(self.pieces[piece][2]))

    def kind(self, piece):
        return self.kinds[self.pieces[piece][0]]

    def source(self, piece, side):
        shard, _, sides = self.pieces[piece]
        return self.shards[shard].at[:, pl.ds(sides[side][0], sides[side][2])]

    def target(self, piece, side, index, depth):
        _, result, sides = self.pieces[piece]
        rows = pl.ds(pl.multiple_of(index * depth, depth), depth)
        return self.fulls[result].at[rows, pl.ds(sides[side][1], sides[side][2])]

    def own_target(self, piece, side):
        index = {
            WHOLE: self.dp * self.seq_size + self.seq, ROWS: self.seq, BLOCKS: self.dp
        }[self.kind(piece)]
        return self.target(piece, side, index, self.shards[self.pieces[piece][0]].shape[0])

    def local_copy(self, piece, side):
        return pltpu.make_async_copy(
            self.source(piece, side), self.own_target(piece, side), self.local_sems.at[piece, side]
        )

    def seq_copy(self, piece, side, step):
        return pltpu.make_async_remote_copy(
            src_ref=self.source(piece, side),
            dst_ref=self.own_target(piece, side),
            send_sem=self.send_sems.at[piece, side, self.dp_size + step],
            recv_sem=self.recv_sems.at[piece, side, self.dp_size + step],
            device_id=self.along(step),
            device_id_type=MESH,
        )

    def block_copy(self, piece, side, held, bit):
        depth = self.fulls[self.pieces[piece][1]].shape[0] // self.dp_size
        owner = self.dp
        for position in range(self.bits):
            if held >> position & 1:
                owner = flipped(owner, position)
        target = self.target(piece, side, owner, depth)
        early = not held and self.kind(piece) == BLOCKS
        return pltpu.make_async_remote_copy(
            src_ref=self.source(piece, side) if early else target,
            dst_ref=target,
            send_sem=self.send_sems.at[piece, side, held | 1 << bit],
            recv_sem=self.recv_sems.at[piece, side, held | 1 << bit],
            device_id=self.across(bit),
            device_id_type=MESH,
        )

    def start(self, copy):
        copy.start()
        self.started.append(copy)

    def begin(self):
        for piece in range(len(self.pieces)):
            for side in self.sides(piece):
                self.local_copy(piece, side).start()

    def send_rows(self, piece):
        if piece in self.begun or piece >= len(self.pieces):
            return
        self.begun.add(piece)
        if self.kind(piece) == BLOCKS:
            return
        for step in range(1, self.seq_size):
            for side in self.sides(piece):
                self.start(self.seq_copy(piece, side, step))

    def advance(self, piece, stage):
        if (piece, stage) in self.done:
            return
        self.done.add((piece, stage))
        self.send_rows(piece)
        kind = self.kind(piece)
        if stage and kind == ROWS:
            return
        for side in self.sides(piece):
            order = self.orders[side] if kind != ROWS else []
            if stage == 0:
                if kind == WHOLE:
                    self.local_copy(piece, side).wait()
                if kind != BLOCKS:
                    for step in range(1, self.seq_size):
                        self.seq_copy(piece, side, step).wait_recv()
                held = [0]
            else:
                reached = [0]
                for bit in order[: stage - 1]:
                    reached += [block | 1 << bit for block in reached]
                held = [block | 1 << order[stage - 1] for block in reached]
                for block in reached:
                    self.block_copy(piece, side, block, order[stage - 1]).wait_recv()
            for bit in order[stage:]:
                for block in held:
                    self.start(self.block_copy(piece, side, block, bit))
        if stage == 0 and not self.hold:
            self.send_rows(piece + self.ahead)

    def events(self, lag):
        for turn in range(len(self.pieces) + lag * self.bits):
            for stage in range(self.bits, -1, -1):
                if 0 <= turn - lag * stage < len(self.pieces):
                    yield (turn - lag * stage, stage)

    def finish(self, lag=1):
        for event in self.events(lag):
            self.advance(*event)
        for piece in range(len(self.pieces)):
            if self.kind(piece) != WHOLE:
                for side in self.sides(piece):
                    self.local_copy(piece, side).wait()
        for copy in self.started:
            copy.wait_send()


def gather_scratch(pieces):
    slots = lax.axis_size("dp") + lax.axis_size("seq")
    return [
        pltpu.SemaphoreType.DMA((pieces, 2)),
        pltpu.SemaphoreType.DMA((pieces, 2, slots)),
        pltpu.SemaphoreType.DMA((pieces, 2, slots)),
    ]


def gather_kernel(kinds, pieces, count, *refs):
    shards, refs = (refs[:count], refs[count:])
    rounded, fulls, sems = (refs[:count], refs[count:-3], refs[-3:])
    for shard, result in zip(shards, rounded):
        result[...] = shard[...].astype(jnp.bfloat16)
    gather = Gather(kinds, pieces, rounded, fulls, *sems)
    greet()
    gather.begin()
    for piece in range(gather.ahead):
        gather.send_rows(piece)
    gather.finish()


def gather_all(kinds, shards, shapes, pieces, collective_id):
    vmem = pl.BlockSpec(memory_space=pltpu.VMEM)
    hbm = pl.BlockSpec(memory_space=pl.ANY)
    count = len(shards)
    out = pl.pallas_call(
        functools.partial(gather_kernel, kinds, pieces, count),
        out_shape=[jax.ShapeDtypeStruct(shard.shape, jnp.bfloat16) for shard in shards]
        + [jax.ShapeDtypeStruct(shape, jnp.bfloat16) for shape in shapes],
        in_specs=[vmem] * count,
        out_specs=[vmem] * count + [hbm] * len(shapes),
        scratch_shapes=gather_scratch(len(pieces)),
        compiler_params=pltpu.CompilerParams(
            collective_id=collective_id, has_side_effects=True, vmem_limit_bytes=32 * 2**20
        ),
        name="gather",
    )(*shards)
    return (out[:count], out[count:])


def token_layout(tokens, lengths, counts, segments):
    seq = lax.axis_index("seq")
    segment = segments[0, seq * tokens]
    start = sum(
        jnp.where(slot < segment, lengths[0, slot], 0) for slot in range(lengths.shape[1])
    )
    valid = (segment < counts[0]).astype(jnp.int32)
    return (start, jnp.where(valid > 0, seq - start // tokens + 1, 1), valid)


def rotated(value, cos, sin):
    first, second = (value[: HD // 2], value[HD // 2 :])
    return jnp.concatenate([first * cos - second * sin, second * cos + first * sin], 0).astype(
        jnp.bfloat16
    )


def attend_kernel(kinds, pieces, lengths, counts, segments, x_ref, gains_ref, w_qkv, *refs):
    count = len(kinds)
    shards = refs[:count]
    q_ref, o_ref, full_ref, lse_ref, kv_all_ref, mid_ref, inner_ref, turned_ref = refs[count : count + 8]
    normed_ref, gain_one, gain_two, cos_ref, sin_ref = refs[count + 8 : count + 13]
    fulls = refs[count + 13 : -11]
    kv_ref, k_rows, slots, kv_send, kv_recv, o_rows, w_buf, w_sems = refs[-11:-3]
    gather = Gather(kinds, pieces, shards, fulls, *refs[-3:])
    seq, seq_size = (gather.seq, gather.seq_size)
    tokens, model = x_ref.shape
    start, reach, valid = token_layout(tokens, lengths, counts, segments)

    def qkv_load(tile, slot):
        return pltpu.make_async_copy(
            w_qkv.at[:, pl.ds(tile * TILE, TILE)], w_buf.at[slot], w_sems.at[slot]
        )

    def qkv_tile(slot):
        return matmul(o_rows[...], w_buf[slot]).T

    def kv_copy(group, step):
        return pltpu.make_async_remote_copy(
            src_ref=kv_ref.at[group],
            dst_ref=slots.at[step, group],
            send_sem=kv_send.at[step, group],
            recv_sem=kv_recv.at[step, group],
            device_id=gather.along(step),
            device_id_type=MESH,
        )

    def send_kv(groups):
        for group in groups:
            for step in range(1, seq_size):

                @pl.when(seq + step < seq_size)
                def _():
                    kv_copy(group, step).start()

    last = w_qkv.shape[1] // TILE - 1
    qkv_load(last, 0).start()
    qkv_load(0, 1).start()
    greet()
    gather.begin()
    gather.send_rows(1)
    gather.send_rows(2)
    gather.hold = True
    gather.advance(0, 0)
    half = lax.broadcasted_iota(jnp.int32, (HD // 2, tokens), 0).astype(jnp.float32)
    inverse = jnp.exp(half * (-2.0 / HD * math.log(ROPE_BASE)))
    place = seq * tokens - start + lax.broadcasted_iota(jnp.int32, (HD // 2, tokens), 1)
    angles = place.astype(jnp.float32) * inverse
    cos, sin = (jnp.cos(angles), jnp.sin(angles))
    cos_ref[...] = cos
    sin_ref[...] = sin
    devices = gather.dp_size * seq_size
    own = model // devices
    for row, gain in enumerate((gain_one, gain_two)):
        for chunk in range(model // 128):
            gain[:, chunk * 128 : (chunk + 1) * 128] = sum(
                pltpu.roll(
                    gains_ref[16 * device + row : 16 * device + row + 1, :].astype(jnp.float32),
                    device * own % 128,
                    1,
                )
                for device in range(chunk * 128 // own, (chunk + 1) * 128 // own)
            )

    @pl.loop(0, tokens // 64)
    def _(chunk):
        part = pl.ds(pl.multiple_of(chunk * 64, 64), 64)
        rows = x_ref[part, :].astype(jnp.float32)
        inverse = lax.rsqrt(jnp.mean(rows * rows, axis=-1, keepdims=True) + NORM_EPS)
        o_rows[part, :] = (rows * inverse * gain_one[...]).astype(jnp.bfloat16)

    qkv_load(last, 0).wait()
    value = qkv_tile(0)
    qkv_load(1, 0).start()
    for group in range(KV_HEADS):
        kv_ref[group, :HD, :] = rotated(value[group * HD : (group + 1) * HD], cos, sin)
        rest = (KV_HEADS + group) * HD
        kv_ref[group, HD:, :] = value[rest : rest + HD].astype(jnp.bfloat16)
    slots[0] = kv_ref[...]
    gather.advance(0, 1)
    for tile in range(last):
        slot = (tile + 1) % 2
        qkv_load(tile, slot).wait()
        value = qkv_tile(slot)
        if tile + 2 < last:
            qkv_load(tile + 2, slot).start()
        for head in range(TILE // HD):
            rows = slice(tile * TILE + head * HD, tile * TILE + (head + 1) * HD)
            q_ref[rows, :] = rotated(value[head * HD : (head + 1) * HD], cos, sin)
        part = slice(tile * TILE, (tile + 1) * TILE)
        normed_ref[part, :] = transposed(o_rows[:, part])
    gather.hold = False
    events = [event for event in gather.events(2) if event not in gather.done]

    def proceed(count):
        for _ in range(min(count, len(events))):
            gather.advance(*events.pop(0))

    for group in range(KV_HEADS):
        proceed(2)
        send_kv([group])
    proceed(2)
    for group in range(KV_HEADS):
        k_rows[0] = transposed(kv_ref[group, :HD, :])
        for step in range(1, seq_size):

            @pl.when(seq >= step)
            def _():
                kv_copy(group, step).wait_recv()
                k_rows[step] = transposed(slots[step, group, :HD, :])

        for part in range(4):

            @pl.loop(group * SHARE + part * SHARE // 4, group * SHARE + (part + 1) * SHARE // 4)
            def _(head):
                attend_head(
                    head, seq + 1, reach, valid, q_ref, slots, group, k_rows, o_ref, full_ref, lse_ref
                )

            proceed(1)
    for step in range(seq_size):

        @pl.when(seq >= step)
        def _():
            kv_all_ref[step] = slots[step]

        @pl.when(seq < step)
        def _():
            kv_all_ref[step] = jnp.zeros_like(kv_ref)

    for group in range(KV_HEADS):
        for step in range(1, seq_size):

            @pl.when(seq + step < seq_size)
            def _():
                kv_copy(group, step).wait_send()

    chunks = model // TILE

    def w_load(chunk):
        return pltpu.make_async_copy(
            fulls[0].at[:, pl.ds(chunk * TILE, TILE)], w_buf.at[chunk % 2], w_sems.at[chunk % 2]
        )

    while (1, gather.bits) not in gather.done:
        proceed(1)
    w_load(0).start()
    for row in range(model // TILE):
        part = slice(row * TILE, (row + 1) * TILE)
        o_rows[:, part] = transposed(o_ref[part, :])
    for chunk in range(chunks):
        w_load(chunk).wait()
        if chunk + 1 < chunks:
            w_load(chunk + 1).start()
        part = slice(chunk * TILE, (chunk + 1) * TILE)
        mid_ref[:, part] = x_ref[:, part].astype(jnp.float32) + matmul(o_rows[...], w_buf[chunk % 2])
        proceed(1)

    @pl.loop(0, tokens // 64)
    def _(chunk):
        part = pl.ds(pl.multiple_of(chunk * 64, 64), 64)
        rows = mid_ref[part, :]
        inverse = lax.rsqrt(jnp.mean(rows * rows, axis=-1, keepdims=True) + NORM_EPS)
        inner_ref[part, :] = (rows * inverse * gain_two[...]).astype(jnp.bfloat16)

    proceed(1)
    for row in range(model // TILE):
        part = slice(row * TILE, (row + 1) * TILE)
        turned_ref[part, :] = transposed(inner_ref[:, part])
    gather.finish(2)


def attend_forward(layout, rows, gains, w_qkv, kinds, shards, shapes, pieces, collective_id):
    tokens, model = rows.shape
    seq_size = lax.axis_size("seq")
    low, wide = (jnp.bfloat16, jnp.float32)
    vmem = pl.BlockSpec(memory_space=pltpu.VMEM)
    smem = pl.BlockSpec(memory_space=pltpu.SMEM)
    hbm = pl.BlockSpec(memory_space=pl.ANY)
    results = [
        ((HEADS * HD, tokens), low),
        ((HEADS * HD, tokens), low),
        ((HEADS * HD, tokens), wide),
        ((HEADS, 1, tokens), wide),
        ((seq_size, KV_HEADS, 2 * HD, tokens), low),
        ((tokens, model), wide),
        ((tokens, model), low),
        ((model, tokens), low),
        ((model, tokens), low),
        ((1, model), wide),
        ((1, model), wide),
        ((HD // 2, tokens), wide),
        ((HD // 2, tokens), wide),
    ]
    out = pl.pallas_call(
        functools.partial(attend_kernel, kinds, pieces),
        out_shape=[jax.ShapeDtypeStruct(*result) for result in results]
        + [jax.ShapeDtypeStruct(shape, low) for shape in shapes],
        in_specs=[smem] * 3 + [vmem] * 2 + [hbm] * (1 + len(shards)),
        out_specs=[vmem] * len(results) + [hbm] * len(shapes),
        scratch_shapes=[
            pltpu.VMEM((KV_HEADS, 2 * HD, tokens), low),
            pltpu.VMEM((seq_size, tokens, HD), low),
            pltpu.VMEM((seq_size, KV_HEADS, 2 * HD, tokens), low),
            pltpu.SemaphoreType.DMA((seq_size, KV_HEADS)),
            pltpu.SemaphoreType.DMA((seq_size, KV_HEADS)),
            pltpu.VMEM((tokens, model), low),
            pltpu.VMEM((2, model, TILE), low),
            pltpu.SemaphoreType.DMA((2,)),
            *gather_scratch(len(pieces)),
        ],
        compiler_params=pltpu.CompilerParams(
            collective_id=collective_id, has_side_effects=True, vmem_limit_bytes=58 * 2**20
        ),
        name="attend_forward",
    )(*layout, rows, gains, w_qkv, *shards)
    return (out[: len(results)], out[len(results) :])


def apart(index, distance, bits):
    return sum(
        lax.rem(index // (1 << bit) + distance // (1 << bit), 2) * (1 << bit) for bit in range(bits)
    )


class Scatter:
    def __init__(self, tiles, shape, refs, deliver):
        self.tiles, (self.size, self.depth, self.columns) = (tiles, shape)
        self.half = self.columns // 2
        self.deliver = deliver
        self.dp, self.seq = (lax.axis_index("dp"), lax.axis_index("seq"))
        self.dp_size, self.seq_size = (lax.axis_size("dp"), lax.axis_size("seq"))
        self.hops = self.size.bit_length() - 1
        refs = list(refs)
        self.own, self.other, self.came = (refs.pop(0), refs.pop(0), refs.pop(0))
        self.sent, self.got, self.kept = ([None], [None], [None])
        for _ in range(self.hops):
            self.sent.append(refs.pop(0))
            self.got.append(refs.pop(0))
            self.kept.append(refs.pop(0))
        self.rows, self.rows_got, self.send_sems, self.recv_sems = refs
        self.steps = tiles + self.hops + 2

    @staticmethod
    def scratch(shape):
        size, depth, columns = shape
        half = columns // 2
        hops = size.bit_length() - 1
        seq_size = lax.axis_size("seq")
        low = jnp.bfloat16
        shapes = [
            pltpu.VMEM((size, depth, columns), low),
            pltpu.VMEM((size, depth, columns), low),
            pltpu.VMEM((2, size, depth, columns), low),
        ]
        for hop in range(1, hops + 1):
            shapes.append(pltpu.VMEM((2, 2, size >> hop, depth, half), low))
            shapes.append(pltpu.VMEM((2, 2, size >> hop, depth, half), low))
            shapes.append(pltpu.VMEM((2, size >> hop, depth, half), low))
        shapes.append(pltpu.VMEM((2, 2, depth, half), low))
        shapes.append(pltpu.VMEM((2, seq_size - 1, 2, depth // seq_size, half), low))
        lanes = max(2, seq_size - 1)
        shapes.append(pltpu.SemaphoreType.DMA((hops + 2, 2, lanes)))
        shapes.append(pltpu.SemaphoreType.DMA((hops + 2, 2, lanes)))
        return shapes

    def bit(self, hop, side):
        return hop if side == 0 else self.hops + 1 - hop

    def copy(self, kind, slot, lane, src, dst, device):
        return pltpu.make_async_remote_copy(
            src_ref=src,
            dst_ref=dst,
            send_sem=self.send_sems.at[kind, slot, lane],
            recv_sem=self.recv_sems.at[kind, slot, lane],
            device_id=device,
            device_id_type=MESH,
        )

    def copies(self, kind, slot):
        if kind == 0:
            return [
                self.copy(0, slot, 0, self.other, self.came.at[slot], {"dp": flipped(self.dp, 0)})
            ]
        if kind <= self.hops:
            return [
                self.copy(
                    kind,
                    slot,
                    side,
                    self.sent[kind].at[slot, side],
                    self.got[kind].at[slot, side],
                    {"dp": flipped(self.dp, self.bit(kind, side))},
                )
                for side in range(2)
            ]
        own = self.depth // self.seq_size
        result = []
        for step in range(1, self.seq_size):
            there = lax.rem(self.seq + step, self.seq_size)
            window = pl.ds(pl.multiple_of(there * own, own), own)
            result.append(
                self.copy(
                    kind,
                    slot,
                    step - 1,
                    self.rows.at[slot, :, window, :],
                    self.rows_got.at[slot, step - 1],
                    {"seq": there},
                )
            )
        return result

    def send(self, kind, tile):
        for copy in self.copies(kind, lax.rem(tile, 2)):
            copy.start()

    def sent_before(self, kind, tile, back):
        @pl.when(tile >= back)
        def _():
            for copy in self.copies(kind, lax.rem(tile + 2 - back, 2)):
                copy.wait_send()

    def plus(self, into, one, two):
        rows = 64 if self.depth % 64 == 0 else 16

        @pl.loop(0, self.depth // rows)
        def _(chunk):
            part = pl.ds(pl.multiple_of(chunk * rows, rows), rows)
            into[part, :] = one[part, :] + two[part, :]

    def stage(self, kind, tile):
        slot = lax.rem(tile, 2)
        for copy in self.copies(kind, slot):
            copy.wait_recv()
        if kind == self.hops + 1:
            own = self.depth // self.seq_size
            window = pl.ds(pl.multiple_of(self.seq * own, own), own)
            for side in range(2):
                total = self.rows[slot, side, window, :].astype(jnp.float32)
                for step in range(self.seq_size - 1):
                    total = total + self.rows_got[slot, step, side].astype(jnp.float32)
                self.deliver(tile, side, total)
            return
        self.sent_before(kind + 1, tile, 2)
        size = self.size >> kind
        for side in range(2):
            columns = pl.ds(side * self.half, self.half)
            for block in range(size):
                if kind == 0:
                    one, two = (self.own.at[block, :, columns], self.came.at[slot, block, :, columns])
                else:
                    one, two = (self.kept[kind].at[side, block], self.got[kind].at[slot, side, block])
                if kind == self.hops:
                    into = self.rows.at[slot, side]
                elif side == 0:
                    place = self.sent if block % 2 else self.kept
                    index = (block // 2,)
                    into = place[kind + 1].at[((slot, 0) if block % 2 else (0,)) + index]
                else:
                    away = block >= size // 2
                    place = self.sent if away else self.kept
                    index = (block - size // 2 if away else block,)
                    into = place[kind + 1].at[((slot, 1) if away else (1,)) + index]
                self.plus(into, one, two)
        self.send(kind + 1, tile)

    def step(self, now, begin):
        for kind in range(self.hops + 1, -1, -1):
            tile = now - kind - 1

            @pl.when((tile >= 0) & (tile < self.tiles))
            def _():
                self.stage(kind, tile)

        @pl.when((now >= 0) & (now < self.tiles))
        def _():
            self.sent_before(0, now, 1)
            begin(now)

    def finish(self):
        for kind in range(self.hops + 2):
            for tile in range(max(0, self.tiles - (1 if kind == 0 else 2)), self.tiles):
                for copy in self.copies(kind, tile % 2):
                    copy.wait_send()


def greet():
    dp, seq = (lax.axis_index("dp"), lax.axis_index("seq"))
    dp_size, seq_size = (lax.axis_size("dp"), lax.axis_size("seq"))
    barrier = pltpu.get_barrier_semaphore()
    others = [{"seq": lax.rem(seq + step, seq_size)} for step in range(1, seq_size)]
    others += [{"dp": flipped(dp, bit)} for bit in range(dp_size.bit_length() - 1)]
    for other in others:
        pl.semaphore_signal(barrier, inc=1, device_id=other, device_id_type=MESH)
    pl.semaphore_wait(barrier, len(others))


TILE = 512


def squares_of(value):
    return sum(
        jnp.sum((part * part).reshape(-1, 8, 128), 0)
        for part in (value[:, c * 128 : (c + 1) * 128] for c in range(value.shape[1] // 128))
    )


def norm_backward_rows(rows_of, gradient, gain_ref, give):
    tokens, model = gradient.shape
    chunk_rows = 64

    def step(chunk, gain_sum):
        part = pl.ds(pl.multiple_of(chunk * chunk_rows, chunk_rows), chunk_rows)
        rows, grad = (rows_of(part), gradient[part, :])
        inverse = lax.rsqrt(jnp.mean(rows * rows, axis=-1, keepdims=True) + NORM_EPS)
        weighted = gain_ref[...] * grad
        scaled = rows * inverse
        mean = jnp.mean(weighted * rows, axis=-1, keepdims=True)
        give(part, inverse * weighted - scaled * (inverse * inverse * mean))
        return gain_sum + jnp.sum(grad * scaled, 0, keepdims=True)

    return lax.fori_loop(
        0, tokens // chunk_rows, step, jnp.zeros((1, model), jnp.float32)
    )


def mlp_kernel(
    rows_ref, turned_ref, gain_ref, grad_hbm, mid_hbm, gu_ref, down_ref, proj_ref,
    down_grad, d_mid_hbm, branch_hbm, block_out_hbm, d_out_hbm, gain_sum, sum_ref, squares,
    grad_ref, mid_ref, gu_buf, down_buf, hidden, d_gu, product, inner_ref, out_ref,
    load_sems, store_sems, out_sems, *scratch
):
    tokens, model = rows_ref.shape
    tiles = FF // TILE
    size, depth, columns = scratch[0].shape

    def deliver(tile, side, total):
        sum_ref[:, pl.ds(pl.multiple_of(side * FF + tile * TILE, TILE), TILE)] = total
        squares[...] += squares_of(total)

    scatter = Scatter(tiles, (size, depth, columns), scratch, deliver)
    bits = scatter.hops + 1

    def loads(tile, slot):
        start = pl.multiple_of(tile * TILE, TILE)
        return [
            pltpu.make_async_copy(
                gu_ref.at[:, pl.ds(start, TILE)], gu_buf.at[slot, 0], load_sems.at[slot, 0]
            ),
            pltpu.make_async_copy(
                gu_ref.at[:, pl.ds(pl.multiple_of(FF + start, TILE), TILE)],
                gu_buf.at[slot, 1],
                load_sems.at[slot, 1],
            ),
            pltpu.make_async_copy(
                down_ref.at[pl.ds(start, TILE), :], down_buf.at[slot], load_sems.at[slot, 2]
            ),
        ]

    def store(tile):
        start = pl.multiple_of(tile * TILE, TILE)
        return pltpu.make_async_copy(
            product, down_grad.at[pl.ds(start, TILE), :], store_sems.at[0]
        )

    grad_load = pltpu.make_async_copy(grad_hbm, grad_ref, store_sems.at[1])
    mid_load = pltpu.make_async_copy(mid_hbm, mid_ref, store_sems.at[2])
    d_mid_store = pltpu.make_async_copy(inner_ref, d_mid_hbm, store_sems.at[3])
    low_stores = []
    for place, result in enumerate((branch_hbm, block_out_hbm)):
        for chunk in range(model // TILE):
            low_stores.append(
                pltpu.make_async_copy(
                    gu_buf.at[0, place, pl.ds(chunk * tokens, tokens), :],
                    result.at[:, pl.ds(chunk * TILE, TILE)],
                    store_sems.at[4 + len(low_stores)],
                )
            )
    chunks = model // TILE

    def proj_load(chunk):
        rows = pl.ds(chunk * TILE, TILE)
        return pltpu.make_async_copy(
            proj_ref.at[rows, :], down_buf.at[chunk % 2], out_sems.at[0, chunk % 2]
        )

    def d_out_store(chunk):
        return pltpu.make_async_copy(
            product.at[:, pl.ds(chunk * tokens, tokens)],
            d_out_hbm.at[pl.ds(chunk * TILE, TILE), :],
            out_sems.at[1, chunk],
        )

    grad_load.start()
    mid_load.start()
    squares[...] = jnp.zeros_like(squares)
    for copy in loads(0, 0):
        copy.start()
    inner_ref[...] = jnp.zeros_like(inner_ref)
    out_ref[...] = jnp.zeros_like(out_ref)
    greet()
    grad_load.wait()

    def begin(tile):
        slot = lax.rem(tile, 2)
        for copy in loads(tile, slot):
            copy.wait()

        @pl.when(tile + 1 < tiles)
        def _():
            for copy in loads(tile + 1, 1 - slot):
                copy.start()

        chunk_rows = min(256, tokens)

        @pl.loop(0, tokens // chunk_rows)
        def _(chunk):
            part = pl.ds(pl.multiple_of(chunk * chunk_rows, chunk_rows), chunk_rows)
            rows = rows_ref[part, :]
            gate = matmul(rows, gu_buf[slot, 0])
            up = matmul(rows, gu_buf[slot, 1])
            d_hidden = contract(grad_ref[part, :], down_buf[slot], 1, 1)
            sigmoid_gate = 1.0 / (1.0 + jnp.exp(-gate))
            silu = gate * sigmoid_gate
            hidden[part, :] = (silu * up).astype(jnp.bfloat16)
            d_gate = d_hidden * up * sigmoid_gate * (1.0 + gate * (1.0 - sigmoid_gate))
            d_gu[part, :TILE] = d_gate.astype(jnp.bfloat16)
            d_gu[part, TILE:] = (d_hidden * silu).astype(jnp.bfloat16)

        def blocks_of(core, into):
            @pl.loop(0, size)
            def _(block):
                owner = apart(scatter.dp, 2 * block + core, bits)
                part = pl.ds(pl.multiple_of(owner * depth, depth), depth)
                into[block] = matmul(turned_ref[part, :], d_gu[...]).astype(jnp.bfloat16)

        blocks_of(1, scatter.other)
        scatter.send(0, tile)
        blocks_of(0, scatter.own)

        @pl.when(tile >= 1)
        def _():
            store(tile - 1).wait()

        hidden_turned = transposed(hidden[...])

        @pl.loop(0, model // TILE)
        def _(chunk):
            part = pl.ds(pl.multiple_of(chunk * TILE, TILE), TILE)
            inner_ref[:, part] += contract(d_gu[:, :TILE], gu_buf[slot, 0, part, :], 1, 1) + contract(
                d_gu[:, TILE:], gu_buf[slot, 1, part, :], 1, 1
            )
            out_ref[:, part] += matmul(hidden[...], down_buf[slot, :, part])
            product[:, part] = matmul(hidden_turned, grad_ref[:, part]).astype(jnp.bfloat16)

        store(tile).start()

    def give(part, back):
        start, count = (part.start, part.size)
        d_mid = grad_ref[part, :].astype(jnp.float32) + back
        inner_ref[part, :] = d_mid
        block_out = mid_ref[part, :] + out_ref[part, :]
        for chunk in range(model // TILE):
            columns = slice(chunk * TILE, (chunk + 1) * TILE)
            rows = pl.ds(pl.multiple_of(chunk * tokens + start, count), count)
            gu_buf[0, 0, rows, :] = d_mid[:, columns].astype(jnp.bfloat16)
            gu_buf[0, 1, rows, :] = block_out[:, columns].astype(jnp.bfloat16)

    @pl.loop(0, scatter.steps)
    def _(now):
        scatter.step(now, begin)

        @pl.when(now == tiles)
        def _():
            mid_load.wait()
            gain_sum[...] = norm_backward_rows(
                lambda part: mid_ref[part, :], inner_ref, gain_ref, give
            )
            d_mid_store.start()
            for copy in low_stores:
                copy.start()
            for chunk in range(2):
                proj_load(chunk).start()

        @pl.when(now == tiles + 1)
        def _():
            store(tiles - 1).wait()
            for chunk in range(chunks):
                proj_load(chunk).wait()
                product[:, chunk * tokens : (chunk + 1) * tokens] = sum(
                    contract(
                        down_buf[chunk % 2, :, part * TILE : (part + 1) * TILE],
                        gu_buf[0, 0, part * tokens : (part + 1) * tokens, :],
                        1,
                        1,
                    )
                    for part in range(chunks)
                ).astype(jnp.bfloat16)
                d_out_store(chunk).start()
                if chunk + 2 < chunks:
                    proj_load(chunk + 2).start()

    d_mid_store.wait()
    for copy in low_stores:
        copy.wait()
    for chunk in range(chunks):
        d_out_store(chunk).wait()
    scatter.finish()


def feed_forward(rows, turned, gain, grad, mid, w_gu, w_down, w_out, collective_id):
    tokens, model = rows.shape
    dp_size, seq_size = (lax.axis_size("dp"), lax.axis_size("seq"))
    shape = (dp_size // 2, model // dp_size, 2 * TILE)
    vmem = pl.BlockSpec(memory_space=pltpu.VMEM)
    hbm = pl.BlockSpec(memory_space=pl.ANY)
    return pl.pallas_call(
        mlp_kernel,
        out_shape=[
            jax.ShapeDtypeStruct((FF, model), jnp.bfloat16),
            jax.ShapeDtypeStruct((tokens, model), jnp.float32),
            jax.ShapeDtypeStruct((tokens, model), jnp.bfloat16),
            jax.ShapeDtypeStruct((tokens, model), jnp.bfloat16),
            jax.ShapeDtypeStruct((model, tokens), jnp.bfloat16),
            jax.ShapeDtypeStruct((1, model), jnp.float32),
            jax.ShapeDtypeStruct((model // (dp_size * seq_size), 2 * FF), jnp.float32),
            jax.ShapeDtypeStruct((8, 128), jnp.float32),
        ],
        in_specs=[vmem, vmem, vmem, hbm, hbm, hbm, hbm, hbm],
        out_specs=[hbm, hbm, hbm, hbm, hbm, vmem, vmem, vmem],
        scratch_shapes=[
            pltpu.VMEM((tokens, model), jnp.bfloat16),
            pltpu.VMEM((tokens, model), jnp.float32),
            pltpu.VMEM((2, 2, model, TILE), jnp.bfloat16),
            pltpu.VMEM((2, TILE, model), jnp.bfloat16),
            pltpu.VMEM((tokens, TILE), jnp.bfloat16),
            pltpu.VMEM((tokens, 2 * TILE), jnp.bfloat16),
            pltpu.VMEM((TILE, model), jnp.bfloat16),
            pltpu.VMEM((tokens, model), jnp.float32),
            pltpu.VMEM((tokens, model), jnp.float32),
            pltpu.SemaphoreType.DMA((2, 3)),
            pltpu.SemaphoreType.DMA((4 + 2 * model // TILE,)),
            pltpu.SemaphoreType.DMA((2, model // TILE)),
            *Scatter.scratch(shape),
        ],
        compiler_params=pltpu.CompilerParams(
            collective_id=collective_id, has_side_effects=True, vmem_limit_bytes=60 * 2**20
        ),
        name="feed_forward",
    )(rows, turned, gain, grad, mid, w_gu, w_down, w_out)


def load_tile(scatter, source, load_sems):
    def copies(tile):
        columns = pl.ds(
            pl.multiple_of(tile * scatter.columns, scatter.columns), scatter.columns
        )
        result = []
        for block in range(2 * scatter.size):
            owner = apart(scatter.dp, block, scatter.hops + 1)
            into = scatter.other if block % 2 else scatter.own
            result.append(
                pltpu.make_async_copy(
                    source.at[owner, :, columns], into.at[block // 2], load_sems.at[block]
                )
            )
        return result

    def begin(tile):
        for copy in copies(tile):
            copy.start()

    def complete(now):
        @pl.when((now >= 0) & (now < scatter.tiles))
        def _():
            for copy in copies(now):
                copy.wait()
            scatter.send(0, now)

    return (begin, complete)


def delivered(ref, columns, squares):
    def deliver(tile, side, total):
        start = pl.multiple_of(tile * columns + side * (columns // 2), columns // 2)
        ref[:, pl.ds(start, columns // 2)] = total
        squares[...] += squares_of(total)

    return deliver


def backward_kernel(
    lengths, counts, segments,
    q_ref, kv_ref, full_ref, lse_ref, do_ref, o_ref, branch_ref, cos_ref, sin_ref, squares_in, down_ref,
    d_qkv_ref, down_sum, proj_sum, squares,
    k_rows, v_rows, dk_acc, dv_acc, dkv_ref, turned, parts, parts_got, part_sends, part_recvs, load_sems, *scratch
):
    tokens = q_ref.shape[1]
    _, reach, valid = token_layout(tokens, lengths, counts, segments)
    count = len(scratch) // 2
    down = Scatter(
        down_ref.shape[2] // scratch[0].shape[2],
        scratch[0].shape,
        scratch[:count],
        delivered(down_sum, scratch[0].shape[2], squares),
    )
    proj = Scatter(
        branch_ref.shape[1] // scratch[count].shape[2],
        scratch[count].shape,
        scratch[count:],
        delivered(proj_sum, scratch[count].shape[2], squares),
    )
    seq, seq_size = (down.seq, down.seq_size)
    blocks = seq + 1
    squares[...] = squares_in[...]
    greet()

    def unrotated(value):
        first, second = (value[: HD // 2], value[HD // 2 :])
        cos, sin = (cos_ref[...], sin_ref[...])
        return jnp.concatenate(
            [first * cos + second * sin, second * cos - first * sin], 0
        ).astype(jnp.bfloat16)

    def part_copy(group, dist):
        return pltpu.make_async_remote_copy(
            src_ref=parts.at[dist, group],
            dst_ref=parts_got.at[dist, group],
            send_sem=part_sends.at[dist, group],
            recv_sem=part_recvs.at[dist, group],
            device_id={"seq": lax.rem(seq + seq_size - dist, seq_size)},
            device_id_type=MESH,
        )

    def one_head(head):
        group = head // SHARE
        rows = pl.ds(pl.multiple_of(head * HD, HD), HD)

        @pl.when(lax.rem(head, SHARE) == 0)
        def _():
            dk_acc[...] = jnp.zeros_like(dk_acc)
            dv_acc[...] = jnp.zeros_like(dv_acc)

            @pl.loop(0, blocks)
            def _(dist):
                k_rows[dist] = transposed(kv_ref[dist, group, :HD, :])
                v_rows[dist] = transposed(kv_ref[dist, group, HD:, :])

        query, grad = (q_ref[rows, :], do_ref[rows, :])
        query_rows, grad_rows = (transposed(query), transposed(grad))
        lse = lse_ref[head]
        centre = jnp.sum(grad.astype(jnp.float32) * full_ref[rows, :], 0, keepdims=True)

        def block(dist, mask):
            scores = matmul(k_rows[dist], query) * (SCORE_SCALE * LOG2E)
            prob = jnp.where(mask, jnp.exp2(scores - lse), 0.0)
            d_prob = matmul(v_rows[dist], grad)
            d_score = (prob * (d_prob - centre) * SCORE_SCALE).astype(jnp.bfloat16)
            dv_acc[dist] += matmul(prob.astype(jnp.bfloat16), grad_rows)
            dk_acc[dist] += matmul(d_score, query_rows)
            return matmul(kv_ref[dist, group, :HD, :], d_score)

        d_query = block(0, causal(tokens, valid))
        d_query = lax.fori_loop(
            1, blocks, lambda dist, acc: acc + block(dist, dist < reach), d_query
        )
        turned[rows, :] = unrotated(d_query)

        @pl.when(lax.rem(head, SHARE) == SHARE - 1)
        def _():
            dkv_ref[group, :HD, :] = dk_acc[0].T
            dkv_ref[group, HD:, :] = dv_acc[0].T
            for dist in range(1, seq_size):

                @pl.when(seq >= dist)
                def _():
                    parts[dist, group, :HD, :] = dk_acc[dist].T.astype(jnp.bfloat16)
                    parts[dist, group, HD:, :] = dv_acc[dist].T.astype(jnp.bfloat16)
                    part_copy(group, dist).start()

    def settle():
        for dist in range(1, seq_size):

            @pl.when(seq + dist < seq_size)
            def _():
                for group in range(KV_HEADS):
                    part_copy(group, dist).wait_recv()
                dkv_ref[...] += parts_got[dist].astype(jnp.float32)

            @pl.when(seq >= dist)
            def _():
                for group in range(KV_HEADS):
                    part_copy(group, dist).wait_send()

        for group in range(KV_HEADS):
            place = (HEADS + group) * HD
            turned[place : place + HD, :] = unrotated(dkv_ref[group, :HD, :])
            place += KV_HEADS * HD
            turned[place : place + HD, :] = dkv_ref[group, HD:, :].astype(jnp.bfloat16)
        for chunk in range(turned.shape[0] // TILE):
            part = slice(chunk * TILE, (chunk + 1) * TILE)
            d_qkv_ref[:, part] = transposed(turned[part, :])

    begin_down, complete_down = load_tile(down, down_ref, load_sems)

    def begin_proj(tile):
        columns = pl.ds(pl.multiple_of(tile * proj.columns, proj.columns), proj.columns)

        def blocks_of(core, into):
            @pl.loop(0, proj.size)
            def _(block):
                owner = apart(proj.dp, 2 * block + core, proj.hops + 1)
                part = pl.ds(pl.multiple_of(owner * proj.depth, proj.depth), proj.depth)
                into[block] = matmul(o_ref[part, :], branch_ref[:, columns]).astype(jnp.bfloat16)

        blocks_of(1, proj.other)
        proj.send(0, tile)
        blocks_of(0, proj.own)

    steps = down.steps
    lag = steps - proj.steps

    @pl.loop(0, steps)
    def _(now):
        down.step(now, begin_down)
        proj.step(now - lag, begin_proj)
        complete_down(now)

        busy = down.tiles

        @pl.loop(jnp.minimum(now, busy) * HEADS // busy, jnp.minimum(now + 1, busy) * HEADS // busy)
        def _(head):
            one_head(head)

        @pl.when(now == busy + 1)
        def _():
            settle()

    down.finish()
    proj.finish()


def attend_backward(
    layout, query, kv, full, lse, grad, attended, branch, cos, sin, squares, g_down, collective_id
):
    tokens, reach = (query.shape[1], kv.shape[0])
    model = branch.shape[1]
    dp_size, seq_size = (lax.axis_size("dp"), lax.axis_size("seq"))
    width = (HEADS + 2 * KV_HEADS) * HD
    vmem = pl.BlockSpec(memory_space=pltpu.VMEM)
    hbm = pl.BlockSpec(memory_space=pl.ANY)
    down_shape = (dp_size // 2, g_down.shape[1], 256)
    proj_shape = (dp_size // 2, HEADS * HD // dp_size, 256)
    return pl.pallas_call(
        backward_kernel,
        out_shape=[
            jax.ShapeDtypeStruct((tokens, width), jnp.bfloat16),
            jax.ShapeDtypeStruct((g_down.shape[1] // seq_size, model), jnp.float32),
            jax.ShapeDtypeStruct((HEADS * HD // (dp_size * seq_size), model), jnp.float32),
            jax.ShapeDtypeStruct((8, 128), jnp.float32),
        ],
        in_specs=[pl.BlockSpec(memory_space=pltpu.SMEM)] * 3 + [vmem] * 10 + [hbm],
        out_specs=[vmem] * 4,
        scratch_shapes=[
            pltpu.VMEM((reach, tokens, HD), jnp.bfloat16),
            pltpu.VMEM((reach, tokens, HD), jnp.bfloat16),
            pltpu.VMEM((reach, tokens, HD), jnp.float32),
            pltpu.VMEM((reach, tokens, HD), jnp.float32),
            pltpu.VMEM((KV_HEADS, 2 * HD, tokens), jnp.float32),
            pltpu.VMEM((width, tokens), jnp.bfloat16),
            pltpu.VMEM((reach, KV_HEADS, 2 * HD, tokens), jnp.bfloat16),
            pltpu.VMEM((reach, KV_HEADS, 2 * HD, tokens), jnp.bfloat16),
            pltpu.SemaphoreType.DMA((reach, KV_HEADS)),
            pltpu.SemaphoreType.DMA((reach, KV_HEADS)),
            pltpu.SemaphoreType.DMA((dp_size,)),
            *Scatter.scratch(down_shape),
            *Scatter.scratch(proj_shape),
        ],
        compiler_params=pltpu.CompilerParams(
            collective_id=collective_id, has_side_effects=True, vmem_limit_bytes=60 * 2**20
        ),
        name="attend_backward",
    )(*layout, query, kv, full, lse, grad, attended, branch, cos, sin, squares, g_down)


def everyone():
    seq_size = lax.axis_size("seq")
    devices = lax.axis_size("dp") * seq_size
    me = lax.axis_index("dp") * seq_size + lax.axis_index("seq")

    def device(distance):
        other = lax.rem(me + distance, devices)
        return (other, (other // seq_size, lax.rem(other, seq_size)))

    return (me, devices, device)


def last_kernel(
    rows_ref, turned_ref, d_qkv_ref, gain_ref, mlp_gain_ref, squares_ref, w_hbm, d_mid_hbm,
    result, gains_sum, total_ref, input_grad_hbm,
    w_buf, d_normed, d_mid, gains, gains_got, mine, totals_got,
    load_sems, tile_sends, tile_recvs, *scratch
):
    tokens, model = rows_ref.shape
    size, depth, columns = scratch[0].shape
    scatter = Scatter(
        d_qkv_ref.shape[1] // columns, scratch[0].shape, scratch, delivered(result, columns, mine)
    )
    bits = scatter.hops + 1
    me, devices, device = everyone()
    own = model // devices
    chunks = model // TILE

    def w_load(chunk, slot):
        rows = pl.ds(pl.multiple_of(chunk * TILE, TILE), TILE)
        return pltpu.make_async_copy(w_hbm.at[rows, :], w_buf.at[slot], load_sems.at[slot])

    mid_load = pltpu.make_async_copy(d_mid_hbm, d_mid, load_sems.at[2])
    input_store = pltpu.make_async_copy(d_mid, input_grad_hbm, load_sems.at[3])

    def copy(kind, distance):
        other, place = device(distance)
        return pltpu.make_async_remote_copy(
            src_ref=mine if kind else gains.at[other * own // 128],
            dst_ref=(totals_got if kind else gains_got).at[distance],
            send_sem=tile_sends.at[kind, distance],
            recv_sem=tile_recvs.at[kind, distance],
            device_id=place,
            device_id_type=MESH,
        )

    mid_load.start()
    w_load(0, 0).start()
    gains[...] = jnp.zeros_like(gains)
    mine[...] = squares_ref[...]
    barrier = pltpu.get_barrier_semaphore()

    @pl.loop(1, devices)
    def _(distance):
        pl.semaphore_signal(barrier, inc=1, device_id=device(distance)[1], device_id_type=MESH)

    pl.semaphore_wait(barrier, devices - 1)

    def begin(tile):
        part_columns = pl.ds(pl.multiple_of(tile * columns, columns), columns)

        def blocks_of(core, into):
            @pl.loop(0, size)
            def _(block):
                owner = apart(scatter.dp, 2 * block + core, bits)
                part = pl.ds(pl.multiple_of(owner * depth, depth), depth)
                into[block] = matmul(turned_ref[part, :], d_qkv_ref[:, part_columns]).astype(
                    jnp.bfloat16
                )

        blocks_of(1, scatter.other)
        scatter.send(0, tile)
        blocks_of(0, scatter.own)

    def give(part, back):
        d_mid[part, :] += back

    @pl.loop(0, scatter.steps)
    def _(now):
        scatter.step(now, begin)

        @pl.when(now < chunks)
        def _():
            slot = lax.rem(now, 2)
            w_load(now, slot).wait()

            @pl.when(now + 1 < chunks)
            def _():
                w_load(now + 1, 1 - slot).start()

            part = pl.ds(pl.multiple_of(now * TILE, TILE), TILE)
            d_normed[:, part] = contract(d_qkv_ref[...], w_buf[slot], 1, 1)

        @pl.when(now == chunks)
        def _():
            mid_load.wait()
            gain_sum = norm_backward_rows(
                lambda part: rows_ref[part, :].astype(jnp.float32), d_normed, gain_ref, give
            )
            input_store.start()
            for chunk in range(model // 128):
                part = slice(chunk * 128, (chunk + 1) * 128)
                gains[chunk, 0:1, :] = gain_sum[:, part]
                gains[chunk, 1:2, :] = mlp_gain_ref[:, part]

            @pl.loop(1, devices)
            def _(distance):
                copy(0, distance).start()

    @pl.loop(1, devices)
    def _(distance):
        copy(0, distance).wait()

    lane = lax.broadcasted_iota(jnp.int32, (8, 128), 1)
    first = lax.rem(me * own, 128)
    total_gains = gains[me * own // 128] + jnp.sum(gains_got[1:], 0)
    total_gains = jnp.where((lane >= first) & (lane < first + own), total_gains, 0.0)
    gains_sum[...] = total_gains
    mine[...] += total_gains * total_gains

    @pl.loop(1, devices)
    def _(distance):
        copy(1, distance).start()

    @pl.loop(1, devices)
    def _(distance):
        copy(1, distance).wait()

    total = jnp.sum(mine[...] + jnp.sum(totals_got[1:], 0))
    total_ref[...] = jnp.full((8, 128), total, jnp.float32)
    input_store.wait()
    scatter.finish()


def last_sums(
    rows, turned, d_qkv, gain, mlp_gain, squares, weight, d_mid, columns, collective_id
):
    tokens, model = rows.shape
    dp_size, seq_size = (lax.axis_size("dp"), lax.axis_size("seq"))
    devices = dp_size * seq_size
    shape = (dp_size // 2, model // dp_size, columns)
    vmem = pl.BlockSpec(memory_space=pltpu.VMEM)
    hbm = pl.BlockSpec(memory_space=pl.ANY)
    return pl.pallas_call(
        last_kernel,
        out_shape=[
            jax.ShapeDtypeStruct((model // devices, d_qkv.shape[1]), jnp.float32),
            jax.ShapeDtypeStruct((8, 128), jnp.float32),
            jax.ShapeDtypeStruct((8, 128), jnp.float32),
            jax.ShapeDtypeStruct((tokens, model), jnp.float32),
        ],
        in_specs=[vmem] * 6 + [hbm] * 2,
        out_specs=[vmem] * 3 + [hbm],
        scratch_shapes=[
            pltpu.VMEM((2, TILE, d_qkv.shape[1]), jnp.bfloat16),
            pltpu.VMEM((tokens, model), jnp.float32),
            pltpu.VMEM((tokens, model), jnp.float32),
            pltpu.VMEM((model // 128, 8, 128), jnp.float32),
            pltpu.VMEM((devices, 8, 128), jnp.float32),
            pltpu.VMEM((8, 128), jnp.float32),
            pltpu.VMEM((devices, 8, 128), jnp.float32),
            pltpu.SemaphoreType.DMA((4,)),
            pltpu.SemaphoreType.DMA((2, devices)),
            pltpu.SemaphoreType.DMA((2, devices)),
            *Scatter.scratch(shape),
        ],
        compiler_params=pltpu.CompilerParams(
            collective_id=collective_id, has_side_effects=True, vmem_limit_bytes=56 * 2**20
        ),
        name="last_sums",
    )(rows, turned, d_qkv, gain, mlp_gain, squares, weight, d_mid)


def per_device(
    hidden_in,
    out_grad,
    seq_lengths,
    seq_counts,
    segment_ids,
    qkv_weight,
    qkv_m,
    qkv_v,
    out_weight,
    out_m,
    out_v,
    gate_up_weight,
    gate_up_m,
    gate_up_v,
    down_weight,
    down_m,
    down_v,
    norm_gains,
    gain_m,
    gain_v,
):
    tok_dev = hidden_in.shape[0]
    layout = (seq_lengths, seq_counts, segment_ids)
    devices = lax.axis_size("dp") * lax.axis_size("seq")
    own = norm_gains.shape[1]
    gain_rows = jnp.pad(norm_gains, ((0, 14), (0, 128 - own)))
    model = out_weight.shape[1]
    seq_size = lax.axis_size("seq")
    down_depth = down_weight.shape[0]
    spare = -down_depth % 16
    down_shard = jnp.pad(down_weight, ((0, spare), (0, 0))) if spare else down_weight
    early = 3 * TILE
    shards, (w_qkv, gain_rows, gu_block) = gather_all(
        [WHOLE, WHOLE, ROWS],
        [qkv_weight, gain_rows, gate_up_weight, out_weight, down_shard],
        [
            (devices * qkv_weight.shape[0], qkv_weight.shape[1]),
            (devices * 16, 128),
            (seq_size * gate_up_weight.shape[0], 2 * early),
        ],
        [
            (1, 1, ((0, 0, 128),)),
            (0, 0, ((0, 0, 512), (512, 512, 384))),
            (0, 0, ((896, 896, 384), (1280, 1280, 512))),
            (0, 0, ((1792, 1792, 384), (2176, 2176, 384))),
            (2, 2, ((0, 0, early), (FF, early, early))),
        ],
        1,
    )
    shards = [shards[3], shards[4], shards[2], gu_block]
    shapes = [(devices * shard.shape[0], shard.shape[1]) for shard in shards[:3]]
    half, quarter = (model // 2, model // 4)
    pieces = [
        (3, 2, ((0, 0, early), (early, FF, early))),
        (0, 0, ((0, 0, half), (half, half, half))),
        (1, 1, ((0, 0, quarter), (quarter, quarter, quarter))),
        (1, 1, ((half, half, quarter), (half + quarter, half + quarter, quarter))),
    ]
    for low, high in ((3, 6), (6, 9), (9, 10), (10, 11)):
        low, high = (low * TILE, high * TILE)
        pieces.append((2, 2, ((low, low, high - low), (FF + low, FF + low, high - low))))
    forward, (w_out, w_down, w_gu) = attend_forward(
        layout, hidden_in, gain_rows, w_qkv, [WHOLE, WHOLE, WHOLE, BLOCKS], shards, shapes, pieces, 2
    )
    if spare:
        w_down = w_down.reshape(devices, -1, model)[:, :down_depth].reshape(-1, model)
    query, attended, attended_full, lse, kv_all, mid_rows, inner_rows, turned = forward[:8]
    normed, gain_one, gain_two, cos, sin = forward[8:]
    g_down, d_mid, d_branch, block_out, d_attended, g_gain_two, g_gu_own, squares = feed_forward(
        inner_rows, turned, gain_two, out_grad, mid_rows, w_gu, w_down, w_out, 3
    )
    dp_size = lax.axis_size("dp")
    if spare:
        g_down = jnp.pad(
            g_down.reshape(devices, down_depth, model), ((0, 0), (0, spare), (0, 0))
        )
    g_down = g_down.reshape(dp_size, -1, model)
    d_qkv, g_down_own, g_out_own, squares = attend_backward(
        layout, query, kv_all, attended_full, lse, d_attended,
        attended, d_branch, cos, sin, squares, g_down, 4,
    )
    g_down_own = g_down_own[:down_depth]
    g_qkv_own, g_gains_own, total_sq, input_grad = last_sums(
        hidden_in,
        normed,
        d_qkv,
        gain_one,
        g_gain_two,
        squares,
        w_qkv,
        d_mid,
        512,
        5,
    )
    place = (lax.axis_index("dp") * seq_size + lax.axis_index("seq")) * own % 128
    g_gains_own = lax.dynamic_slice(g_gains_own, (0, place), (2, own))
    grad_norm = jnp.sqrt(total_sq[0, 0])
    clip_factor = jnp.minimum(1.0, CLIP_NORM / (grad_norm + 1e-06))
    new_qkv, new_qkv_m, new_qkv_v = adam_update(
        qkv_weight, qkv_m, qkv_v, g_qkv_own, clip_factor, 0.06, WEIGHT_DECAY
    )
    new_out, new_out_m, new_out_v = adam_update(
        out_weight, out_m, out_v, g_out_own, clip_factor, 0.4, WEIGHT_DECAY
    )
    new_gu, new_gu_m, new_gu_v = adam_update(
        gate_up_weight, gate_up_m, gate_up_v, g_gu_own, clip_factor, 0.06, WEIGHT_DECAY
    )
    new_down, new_down_m, new_down_v = adam_update(
        down_weight, down_m, down_v, g_down_own, clip_factor, 0.06, WEIGHT_DECAY
    )
    new_gains, new_gain_m, new_gain_v = adam_update(
        norm_gains, gain_m, gain_v, g_gains_own, clip_factor, 0.6, 0.0
    )
    return (
        block_out,
        input_grad,
        grad_norm,
        new_qkv,
        new_qkv_m,
        new_qkv_v,
        new_out,
        new_out_m,
        new_out_v,
        new_gu,
        new_gu_m,
        new_gu_v,
        new_down,
        new_down_m,
        new_down_v,
        new_gains,
        new_gain_m,
        new_gain_v,
    )


def solution(mesh):
    in_specs = (
        P(("dp", "seq"), None),
        P(("dp", "seq"), None),
        P("dp", None),
        P("dp"),
        P("dp", None),
        P(("dp", "seq"), None),
        P(("dp", "seq"), None),
        P(("dp", "seq"), None),
        P(("dp", "seq"), None),
        P(("dp", "seq"), None),
        P(("dp", "seq"), None),
        P(("dp", "seq"), None),
        P(("dp", "seq"), None),
        P(("dp", "seq"), None),
        P(("dp", "seq"), None),
        P(("dp", "seq"), None),
        P(("dp", "seq"), None),
        P(None, ("dp", "seq")),
        P(None, ("dp", "seq")),
        P(None, ("dp", "seq")),
    )
    out_specs = (
        P(("dp", "seq"), None),
        P(("dp", "seq"), None),
        P(),
        P(("dp", "seq"), None),
        P(("dp", "seq"), None),
        P(("dp", "seq"), None),
        P(("dp", "seq"), None),
        P(("dp", "seq"), None),
        P(("dp", "seq"), None),
        P(("dp", "seq"), None),
        P(("dp", "seq"), None),
        P(("dp", "seq"), None),
        P(("dp", "seq"), None),
        P(("dp", "seq"), None),
        P(("dp", "seq"), None),
        P(None, ("dp", "seq")),
        P(None, ("dp", "seq")),
        P(None, ("dp", "seq")),
    )
    return jax.shard_map(
        per_device, mesh=mesh, in_specs=in_specs, out_specs=out_specs, check_vma=False
    )
```

```python
import functools
import math

import jax
import jax.numpy as jnp
from jax import lax
from jax.experimental import pallas as pl
from jax.experimental.pallas import tpu as pltpu
from jax.sharding import PartitionSpec as P

HEADS = 32
KV_HEADS = 4
HD = 64
FF = 5632
STEP = 10


NORM_EPS = 1e-05
ROPE_BASE = 10000.0
CLIP_NORM = 1.0
BETA_ONE = 0.9
BETA_TWO = 0.999
ADAM_EPS = 1e-08
WEIGHT_DECAY = 0.1
MASKED = -1e30


def matmul(left, right):
    return jnp.dot(left, right, preferred_element_type=jnp.float32)


def contract(left, right, left_dim, right_dim):
    return lax.dot_general(
        left, right, (((left_dim,), (right_dim,)), ((), ())), preferred_element_type=jnp.float32
    )


LOG2E = 1.4426950408889634
SCORE_SCALE = HD ** (-0.5)
SHARE = HEADS // KV_HEADS


def transposed(block):
    return block.astype(jnp.float32).T.astype(block.dtype)


def causal(tokens, valid):
    key_ids = lax.broadcasted_iota(jnp.int32, (tokens, tokens), 0)
    row_ids = lax.broadcasted_iota(jnp.int32, (tokens, tokens), 1)
    return (key_ids == row_ids) | ((key_ids < row_ids) & (valid > 0))


def attend_head(head, blocks, reach, valid, q_ref, kv_ref, group, k_rows, o_ref, full_ref, lse_ref):
    tokens = q_ref.shape[1]
    rows = pl.ds(pl.multiple_of(head * HD, HD), HD)
    query = q_ref[rows, :]

    def scores_of(dist):
        return matmul(k_rows[dist], query) * (SCORE_SCALE * LOG2E)

    def values_of(dist):
        return kv_ref[dist, group, HD:, :]

    scores = jnp.where(causal(tokens, valid), scores_of(0), MASKED)
    top = jnp.max(scores, 0, keepdims=True)
    weights = jnp.exp2(scores - top)
    total = jnp.sum(weights, 0, keepdims=True)
    acc = matmul(values_of(0), weights.astype(jnp.bfloat16))

    def step(dist, carry):
        top, total, acc = carry
        scores = jnp.where(dist < reach, scores_of(dist), MASKED)
        new_top = jnp.maximum(top, jnp.max(scores, 0, keepdims=True))
        weights = jnp.exp2(scores - new_top)
        fade = jnp.exp2(top - new_top)
        total = total * fade + jnp.sum(weights, 0, keepdims=True)
        acc = acc * fade + matmul(values_of(dist), weights.astype(jnp.bfloat16))
        return (new_top, total, acc)

    top, total, acc = lax.fori_loop(1, blocks, step, (top, total, acc))
    out = acc / total
    o_ref[rows, :] = out.astype(jnp.bfloat16)
    full_ref[rows, :] = out
    lse_ref[head] = top + jnp.log2(total)


def adam_update(weight, first_mom, second_mom, gradient, clip_factor, rate, decay):
    step_grad = gradient * clip_factor
    first_new = BETA_ONE * first_mom + (1.0 - BETA_ONE) * step_grad
    second_new = BETA_TWO * second_mom + (1.0 - BETA_TWO) * step_grad * step_grad
    mean_hat = first_new / (1.0 - BETA_ONE**STEP)
    square_hat = second_new / (1.0 - BETA_TWO**STEP)
    weight_new = weight - rate * (mean_hat / (jnp.sqrt(square_hat) + ADAM_EPS) + decay * weight)
    return (weight_new, first_new, second_new)


MESH = pl.DeviceIdType.MESH


def flipped(index, bit):
    return index + (1 << bit) * (1 - 2 * ((index // (1 << bit)) % 2))


WHOLE, ROWS, BLOCKS = range(3)


class Gather:
    ahead = 2

    def __init__(self, kinds, pieces, shards, fulls, local_sems, send_sems, recv_sems):
        self.kinds, self.pieces, self.shards, self.fulls = (kinds, pieces, shards, fulls)
        self.local_sems, self.send_sems, self.recv_sems = (local_sems, send_sems, recv_sems)
        self.dp, self.seq = (lax.axis_index("dp"), lax.axis_index("seq"))
        self.dp_size, self.seq_size = (lax.axis_size("dp"), lax.axis_size("seq"))
        self.bits = self.dp_size.bit_length() - 1
        up = list(range(1, self.bits))
        self.orders = (up + [0], up[::-1] + [0])
        self.started = []
        self.done, self.begun = (set(), set())
        self.hold = False

    def along(self, step):
        return {"seq": lax.rem(self.seq + step, self.seq_size)}

    def across(self, bit):
        return {"dp": flipped(self.dp, bit)}

    def sides(self, piece):
        return range(len(self.pieces[piece][2]))

    def kind(self, piece):
        return self.kinds[self.pieces[piece][0]]

    def source(self, piece, side):
        shard, _, sides = self.pieces[piece]
        return self.shards[shard].at[:, pl.ds(sides[side][0], sides[side][2])]

    def target(self, piece, side, index, depth):
        _, result, sides = self.pieces[piece]
        rows = pl.ds(pl.multiple_of(index * depth, depth), depth)
        return self.fulls[result].at[rows, pl.ds(sides[side][1], sides[side][2])]

    def own_target(self, piece, side):
        index = {
            WHOLE: self.dp * self.seq_size + self.seq, ROWS: self.seq, BLOCKS: self.dp
        }[self.kind(piece)]
        return self.target(piece, side, index, self.shards[self.pieces[piece][0]].shape[0])

    def local_copy(self, piece, side):
        return pltpu.make_async_copy(
            self.source(piece, side), self.own_target(piece, side), self.local_sems.at[piece, side]
        )

    def seq_copy(self, piece, side, step):
        return pltpu.make_async_remote_copy(
            src_ref=self.source(piece, side),
            dst_ref=self.own_target(piece, side),
            send_sem=self.send_sems.at[piece, side, self.dp_size + step],
            recv_sem=self.recv_sems.at[piece, side, self.dp_size + step],
            device_id=self.along(step),
            device_id_type=MESH,
        )

    def block_copy(self, piece, side, held, bit):
        depth = self.fulls[self.pieces[piece][1]].shape[0] // self.dp_size
        owner = self.dp
        for position in range(self.bits):
            if held >> position & 1:
                owner = flipped(owner, position)
        target = self.target(piece, side, owner, depth)
        early = not held and self.kind(piece) == BLOCKS
        return pltpu.make_async_remote_copy(
            src_ref=self.source(piece, side) if early else target,
            dst_ref=target,
            send_sem=self.send_sems.at[piece, side, held | 1 << bit],
            recv_sem=self.recv_sems.at[piece, side, held | 1 << bit],
            device_id=self.across(bit),
            device_id_type=MESH,
        )

    def start(self, copy):
        copy.start()
        self.started.append(copy)

    def begin(self):
        for piece in range(len(self.pieces)):
            for side in self.sides(piece):
                self.local_copy(piece, side).start()

    def send_rows(self, piece):
        if piece in self.begun or piece >= len(self.pieces):
            return
        self.begun.add(piece)
        if self.kind(piece) == BLOCKS:
            return
        for step in range(1, self.seq_size):
            for side in self.sides(piece):
                self.start(self.seq_copy(piece, side, step))

    def advance(self, piece, stage):
        if (piece, stage) in self.done:
            return
        self.done.add((piece, stage))
        self.send_rows(piece)
        kind = self.kind(piece)
        if stage and kind == ROWS:
            return
        for side in self.sides(piece):
            order = self.orders[side] if kind != ROWS else []
            if stage == 0:
                if kind == WHOLE:
                    self.local_copy(piece, side).wait()
                if kind != BLOCKS:
                    for step in range(1, self.seq_size):
                        self.seq_copy(piece, side, step).wait_recv()
                held = [0]
            else:
                reached = [0]
                for bit in order[: stage - 1]:
                    reached += [block | 1 << bit for block in reached]
                held = [block | 1 << order[stage - 1] for block in reached]
                for block in reached:
                    self.block_copy(piece, side, block, order[stage - 1]).wait_recv()
            for bit in order[stage:]:
                for block in held:
                    self.start(self.block_copy(piece, side, block, bit))
        if stage == 0 and not self.hold:
            self.send_rows(piece + self.ahead)

    def events(self, lag):
        for turn in range(len(self.pieces) + lag * self.bits):
            for stage in range(self.bits, -1, -1):
                if 0 <= turn - lag * stage < len(self.pieces):
                    yield (turn - lag * stage, stage)

    def finish(self, lag=1):
        for event in self.events(lag):
            self.advance(*event)
        for piece in range(len(self.pieces)):
            if self.kind(piece) != WHOLE:
                for side in self.sides(piece):
                    self.local_copy(piece, side).wait()
        for copy in self.started:
            copy.wait_send()


def gather_scratch(pieces):
    slots = lax.axis_size("dp") + lax.axis_size("seq")
    return [
        pltpu.SemaphoreType.DMA((pieces, 2)),
        pltpu.SemaphoreType.DMA((pieces, 2, slots)),
        pltpu.SemaphoreType.DMA((pieces, 2, slots)),
    ]


def gather_kernel(kinds, pieces, count, *refs):
    shards, refs = (refs[:count], refs[count:])
    rounded, fulls, sems = (refs[:count], refs[count:-3], refs[-3:])
    for shard, result in zip(shards, rounded):
        result[...] = shard[...].astype(jnp.bfloat16)
    gather = Gather(kinds, pieces, rounded, fulls, *sems)
    greet()
    gather.begin()
    for piece in range(gather.ahead):
        gather.send_rows(piece)
    gather.finish()


def gather_all(kinds, shards, shapes, pieces, collective_id):
    vmem = pl.BlockSpec(memory_space=pltpu.VMEM)
    hbm = pl.BlockSpec(memory_space=pl.ANY)
    count = len(shards)
    out = pl.pallas_call(
        functools.partial(gather_kernel, kinds, pieces, count),
        out_shape=[jax.ShapeDtypeStruct(shard.shape, jnp.bfloat16) for shard in shards]
        + [jax.ShapeDtypeStruct(shape, jnp.bfloat16) for shape in shapes],
        in_specs=[vmem] * count,
        out_specs=[vmem] * count + [hbm] * len(shapes),
        scratch_shapes=gather_scratch(len(pieces)),
        compiler_params=pltpu.CompilerParams(
            collective_id=collective_id, has_side_effects=True, vmem_limit_bytes=60 * 2**20
        ),
        name="gather",
    )(*shards)
    return (out[:count], out[count:])


def token_layout(tokens, lengths, counts, segments):
    seq = lax.axis_index("seq")
    segment = segments[0, seq * tokens]
    start = sum(
        jnp.where(slot < segment, lengths[0, slot], 0) for slot in range(lengths.shape[1])
    )
    valid = (segment < counts[0]).astype(jnp.int32)
    return (start, jnp.where(valid > 0, seq - start // tokens + 1, 1), valid)


def rotated(value, cos, sin):
    first, second = (value[: HD // 2], value[HD // 2 :])
    return jnp.concatenate([first * cos - second * sin, second * cos + first * sin], 0).astype(
        jnp.bfloat16
    )


def attend_kernel(kinds, pieces, lengths, counts, segments, x_ref, gains_ref, w_qkv, *refs):
    count = len(kinds)
    shards = refs[:count]
    q_ref, o_ref, full_ref, lse_ref, kv_all_ref, mid_ref, inner_ref, turned_ref = refs[count : count + 8]
    normed_ref, gain_one, gain_two, cos_ref, sin_ref = refs[count + 8 : count + 13]
    fulls = refs[count + 13 : -11]
    kv_ref, k_rows, slots, kv_send, kv_recv, o_rows, w_buf, w_sems = refs[-11:-3]
    gather = Gather(kinds, pieces, shards, fulls, *refs[-3:])
    seq, seq_size = (gather.seq, gather.seq_size)
    tokens, model = x_ref.shape
    start, reach, valid = token_layout(tokens, lengths, counts, segments)

    def qkv_load(tile, slot):
        return pltpu.make_async_copy(
            w_qkv.at[:, pl.ds(tile * TILE, TILE)], w_buf.at[slot], w_sems.at[slot]
        )

    def qkv_tile(slot):
        return matmul(o_rows[...], w_buf[slot]).T

    def kv_copy(group, step):
        return pltpu.make_async_remote_copy(
            src_ref=kv_ref.at[group],
            dst_ref=slots.at[step, group],
            send_sem=kv_send.at[step, group],
            recv_sem=kv_recv.at[step, group],
            device_id=gather.along(step),
            device_id_type=MESH,
        )

    def send_kv(groups):
        for group in groups:
            for step in range(1, seq_size):

                @pl.when(seq + step < seq_size)
                def _():
                    kv_copy(group, step).start()

    last = w_qkv.shape[1] // TILE - 1
    qkv_load(last, 0).start()
    qkv_load(0, 1).start()
    greet()
    gather.begin()
    gather.send_rows(1)
    gather.send_rows(2)
    gather.hold = True
    gather.advance(0, 0)
    half = lax.broadcasted_iota(jnp.int32, (HD // 2, tokens), 0).astype(jnp.float32)
    inverse = jnp.exp(half * (-2.0 / HD * math.log(ROPE_BASE)))
    place = seq * tokens - start + lax.broadcasted_iota(jnp.int32, (HD // 2, tokens), 1)
    angles = place.astype(jnp.float32) * inverse
    cos, sin = (jnp.cos(angles), jnp.sin(angles))
    cos_ref[...] = cos
    sin_ref[...] = sin
    devices = gather.dp_size * seq_size
    own = model // devices
    for row, gain in enumerate((gain_one, gain_two)):
        for chunk in range(model // 128):
            gain[:, chunk * 128 : (chunk + 1) * 128] = sum(
                pltpu.roll(
                    gains_ref[16 * device + row : 16 * device + row + 1, :].astype(jnp.float32),
                    device * own % 128,
                    1,
                )
                for device in range(chunk * 128 // own, (chunk + 1) * 128 // own)
            )

    @pl.loop(0, tokens // 64)
    def _(chunk):
        part = pl.ds(pl.multiple_of(chunk * 64, 64), 64)
        rows = x_ref[part, :].astype(jnp.float32)
        inverse = lax.rsqrt(jnp.mean(rows * rows, axis=-1, keepdims=True) + NORM_EPS)
        o_rows[part, :] = (rows * inverse * gain_one[...]).astype(jnp.bfloat16)

    qkv_load(last, 0).wait()
    value = qkv_tile(0)
    qkv_load(1, 0).start()
    for group in range(KV_HEADS):
        kv_ref[group, :HD, :] = rotated(value[group * HD : (group + 1) * HD], cos, sin)
        rest = (KV_HEADS + group) * HD
        kv_ref[group, HD:, :] = value[rest : rest + HD].astype(jnp.bfloat16)
    slots[0] = kv_ref[...]
    gather.advance(0, 1)
    for tile in range(last):
        slot = (tile + 1) % 2
        qkv_load(tile, slot).wait()
        value = qkv_tile(slot)
        if tile + 2 < last:
            qkv_load(tile + 2, slot).start()
        for head in range(TILE // HD):
            rows = slice(tile * TILE + head * HD, tile * TILE + (head + 1) * HD)
            q_ref[rows, :] = rotated(value[head * HD : (head + 1) * HD], cos, sin)
        part = slice(tile * TILE, (tile + 1) * TILE)
        normed_ref[part, :] = transposed(o_rows[:, part])
    gather.hold = False
    events = [event for event in gather.events(2) if event not in gather.done]

    def proceed(count):
        for _ in range(min(count, len(events))):
            gather.advance(*events.pop(0))

    for group in range(KV_HEADS):
        proceed(2)
        send_kv([group])
    proceed(2)
    for group in range(KV_HEADS):
        k_rows[0] = transposed(kv_ref[group, :HD, :])
        for step in range(1, seq_size):

            @pl.when(seq >= step)
            def _():
                kv_copy(group, step).wait_recv()
                k_rows[step] = transposed(slots[step, group, :HD, :])

        for part in range(4):

            @pl.loop(group * SHARE + part * SHARE // 4, group * SHARE + (part + 1) * SHARE // 4)
            def _(head):
                attend_head(
                    head, seq + 1, reach, valid, q_ref, slots, group, k_rows, o_ref, full_ref, lse_ref
                )

            proceed(1)
    for step in range(seq_size):

        @pl.when(seq >= step)
        def _():
            kv_all_ref[step] = slots[step]

        @pl.when(seq < step)
        def _():
            kv_all_ref[step] = jnp.zeros_like(kv_ref)

    for group in range(KV_HEADS):
        for step in range(1, seq_size):

            @pl.when(seq + step < seq_size)
            def _():
                kv_copy(group, step).wait_send()

    chunks = model // TILE

    def w_load(chunk):
        return pltpu.make_async_copy(
            fulls[0].at[:, pl.ds(chunk * TILE, TILE)], w_buf.at[chunk % 2], w_sems.at[chunk % 2]
        )

    while (1, gather.bits) not in gather.done:
        proceed(1)
    w_load(0).start()
    for row in range(model // TILE):
        part = slice(row * TILE, (row + 1) * TILE)
        o_rows[:, part] = transposed(o_ref[part, :])
    for chunk in range(chunks):
        w_load(chunk).wait()
        if chunk + 1 < chunks:
            w_load(chunk + 1).start()
        part = slice(chunk * TILE, (chunk + 1) * TILE)
        mid_ref[:, part] = x_ref[:, part].astype(jnp.float32) + matmul(o_rows[...], w_buf[chunk % 2])
        proceed(1)

    @pl.loop(0, tokens // 64)
    def _(chunk):
        part = pl.ds(pl.multiple_of(chunk * 64, 64), 64)
        rows = mid_ref[part, :]
        inverse = lax.rsqrt(jnp.mean(rows * rows, axis=-1, keepdims=True) + NORM_EPS)
        inner_ref[part, :] = (rows * inverse * gain_two[...]).astype(jnp.bfloat16)

    proceed(1)
    for row in range(model // TILE):
        part = slice(row * TILE, (row + 1) * TILE)
        turned_ref[part, :] = transposed(inner_ref[:, part])
    gather.finish(2)


def attend_forward(layout, rows, gains, w_qkv, kinds, shards, shapes, pieces, collective_id):
    tokens, model = rows.shape
    seq_size = lax.axis_size("seq")
    low, wide = (jnp.bfloat16, jnp.float32)
    vmem = pl.BlockSpec(memory_space=pltpu.VMEM)
    smem = pl.BlockSpec(memory_space=pltpu.SMEM)
    hbm = pl.BlockSpec(memory_space=pl.ANY)
    results = [
        ((HEADS * HD, tokens), low),
        ((HEADS * HD, tokens), low),
        ((HEADS * HD, tokens), wide),
        ((HEADS, 1, tokens), wide),
        ((seq_size, KV_HEADS, 2 * HD, tokens), low),
        ((tokens, model), wide),
        ((tokens, model), low),
        ((model, tokens), low),
        ((model, tokens), low),
        ((1, model), wide),
        ((1, model), wide),
        ((HD // 2, tokens), wide),
        ((HD // 2, tokens), wide),
    ]
    out = pl.pallas_call(
        functools.partial(attend_kernel, kinds, pieces),
        out_shape=[jax.ShapeDtypeStruct(*result) for result in results]
        + [jax.ShapeDtypeStruct(shape, low) for shape in shapes],
        in_specs=[smem] * 3 + [vmem] * 2 + [hbm] * (1 + len(shards)),
        out_specs=[vmem] * len(results) + [hbm] * len(shapes),
        scratch_shapes=[
            pltpu.VMEM((KV_HEADS, 2 * HD, tokens), low),
            pltpu.VMEM((seq_size, tokens, HD), low),
            pltpu.VMEM((seq_size, KV_HEADS, 2 * HD, tokens), low),
            pltpu.SemaphoreType.DMA((seq_size, KV_HEADS)),
            pltpu.SemaphoreType.DMA((seq_size, KV_HEADS)),
            pltpu.VMEM((tokens, model), low),
            pltpu.VMEM((2, model, TILE), low),
            pltpu.SemaphoreType.DMA((2,)),
            *gather_scratch(len(pieces)),
        ],
        compiler_params=pltpu.CompilerParams(
            collective_id=collective_id, has_side_effects=True, vmem_limit_bytes=58 * 2**20
        ),
        name="attend_forward",
    )(*layout, rows, gains, w_qkv, *shards)
    return (out[: len(results)], out[len(results) :])


def apart(index, distance, bits):
    return sum(
        lax.rem(index // (1 << bit) + distance // (1 << bit), 2) * (1 << bit) for bit in range(bits)
    )


class Scatter:
    def __init__(self, tiles, shape, refs, deliver):
        self.tiles, (self.size, self.depth, self.columns) = (tiles, shape)
        self.half = self.columns // 2
        self.deliver = deliver
        self.dp, self.seq = (lax.axis_index("dp"), lax.axis_index("seq"))
        self.dp_size, self.seq_size = (lax.axis_size("dp"), lax.axis_size("seq"))
        self.hops = self.size.bit_length() - 1
        refs = list(refs)
        self.own, self.other, self.came = (refs.pop(0), refs.pop(0), refs.pop(0))
        self.sent, self.got, self.kept = ([None], [None], [None])
        for _ in range(self.hops):
            self.sent.append(refs.pop(0))
            self.got.append(refs.pop(0))
            self.kept.append(refs.pop(0))
        self.rows, self.rows_got, self.send_sems, self.recv_sems = refs
        self.steps = tiles + self.hops + 2

    @staticmethod
    def scratch(shape):
        size, depth, columns = shape
        half = columns // 2
        hops = size.bit_length() - 1
        seq_size = lax.axis_size("seq")
        low = jnp.bfloat16
        shapes = [
            pltpu.VMEM((size, depth, columns), low),
            pltpu.VMEM((size, depth, columns), low),
            pltpu.VMEM((2, size, depth, columns), low),
        ]
        for hop in range(1, hops + 1):
            shapes.append(pltpu.VMEM((2, 2, size >> hop, depth, half), low))
            shapes.append(pltpu.VMEM((2, 2, size >> hop, depth, half), low))
            shapes.append(pltpu.VMEM((2, size >> hop, depth, half), low))
        shapes.append(pltpu.VMEM((2, 2, depth, half), low))
        shapes.append(pltpu.VMEM((2, seq_size - 1, 2, depth // seq_size, half), low))
        lanes = max(2, seq_size - 1)
        shapes.append(pltpu.SemaphoreType.DMA((hops + 2, 2, lanes)))
        shapes.append(pltpu.SemaphoreType.DMA((hops + 2, 2, lanes)))
        return shapes

    def bit(self, hop, side):
        return hop if side == 0 else self.hops + 1 - hop

    def copy(self, kind, slot, lane, src, dst, device):
        return pltpu.make_async_remote_copy(
            src_ref=src,
            dst_ref=dst,
            send_sem=self.send_sems.at[kind, slot, lane],
            recv_sem=self.recv_sems.at[kind, slot, lane],
            device_id=device,
            device_id_type=MESH,
        )

    def copies(self, kind, slot):
        if kind == 0:
            return [
                self.copy(0, slot, 0, self.other, self.came.at[slot], {"dp": flipped(self.dp, 0)})
            ]
        if kind <= self.hops:
            return [
                self.copy(
                    kind,
                    slot,
                    side,
                    self.sent[kind].at[slot, side],
                    self.got[kind].at[slot, side],
                    {"dp": flipped(self.dp, self.bit(kind, side))},
                )
                for side in range(2)
            ]
        own = self.depth // self.seq_size
        result = []
        for step in range(1, self.seq_size):
            there = lax.rem(self.seq + step, self.seq_size)
            window = pl.ds(pl.multiple_of(there * own, own), own)
            result.append(
                self.copy(
                    kind,
                    slot,
                    step - 1,
                    self.rows.at[slot, :, window, :],
                    self.rows_got.at[slot, step - 1],
                    {"seq": there},
                )
            )
        return result

    def send(self, kind, tile):
        for copy in self.copies(kind, lax.rem(tile, 2)):
            copy.start()

    def sent_before(self, kind, tile, back):
        @pl.when(tile >= back)
        def _():
            for copy in self.copies(kind, lax.rem(tile + 2 - back, 2)):
                copy.wait_send()

    def plus(self, into, one, two):
        rows = 64 if self.depth % 64 == 0 else 16

        @pl.loop(0, self.depth // rows)
        def _(chunk):
            part = pl.ds(pl.multiple_of(chunk * rows, rows), rows)
            into[part, :] = one[part, :] + two[part, :]

    def stage(self, kind, tile):
        slot = lax.rem(tile, 2)
        for copy in self.copies(kind, slot):
            copy.wait_recv()
        if kind == self.hops + 1:
            own = self.depth // self.seq_size
            window = pl.ds(pl.multiple_of(self.seq * own, own), own)
            for side in range(2):
                total = self.rows[slot, side, window, :].astype(jnp.float32)
                for step in range(self.seq_size - 1):
                    total = total + self.rows_got[slot, step, side].astype(jnp.float32)
                self.deliver(tile, side, total)
            return
        self.sent_before(kind + 1, tile, 2)
        size = self.size >> kind
        for side in range(2):
            columns = pl.ds(side * self.half, self.half)
            for block in range(size):
                if kind == 0:
                    one, two = (self.own.at[block, :, columns], self.came.at[slot, block, :, columns])
                else:
                    one, two = (self.kept[kind].at[side, block], self.got[kind].at[slot, side, block])
                if kind == self.hops:
                    into = self.rows.at[slot, side]
                elif side == 0:
                    place = self.sent if block % 2 else self.kept
                    index = (block // 2,)
                    into = place[kind + 1].at[((slot, 0) if block % 2 else (0,)) + index]
                else:
                    away = block >= size // 2
                    place = self.sent if away else self.kept
                    index = (block - size // 2 if away else block,)
                    into = place[kind + 1].at[((slot, 1) if away else (1,)) + index]
                self.plus(into, one, two)
        self.send(kind + 1, tile)

    def step(self, now, begin):
        for kind in range(self.hops + 1, -1, -1):
            tile = now - kind - 1

            @pl.when((tile >= 0) & (tile < self.tiles))
            def _():
                self.stage(kind, tile)

        @pl.when((now >= 0) & (now < self.tiles))
        def _():
            self.sent_before(0, now, 1)
            begin(now)

    def finish(self):
        for kind in range(self.hops + 2):
            for tile in range(max(0, self.tiles - (1 if kind == 0 else 2)), self.tiles):
                for copy in self.copies(kind, tile % 2):
                    copy.wait_send()


def greet():
    dp, seq = (lax.axis_index("dp"), lax.axis_index("seq"))
    dp_size, seq_size = (lax.axis_size("dp"), lax.axis_size("seq"))
    barrier = pltpu.get_barrier_semaphore()
    others = [{"seq": lax.rem(seq + step, seq_size)} for step in range(1, seq_size)]
    others += [{"dp": flipped(dp, bit)} for bit in range(dp_size.bit_length() - 1)]
    for other in others:
        pl.semaphore_signal(barrier, inc=1, device_id=other, device_id_type=MESH)
    pl.semaphore_wait(barrier, len(others))


TILE = 512


def squares_of(value):
    return sum(
        jnp.sum((part * part).reshape(-1, 8, 128), 0)
        for part in (value[:, c * 128 : (c + 1) * 128] for c in range(value.shape[1] // 128))
    )


def norm_backward_rows(rows_of, gradient, gain_ref, give):
    tokens, model = gradient.shape
    chunk_rows = 64

    def step(chunk, gain_sum):
        part = pl.ds(pl.multiple_of(chunk * chunk_rows, chunk_rows), chunk_rows)
        rows, grad = (rows_of(part), gradient[part, :])
        inverse = lax.rsqrt(jnp.mean(rows * rows, axis=-1, keepdims=True) + NORM_EPS)
        weighted = gain_ref[...] * grad
        scaled = rows * inverse
        mean = jnp.mean(weighted * rows, axis=-1, keepdims=True)
        give(part, inverse * weighted - scaled * (inverse * inverse * mean))
        return gain_sum + jnp.sum(grad * scaled, 0, keepdims=True)

    return lax.fori_loop(
        0, tokens // chunk_rows, step, jnp.zeros((1, model), jnp.float32)
    )


def mlp_kernel(
    rows_ref, turned_ref, gain_ref, grad_hbm, mid_hbm, gu_ref, down_ref, proj_ref,
    down_grad, d_mid_hbm, branch_hbm, block_out_hbm, d_out_hbm, gain_sum, sum_ref, squares,
    grad_ref, mid_ref, gu_buf, down_buf, hidden, d_gu, product, inner_ref, out_ref,
    load_sems, store_sems, out_sems, *scratch
):
    tokens, model = rows_ref.shape
    tiles = FF // TILE
    size, depth, columns = scratch[0].shape

    def deliver(tile, side, total):
        sum_ref[:, pl.ds(pl.multiple_of(side * FF + tile * TILE, TILE), TILE)] = total
        squares[...] += squares_of(total)

    scatter = Scatter(tiles, (size, depth, columns), scratch, deliver)
    bits = scatter.hops + 1

    def loads(tile, slot):
        start = pl.multiple_of(tile * TILE, TILE)
        return [
            pltpu.make_async_copy(
                gu_ref.at[:, pl.ds(start, TILE)], gu_buf.at[slot, 0], load_sems.at[slot, 0]
            ),
            pltpu.make_async_copy(
                gu_ref.at[:, pl.ds(pl.multiple_of(FF + start, TILE), TILE)],
                gu_buf.at[slot, 1],
                load_sems.at[slot, 1],
            ),
            pltpu.make_async_copy(
                down_ref.at[pl.ds(start, TILE), :], down_buf.at[slot], load_sems.at[slot, 2]
            ),
        ]

    def store(tile):
        start = pl.multiple_of(tile * TILE, TILE)
        return pltpu.make_async_copy(
            product, down_grad.at[pl.ds(start, TILE), :], store_sems.at[0]
        )

    grad_load = pltpu.make_async_copy(grad_hbm, grad_ref, store_sems.at[1])
    mid_load = pltpu.make_async_copy(mid_hbm, mid_ref, store_sems.at[2])
    d_mid_store = pltpu.make_async_copy(inner_ref, d_mid_hbm, store_sems.at[3])
    low_stores = []
    for place, result in enumerate((branch_hbm, block_out_hbm)):
        for chunk in range(model // TILE):
            low_stores.append(
                pltpu.make_async_copy(
                    gu_buf.at[0, place, pl.ds(chunk * tokens, tokens), :],
                    result.at[:, pl.ds(chunk * TILE, TILE)],
                    store_sems.at[4 + len(low_stores)],
                )
            )
    chunks = model // TILE

    def proj_load(chunk):
        rows = pl.ds(chunk * TILE, TILE)
        return pltpu.make_async_copy(
            proj_ref.at[rows, :], down_buf.at[chunk % 2], out_sems.at[0, chunk % 2]
        )

    def d_out_store(chunk):
        return pltpu.make_async_copy(
            product.at[:, pl.ds(chunk * tokens, tokens)],
            d_out_hbm.at[pl.ds(chunk * TILE, TILE), :],
            out_sems.at[1, chunk],
        )

    grad_load.start()
    mid_load.start()
    squares[...] = jnp.zeros_like(squares)
    for copy in loads(0, 0):
        copy.start()
    inner_ref[...] = jnp.zeros_like(inner_ref)
    out_ref[...] = jnp.zeros_like(out_ref)
    greet()
    grad_load.wait()

    def begin(tile):
        slot = lax.rem(tile, 2)
        for copy in loads(tile, slot):
            copy.wait()

        @pl.when(tile + 1 < tiles)
        def _():
            for copy in loads(tile + 1, 1 - slot):
                copy.start()

        chunk_rows = min(256, tokens)

        @pl.loop(0, tokens // chunk_rows)
        def _(chunk):
            part = pl.ds(pl.multiple_of(chunk * chunk_rows, chunk_rows), chunk_rows)
            rows = rows_ref[part, :]
            gate = matmul(rows, gu_buf[slot, 0])
            up = matmul(rows, gu_buf[slot, 1])
            d_hidden = contract(grad_ref[part, :], down_buf[slot], 1, 1)
            sigmoid_gate = 1.0 / (1.0 + jnp.exp(-gate))
            silu = gate * sigmoid_gate
            hidden[part, :] = (silu * up).astype(jnp.bfloat16)
            d_gate = d_hidden * up * sigmoid_gate * (1.0 + gate * (1.0 - sigmoid_gate))
            d_gu[part, :TILE] = d_gate.astype(jnp.bfloat16)
            d_gu[part, TILE:] = (d_hidden * silu).astype(jnp.bfloat16)

        def blocks_of(core, into):
            @pl.loop(0, size)
            def _(block):
                owner = apart(scatter.dp, 2 * block + core, bits)
                part = pl.ds(pl.multiple_of(owner * depth, depth), depth)
                into[block] = matmul(turned_ref[part, :], d_gu[...]).astype(jnp.bfloat16)

        blocks_of(1, scatter.other)
        scatter.send(0, tile)
        blocks_of(0, scatter.own)

        @pl.when(tile >= 1)
        def _():
            store(tile - 1).wait()

        hidden_turned = transposed(hidden[...])

        @pl.loop(0, model // TILE)
        def _(chunk):
            part = pl.ds(pl.multiple_of(chunk * TILE, TILE), TILE)
            inner_ref[:, part] += contract(d_gu[:, :TILE], gu_buf[slot, 0, part, :], 1, 1) + contract(
                d_gu[:, TILE:], gu_buf[slot, 1, part, :], 1, 1
            )
            out_ref[:, part] += matmul(hidden[...], down_buf[slot, :, part])
            product[:, part] = matmul(hidden_turned, grad_ref[:, part]).astype(jnp.bfloat16)

        store(tile).start()

    def give(part, back):
        start, count = (part.start, part.size)
        d_mid = grad_ref[part, :].astype(jnp.float32) + back
        inner_ref[part, :] = d_mid
        block_out = mid_ref[part, :] + out_ref[part, :]
        for chunk in range(model // TILE):
            columns = slice(chunk * TILE, (chunk + 1) * TILE)
            rows = pl.ds(pl.multiple_of(chunk * tokens + start, count), count)
            gu_buf[0, 0, rows, :] = d_mid[:, columns].astype(jnp.bfloat16)
            gu_buf[0, 1, rows, :] = block_out[:, columns].astype(jnp.bfloat16)

    @pl.loop(0, scatter.steps)
    def _(now):
        scatter.step(now, begin)

        @pl.when(now == tiles)
        def _():
            mid_load.wait()
            gain_sum[...] = norm_backward_rows(
                lambda part: mid_ref[part, :], inner_ref, gain_ref, give
            )
            d_mid_store.start()
            for copy in low_stores:
                copy.start()
            for chunk in range(2):
                proj_load(chunk).start()

        @pl.when(now == tiles + 1)
        def _():
            store(tiles - 1).wait()
            for chunk in range(chunks):
                proj_load(chunk).wait()
                product[:, chunk * tokens : (chunk + 1) * tokens] = sum(
                    contract(
                        down_buf[chunk % 2, :, part * TILE : (part + 1) * TILE],
                        gu_buf[0, 0, part * tokens : (part + 1) * tokens, :],
                        1,
                        1,
                    )
                    for part in range(chunks)
                ).astype(jnp.bfloat16)
                d_out_store(chunk).start()
                if chunk + 2 < chunks:
                    proj_load(chunk + 2).start()

    d_mid_store.wait()
    for copy in low_stores:
        copy.wait()
    for chunk in range(chunks):
        d_out_store(chunk).wait()
    scatter.finish()


def feed_forward(rows, turned, gain, grad, mid, w_gu, w_down, w_out, collective_id):
    tokens, model = rows.shape
    dp_size, seq_size = (lax.axis_size("dp"), lax.axis_size("seq"))
    shape = (dp_size // 2, model // dp_size, 2 * TILE)
    vmem = pl.BlockSpec(memory_space=pltpu.VMEM)
    hbm = pl.BlockSpec(memory_space=pl.ANY)
    return pl.pallas_call(
        mlp_kernel,
        out_shape=[
            jax.ShapeDtypeStruct((FF, model), jnp.bfloat16),
            jax.ShapeDtypeStruct((tokens, model), jnp.float32),
            jax.ShapeDtypeStruct((tokens, model), jnp.bfloat16),
            jax.ShapeDtypeStruct((tokens, model), jnp.bfloat16),
            jax.ShapeDtypeStruct((model, tokens), jnp.bfloat16),
            jax.ShapeDtypeStruct((1, model), jnp.float32),
            jax.ShapeDtypeStruct((model // (dp_size * seq_size), 2 * FF), jnp.float32),
            jax.ShapeDtypeStruct((8, 128), jnp.float32),
        ],
        in_specs=[vmem, vmem, vmem, hbm, hbm, hbm, hbm, hbm],
        out_specs=[hbm, hbm, hbm, hbm, hbm, vmem, vmem, vmem],
        scratch_shapes=[
            pltpu.VMEM((tokens, model), jnp.bfloat16),
            pltpu.VMEM((tokens, model), jnp.float32),
            pltpu.VMEM((2, 2, model, TILE), jnp.bfloat16),
            pltpu.VMEM((2, TILE, model), jnp.bfloat16),
            pltpu.VMEM((tokens, TILE), jnp.bfloat16),
            pltpu.VMEM((tokens, 2 * TILE), jnp.bfloat16),
            pltpu.VMEM((TILE, model), jnp.bfloat16),
            pltpu.VMEM((tokens, model), jnp.float32),
            pltpu.VMEM((tokens, model), jnp.float32),
            pltpu.SemaphoreType.DMA((2, 3)),
            pltpu.SemaphoreType.DMA((4 + 2 * model // TILE,)),
            pltpu.SemaphoreType.DMA((2, model // TILE)),
            *Scatter.scratch(shape),
        ],
        compiler_params=pltpu.CompilerParams(
            collective_id=collective_id, has_side_effects=True, vmem_limit_bytes=60 * 2**20
        ),
        name="feed_forward",
    )(rows, turned, gain, grad, mid, w_gu, w_down, w_out)


def load_tile(scatter, source, load_sems):
    def copies(tile):
        columns = pl.ds(
            pl.multiple_of(tile * scatter.columns, scatter.columns), scatter.columns
        )
        result = []
        for block in range(2 * scatter.size):
            owner = apart(scatter.dp, block, scatter.hops + 1)
            into = scatter.other if block % 2 else scatter.own
            result.append(
                pltpu.make_async_copy(
                    source.at[owner, :, columns], into.at[block // 2], load_sems.at[block]
                )
            )
        return result

    def begin(tile):
        for copy in copies(tile):
            copy.start()

    def complete(now):
        @pl.when((now >= 0) & (now < scatter.tiles))
        def _():
            for copy in copies(now):
                copy.wait()
            scatter.send(0, now)

    return (begin, complete)


def delivered(ref, columns, squares):
    def deliver(tile, side, total):
        start = pl.multiple_of(tile * columns + side * (columns // 2), columns // 2)
        ref[:, pl.ds(start, columns // 2)] = total
        squares[...] += squares_of(total)

    return deliver


def backward_kernel(
    lengths, counts, segments,
    q_ref, kv_ref, full_ref, lse_ref, do_ref, o_ref, branch_ref, cos_ref, sin_ref, squares_in, down_ref,
    d_qkv_ref, down_sum, proj_sum, squares,
    k_rows, v_rows, dk_acc, dv_acc, dkv_ref, turned, parts, parts_got, part_sends, part_recvs, load_sems, *scratch
):
    tokens = q_ref.shape[1]
    _, reach, valid = token_layout(tokens, lengths, counts, segments)
    count = len(scratch) // 2
    down = Scatter(
        down_ref.shape[2] // scratch[0].shape[2],
        scratch[0].shape,
        scratch[:count],
        delivered(down_sum, scratch[0].shape[2], squares),
    )
    proj = Scatter(
        branch_ref.shape[1] // scratch[count].shape[2],
        scratch[count].shape,
        scratch[count:],
        delivered(proj_sum, scratch[count].shape[2], squares),
    )
    seq, seq_size = (down.seq, down.seq_size)
    blocks = seq + 1
    squares[...] = squares_in[...]
    greet()

    def unrotated(value):
        first, second = (value[: HD // 2], value[HD // 2 :])
        cos, sin = (cos_ref[...], sin_ref[...])
        return jnp.concatenate(
            [first * cos + second * sin, second * cos - first * sin], 0
        ).astype(jnp.bfloat16)

    def part_copy(group, dist):
        return pltpu.make_async_remote_copy(
            src_ref=parts.at[dist, group],
            dst_ref=parts_got.at[dist, group],
            send_sem=part_sends.at[dist, group],
            recv_sem=part_recvs.at[dist, group],
            device_id={"seq": lax.rem(seq + seq_size - dist, seq_size)},
            device_id_type=MESH,
        )

    def one_head(head):
        group = head // SHARE
        rows = pl.ds(pl.multiple_of(head * HD, HD), HD)

        @pl.when(lax.rem(head, SHARE) == 0)
        def _():
            dk_acc[...] = jnp.zeros_like(dk_acc)
            dv_acc[...] = jnp.zeros_like(dv_acc)

            @pl.loop(0, blocks)
            def _(dist):
                k_rows[dist] = transposed(kv_ref[dist, group, :HD, :])
                v_rows[dist] = transposed(kv_ref[dist, group, HD:, :])

        query, grad = (q_ref[rows, :], do_ref[rows, :])
        query_rows, grad_rows = (transposed(query), transposed(grad))
        lse = lse_ref[head]
        centre = jnp.sum(grad.astype(jnp.float32) * full_ref[rows, :], 0, keepdims=True)

        def block(dist, mask):
            scores = matmul(k_rows[dist], query) * (SCORE_SCALE * LOG2E)
            prob = jnp.where(mask, jnp.exp2(scores - lse), 0.0)
            d_prob = matmul(v_rows[dist], grad)
            d_score = (prob * (d_prob - centre) * SCORE_SCALE).astype(jnp.bfloat16)
            dv_acc[dist] += matmul(prob.astype(jnp.bfloat16), grad_rows)
            dk_acc[dist] += matmul(d_score, query_rows)
            return matmul(kv_ref[dist, group, :HD, :], d_score)

        d_query = block(0, causal(tokens, valid))
        d_query = lax.fori_loop(
            1, blocks, lambda dist, acc: acc + block(dist, dist < reach), d_query
        )
        turned[rows, :] = unrotated(d_query)

        @pl.when(lax.rem(head, SHARE) == SHARE - 1)
        def _():
            dkv_ref[group, :HD, :] = dk_acc[0].T
            dkv_ref[group, HD:, :] = dv_acc[0].T
            for dist in range(1, seq_size):

                @pl.when(seq >= dist)
                def _():
                    parts[dist, group, :HD, :] = dk_acc[dist].T.astype(jnp.bfloat16)
                    parts[dist, group, HD:, :] = dv_acc[dist].T.astype(jnp.bfloat16)
                    part_copy(group, dist).start()

    def settle():
        for dist in range(1, seq_size):

            @pl.when(seq + dist < seq_size)
            def _():
                for group in range(KV_HEADS):
                    part_copy(group, dist).wait_recv()
                dkv_ref[...] += parts_got[dist].astype(jnp.float32)

            @pl.when(seq >= dist)
            def _():
                for group in range(KV_HEADS):
                    part_copy(group, dist).wait_send()

        for group in range(KV_HEADS):
            place = (HEADS + group) * HD
            turned[place : place + HD, :] = unrotated(dkv_ref[group, :HD, :])
            place += KV_HEADS * HD
            turned[place : place + HD, :] = dkv_ref[group, HD:, :].astype(jnp.bfloat16)
        for chunk in range(turned.shape[0] // TILE):
            part = slice(chunk * TILE, (chunk + 1) * TILE)
            d_qkv_ref[:, part] = transposed(turned[part, :])

    begin_down, complete_down = load_tile(down, down_ref, load_sems)

    def begin_proj(tile):
        columns = pl.ds(pl.multiple_of(tile * proj.columns, proj.columns), proj.columns)

        def blocks_of(core, into):
            @pl.loop(0, proj.size)
            def _(block):
                owner = apart(proj.dp, 2 * block + core, proj.hops + 1)
                part = pl.ds(pl.multiple_of(owner * proj.depth, proj.depth), proj.depth)
                into[block] = matmul(o_ref[part, :], branch_ref[:, columns]).astype(jnp.bfloat16)

        blocks_of(1, proj.other)
        proj.send(0, tile)
        blocks_of(0, proj.own)

    steps = down.steps
    lag = steps - proj.steps

    @pl.loop(0, steps)
    def _(now):
        down.step(now, begin_down)
        proj.step(now - lag, begin_proj)
        complete_down(now)

        busy, first = (down.tiles, 2)

        def heads_before(step):
            return jnp.minimum(jnp.maximum(step - first, 0), busy) * HEADS // busy

        @pl.loop(heads_before(now), heads_before(now + 1))
        def _(head):
            one_head(head)

        @pl.when(now == first + busy)
        def _():
            settle()

    down.finish()
    proj.finish()


def attend_backward(
    layout, query, kv, full, lse, grad, attended, branch, cos, sin, squares, g_down, collective_id
):
    tokens, reach = (query.shape[1], kv.shape[0])
    model = branch.shape[1]
    dp_size, seq_size = (lax.axis_size("dp"), lax.axis_size("seq"))
    width = (HEADS + 2 * KV_HEADS) * HD
    vmem = pl.BlockSpec(memory_space=pltpu.VMEM)
    hbm = pl.BlockSpec(memory_space=pl.ANY)
    down_shape = (dp_size // 2, g_down.shape[1], 256)
    proj_shape = (dp_size // 2, HEADS * HD // dp_size, 256)
    return pl.pallas_call(
        backward_kernel,
        out_shape=[
            jax.ShapeDtypeStruct((tokens, width), jnp.bfloat16),
            jax.ShapeDtypeStruct((g_down.shape[1] // seq_size, model), jnp.float32),
            jax.ShapeDtypeStruct((HEADS * HD // (dp_size * seq_size), model), jnp.float32),
            jax.ShapeDtypeStruct((8, 128), jnp.float32),
        ],
        in_specs=[pl.BlockSpec(memory_space=pltpu.SMEM)] * 3 + [vmem] * 10 + [hbm],
        out_specs=[vmem] * 4,
        scratch_shapes=[
            pltpu.VMEM((reach, tokens, HD), jnp.bfloat16),
            pltpu.VMEM((reach, tokens, HD), jnp.bfloat16),
            pltpu.VMEM((reach, tokens, HD), jnp.float32),
            pltpu.VMEM((reach, tokens, HD), jnp.float32),
            pltpu.VMEM((KV_HEADS, 2 * HD, tokens), jnp.float32),
            pltpu.VMEM((width, tokens), jnp.bfloat16),
            pltpu.VMEM((reach, KV_HEADS, 2 * HD, tokens), jnp.bfloat16),
            pltpu.VMEM((reach, KV_HEADS, 2 * HD, tokens), jnp.bfloat16),
            pltpu.SemaphoreType.DMA((reach, KV_HEADS)),
            pltpu.SemaphoreType.DMA((reach, KV_HEADS)),
            pltpu.SemaphoreType.DMA((dp_size,)),
            *Scatter.scratch(down_shape),
            *Scatter.scratch(proj_shape),
        ],
        compiler_params=pltpu.CompilerParams(
            collective_id=collective_id, has_side_effects=True, vmem_limit_bytes=60 * 2**20
        ),
        name="attend_backward",
    )(*layout, query, kv, full, lse, grad, attended, branch, cos, sin, squares, g_down)


def everyone():
    seq_size = lax.axis_size("seq")
    devices = lax.axis_size("dp") * seq_size
    me = lax.axis_index("dp") * seq_size + lax.axis_index("seq")

    def device(distance):
        other = lax.rem(me + distance, devices)
        return (other, (other // seq_size, lax.rem(other, seq_size)))

    return (me, devices, device)


def last_kernel(
    rows_ref, turned_ref, d_qkv_ref, gain_ref, mlp_gain_ref, squares_ref, w_hbm, d_mid_hbm,
    result, gains_sum, total_ref, input_grad_hbm,
    w_buf, d_normed, d_mid, gains, gains_got, mine, totals_got,
    load_sems, tile_sends, tile_recvs, *scratch
):
    tokens, model = rows_ref.shape
    size, depth, columns = scratch[0].shape
    scatter = Scatter(
        d_qkv_ref.shape[1] // columns, scratch[0].shape, scratch, delivered(result, columns, mine)
    )
    bits = scatter.hops + 1
    me, devices, device = everyone()
    own = model // devices
    chunks = model // TILE

    def w_load(chunk, slot):
        rows = pl.ds(pl.multiple_of(chunk * TILE, TILE), TILE)
        return pltpu.make_async_copy(w_hbm.at[rows, :], w_buf.at[slot], load_sems.at[slot])

    mid_load = pltpu.make_async_copy(d_mid_hbm, d_mid, load_sems.at[2])
    input_store = pltpu.make_async_copy(d_mid, input_grad_hbm, load_sems.at[3])

    def copy(kind, distance):
        other, place = device(distance)
        return pltpu.make_async_remote_copy(
            src_ref=mine if kind else gains.at[other * own // 128],
            dst_ref=(totals_got if kind else gains_got).at[distance],
            send_sem=tile_sends.at[kind, distance],
            recv_sem=tile_recvs.at[kind, distance],
            device_id=place,
            device_id_type=MESH,
        )

    mid_load.start()
    w_load(0, 0).start()
    gains[...] = jnp.zeros_like(gains)
    mine[...] = squares_ref[...]
    barrier = pltpu.get_barrier_semaphore()

    @pl.loop(1, devices)
    def _(distance):
        pl.semaphore_signal(barrier, inc=1, device_id=device(distance)[1], device_id_type=MESH)

    pl.semaphore_wait(barrier, devices - 1)

    def begin(tile):
        part_columns = pl.ds(pl.multiple_of(tile * columns, columns), columns)

        def blocks_of(core, into):
            @pl.loop(0, size)
            def _(block):
                owner = apart(scatter.dp, 2 * block + core, bits)
                part = pl.ds(pl.multiple_of(owner * depth, depth), depth)
                into[block] = matmul(turned_ref[part, :], d_qkv_ref[:, part_columns]).astype(
                    jnp.bfloat16
                )

        blocks_of(1, scatter.other)
        scatter.send(0, tile)
        blocks_of(0, scatter.own)

    def give(part, back):
        d_mid[part, :] += back

    @pl.loop(0, scatter.steps)
    def _(now):
        scatter.step(now, begin)

        @pl.when(now < chunks)
        def _():
            slot = lax.rem(now, 2)
            w_load(now, slot).wait()

            @pl.when(now + 1 < chunks)
            def _():
                w_load(now + 1, 1 - slot).start()

            part = pl.ds(pl.multiple_of(now * TILE, TILE), TILE)
            d_normed[:, part] = contract(d_qkv_ref[...], w_buf[slot], 1, 1)

        @pl.when(now == chunks)
        def _():
            mid_load.wait()
            gain_sum = norm_backward_rows(
                lambda part: rows_ref[part, :].astype(jnp.float32), d_normed, gain_ref, give
            )
            input_store.start()
            for chunk in range(model // 128):
                part = slice(chunk * 128, (chunk + 1) * 128)
                gains[chunk, 0:1, :] = gain_sum[:, part]
                gains[chunk, 1:2, :] = mlp_gain_ref[:, part]

            @pl.loop(1, devices)
            def _(distance):
                copy(0, distance).start()

    @pl.loop(1, devices)
    def _(distance):
        copy(0, distance).wait()

    lane = lax.broadcasted_iota(jnp.int32, (8, 128), 1)
    first = lax.rem(me * own, 128)
    total_gains = gains[me * own // 128] + jnp.sum(gains_got[1:], 0)
    total_gains = jnp.where((lane >= first) & (lane < first + own), total_gains, 0.0)
    gains_sum[...] = total_gains
    mine[...] += total_gains * total_gains

    @pl.loop(1, devices)
    def _(distance):
        copy(1, distance).start()

    @pl.loop(1, devices)
    def _(distance):
        copy(1, distance).wait()

    total = jnp.sum(mine[...] + jnp.sum(totals_got[1:], 0))
    total_ref[...] = jnp.full((8, 128), total, jnp.float32)
    input_store.wait()
    scatter.finish()


def last_sums(
    rows, turned, d_qkv, gain, mlp_gain, squares, weight, d_mid, columns, collective_id
):
    tokens, model = rows.shape
    dp_size, seq_size = (lax.axis_size("dp"), lax.axis_size("seq"))
    devices = dp_size * seq_size
    shape = (dp_size // 2, model // dp_size, columns)
    vmem = pl.BlockSpec(memory_space=pltpu.VMEM)
    hbm = pl.BlockSpec(memory_space=pl.ANY)
    return pl.pallas_call(
        last_kernel,
        out_shape=[
            jax.ShapeDtypeStruct((model // devices, d_qkv.shape[1]), jnp.float32),
            jax.ShapeDtypeStruct((8, 128), jnp.float32),
            jax.ShapeDtypeStruct((8, 128), jnp.float32),
            jax.ShapeDtypeStruct((tokens, model), jnp.float32),
        ],
        in_specs=[vmem] * 6 + [hbm] * 2,
        out_specs=[vmem] * 3 + [hbm],
        scratch_shapes=[
            pltpu.VMEM((2, TILE, d_qkv.shape[1]), jnp.bfloat16),
            pltpu.VMEM((tokens, model), jnp.float32),
            pltpu.VMEM((tokens, model), jnp.float32),
            pltpu.VMEM((model // 128, 8, 128), jnp.float32),
            pltpu.VMEM((devices, 8, 128), jnp.float32),
            pltpu.VMEM((8, 128), jnp.float32),
            pltpu.VMEM((devices, 8, 128), jnp.float32),
            pltpu.SemaphoreType.DMA((4,)),
            pltpu.SemaphoreType.DMA((2, devices)),
            pltpu.SemaphoreType.DMA((2, devices)),
            *Scatter.scratch(shape),
        ],
        compiler_params=pltpu.CompilerParams(
            collective_id=collective_id, has_side_effects=True, vmem_limit_bytes=56 * 2**20
        ),
        name="last_sums",
    )(rows, turned, d_qkv, gain, mlp_gain, squares, weight, d_mid)


def per_device(
    hidden_in,
    out_grad,
    seq_lengths,
    seq_counts,
    segment_ids,
    qkv_weight,
    qkv_m,
    qkv_v,
    out_weight,
    out_m,
    out_v,
    gate_up_weight,
    gate_up_m,
    gate_up_v,
    down_weight,
    down_m,
    down_v,
    norm_gains,
    gain_m,
    gain_v,
):
    tok_dev = hidden_in.shape[0]
    layout = (seq_lengths, seq_counts, segment_ids)
    devices = lax.axis_size("dp") * lax.axis_size("seq")
    own = norm_gains.shape[1]
    gain_rows = jnp.pad(norm_gains, ((0, 14), (0, 128 - own)))
    model = out_weight.shape[1]
    seq_size = lax.axis_size("seq")
    down_depth = down_weight.shape[0]
    spare = -down_depth % 16
    down_shard = jnp.pad(down_weight, ((0, spare), (0, 0))) if spare else down_weight
    early = 3 * TILE
    shards, (w_qkv, gain_rows, gu_block) = gather_all(
        [WHOLE, WHOLE, ROWS],
        [qkv_weight, gain_rows, gate_up_weight, out_weight, down_shard],
        [
            (devices * qkv_weight.shape[0], qkv_weight.shape[1]),
            (devices * 16, 128),
            (seq_size * gate_up_weight.shape[0], 2 * early),
        ],
        [
            (1, 1, ((0, 0, 128),)),
            (0, 0, ((0, 0, 512), (512, 512, 384))),
            (0, 0, ((896, 896, 384), (1280, 1280, 512))),
            (0, 0, ((1792, 1792, 384), (2176, 2176, 384))),
            (2, 2, ((0, 0, early), (FF, early, early))),
        ],
        1,
    )
    shards = [shards[3], shards[4], shards[2], gu_block]
    shapes = [(devices * shard.shape[0], shard.shape[1]) for shard in shards[:3]]
    half, quarter = (model // 2, model // 4)
    pieces = [
        (3, 2, ((0, 0, early), (early, FF, early))),
        (0, 0, ((0, 0, half), (half, half, half))),
        (1, 1, ((0, 0, quarter), (quarter, quarter, quarter))),
        (1, 1, ((half, half, quarter), (half + quarter, half + quarter, quarter))),
    ]
    for low, high in ((3, 6), (6, 9), (9, 10), (10, 11)):
        low, high = (low * TILE, high * TILE)
        pieces.append((2, 2, ((low, low, high - low), (FF + low, FF + low, high - low))))
    forward, (w_out, w_down, w_gu) = attend_forward(
        layout, hidden_in, gain_rows, w_qkv, [WHOLE, WHOLE, WHOLE, BLOCKS], shards, shapes, pieces, 2
    )
    if spare:
        w_down = w_down.reshape(devices, -1, model)[:, :down_depth].reshape(-1, model)
    query, attended, attended_full, lse, kv_all, mid_rows, inner_rows, turned = forward[:8]
    normed, gain_one, gain_two, cos, sin = forward[8:]
    g_down, d_mid, d_branch, block_out, d_attended, g_gain_two, g_gu_own, squares = feed_forward(
        inner_rows, turned, gain_two, out_grad, mid_rows, w_gu, w_down, w_out, 3
    )
    dp_size = lax.axis_size("dp")
    if spare:
        g_down = jnp.pad(
            g_down.reshape(devices, down_depth, model), ((0, 0), (0, spare), (0, 0))
        )
    g_down = g_down.reshape(dp_size, -1, model)
    d_qkv, g_down_own, g_out_own, squares = attend_backward(
        layout, query, kv_all, attended_full, lse, d_attended,
        attended, d_branch, cos, sin, squares, g_down, 4,
    )
    g_down_own = g_down_own[:down_depth]
    g_qkv_own, g_gains_own, total_sq, input_grad = last_sums(
        hidden_in,
        normed,
        d_qkv,
        gain_one,
        g_gain_two,
        squares,
        w_qkv,
        d_mid,
        512,
        5,
    )
    place = (lax.axis_index("dp") * seq_size + lax.axis_index("seq")) * own % 128
    g_gains_own = lax.dynamic_slice(g_gains_own, (0, place), (2, own))
    grad_norm = jnp.sqrt(total_sq[0, 0])
    clip_factor = jnp.minimum(1.0, CLIP_NORM / (grad_norm + 1e-06))
    new_qkv, new_qkv_m, new_qkv_v = adam_update(
        qkv_weight, qkv_m, qkv_v, g_qkv_own, clip_factor, 0.06, WEIGHT_DECAY
    )
    new_out, new_out_m, new_out_v = adam_update(
        out_weight, out_m, out_v, g_out_own, clip_factor, 0.4, WEIGHT_DECAY
    )
    new_gu, new_gu_m, new_gu_v = adam_update(
        gate_up_weight, gate_up_m, gate_up_v, g_gu_own, clip_factor, 0.06, WEIGHT_DECAY
    )
    new_down, new_down_m, new_down_v = adam_update(
        down_weight, down_m, down_v, g_down_own, clip_factor, 0.06, WEIGHT_DECAY
    )
    new_gains, new_gain_m, new_gain_v = adam_update(
        norm_gains, gain_m, gain_v, g_gains_own, clip_factor, 0.6, 0.0
    )
    return (
        block_out,
        input_grad,
        grad_norm,
        new_qkv,
        new_qkv_m,
        new_qkv_v,
        new_out,
        new_out_m,
        new_out_v,
        new_gu,
        new_gu_m,
        new_gu_v,
        new_down,
        new_down_m,
        new_down_v,
        new_gains,
        new_gain_m,
        new_gain_v,
    )


def solution(mesh):
    in_specs = (
        P(("dp", "seq"), None),
        P(("dp", "seq"), None),
        P("dp", None),
        P("dp"),
        P("dp", None),
        P(("dp", "seq"), None),
        P(("dp", "seq"), None),
        P(("dp", "seq"), None),
        P(("dp", "seq"), None),
        P(("dp", "seq"), None),
        P(("dp", "seq"), None),
        P(("dp", "seq"), None),
        P(("dp", "seq"), None),
        P(("dp", "seq"), None),
        P(("dp", "seq"), None),
        P(("dp", "seq"), None),
        P(("dp", "seq"), None),
        P(None, ("dp", "seq")),
        P(None, ("dp", "seq")),
        P(None, ("dp", "seq")),
    )
    out_specs = (
        P(("dp", "seq"), None),
        P(("dp", "seq"), None),
        P(),
        P(("dp", "seq"), None),
        P(("dp", "seq"), None),
        P(("dp", "seq"), None),
        P(("dp", "seq"), None),
        P(("dp", "seq"), None),
        P(("dp", "seq"), None),
        P(("dp", "seq"), None),
        P(("dp", "seq"), None),
        P(("dp", "seq"), None),
        P(("dp", "seq"), None),
        P(("dp", "seq"), None),
        P(("dp", "seq"), None),
        P(None, ("dp", "seq")),
        P(None, ("dp", "seq")),
        P(None, ("dp", "seq")),
    )
    return jax.shard_map(
        per_device, mesh=mesh, in_specs=in_specs, out_specs=out_specs, check_vma=False
    )
```

```python
import functools
import math

import jax
import jax.numpy as jnp
from jax import lax
from jax.experimental import pallas as pl
from jax.experimental.pallas import tpu as pltpu
from jax.sharding import PartitionSpec as P

HEADS = 32
KV_HEADS = 4
HD = 64
FF = 5632
STEP = 10


NORM_EPS = 1e-05
ROPE_BASE = 10000.0
CLIP_NORM = 1.0
BETA_ONE = 0.9
BETA_TWO = 0.999
ADAM_EPS = 1e-08
WEIGHT_DECAY = 0.1
MASKED = -1e30


def matmul(left, right):
    return jnp.dot(left, right, preferred_element_type=jnp.float32)


def contract(left, right, left_dim, right_dim):
    return lax.dot_general(
        left, right, (((left_dim,), (right_dim,)), ((), ())), preferred_element_type=jnp.float32
    )


LOG2E = 1.4426950408889634
SCORE_SCALE = HD ** (-0.5)
SHARE = HEADS // KV_HEADS


def transposed(block):
    return block.astype(jnp.float32).T.astype(block.dtype)


def causal(tokens, valid):
    key_ids = lax.broadcasted_iota(jnp.int32, (tokens, tokens), 0)
    row_ids = lax.broadcasted_iota(jnp.int32, (tokens, tokens), 1)
    return (key_ids == row_ids) | ((key_ids < row_ids) & (valid > 0))


def attend_head(head, blocks, reach, valid, q_ref, kv_ref, group, k_rows, o_ref, full_ref, lse_ref):
    tokens = q_ref.shape[1]
    rows = pl.ds(pl.multiple_of(head * HD, HD), HD)
    query = q_ref[rows, :]

    def scores_of(dist):
        return matmul(k_rows[dist], query) * (SCORE_SCALE * LOG2E)

    def values_of(dist):
        return kv_ref[dist, group, HD:, :]

    scores = jnp.where(causal(tokens, valid), scores_of(0), MASKED)
    top = jnp.max(scores, 0, keepdims=True)
    weights = jnp.exp2(scores - top)
    total = jnp.sum(weights, 0, keepdims=True)
    acc = matmul(values_of(0), weights.astype(jnp.bfloat16))

    def step(dist, carry):
        top, total, acc = carry
        scores = jnp.where(dist < reach, scores_of(dist), MASKED)
        new_top = jnp.maximum(top, jnp.max(scores, 0, keepdims=True))
        weights = jnp.exp2(scores - new_top)
        fade = jnp.exp2(top - new_top)
        total = total * fade + jnp.sum(weights, 0, keepdims=True)
        acc = acc * fade + matmul(values_of(dist), weights.astype(jnp.bfloat16))
        return (new_top, total, acc)

    top, total, acc = lax.fori_loop(1, blocks, step, (top, total, acc))
    out = acc / total
    o_ref[rows, :] = out.astype(jnp.bfloat16)
    full_ref[rows, :] = out
    lse_ref[head] = top + jnp.log2(total)


def adam_update(weight, first_mom, second_mom, gradient, clip_factor, rate, decay):
    step_grad = gradient * clip_factor
    first_new = BETA_ONE * first_mom + (1.0 - BETA_ONE) * step_grad
    second_new = BETA_TWO * second_mom + (1.0 - BETA_TWO) * step_grad * step_grad
    mean_hat = first_new / (1.0 - BETA_ONE**STEP)
    square_hat = second_new / (1.0 - BETA_TWO**STEP)
    weight_new = weight - rate * (mean_hat / (jnp.sqrt(square_hat) + ADAM_EPS) + decay * weight)
    return (weight_new, first_new, second_new)


MESH = pl.DeviceIdType.MESH


def flipped(index, bit):
    return index + (1 << bit) * (1 - 2 * ((index // (1 << bit)) % 2))


WHOLE, ROWS, BLOCKS = range(3)


class Gather:
    ahead = 2

    def __init__(self, kinds, pieces, shards, fulls, local_sems, send_sems, recv_sems):
        self.kinds, self.pieces, self.shards, self.fulls = (kinds, pieces, shards, fulls)
        self.local_sems, self.send_sems, self.recv_sems = (local_sems, send_sems, recv_sems)
        self.dp, self.seq = (lax.axis_index("dp"), lax.axis_index("seq"))
        self.dp_size, self.seq_size = (lax.axis_size("dp"), lax.axis_size("seq"))
        self.bits = self.dp_size.bit_length() - 1
        up = list(range(1, self.bits))
        self.orders = (up + [0], up[::-1] + [0])
        self.started = []
        self.done, self.begun = (set(), set())
        self.hold = False

    def along(self, step):
        return {"seq": lax.rem(self.seq + step, self.seq_size)}

    def across(self, bit):
        return {"dp": flipped(self.dp, bit)}

    def sides(self, piece):
        return range(len(self.pieces[piece][2]))

    def kind(self, piece):
        return self.kinds[self.pieces[piece][0]]

    def source(self, piece, side):
        shard, _, sides = self.pieces[piece]
        return self.shards[shard].at[:, pl.ds(sides[side][0], sides[side][2])]

    def target(self, piece, side, index, depth):
        _, result, sides = self.pieces[piece]
        rows = pl.ds(pl.multiple_of(index * depth, depth), depth)
        return self.fulls[result].at[rows, pl.ds(sides[side][1], sides[side][2])]

    def own_target(self, piece, side):
        index = {
            WHOLE: self.dp * self.seq_size + self.seq, ROWS: self.seq, BLOCKS: self.dp
        }[self.kind(piece)]
        return self.target(piece, side, index, self.shards[self.pieces[piece][0]].shape[0])

    def local_copy(self, piece, side):
        return pltpu.make_async_copy(
            self.source(piece, side), self.own_target(piece, side), self.local_sems.at[piece, side]
        )

    def seq_copy(self, piece, side, step):
        return pltpu.make_async_remote_copy(
            src_ref=self.source(piece, side),
            dst_ref=self.own_target(piece, side),
            send_sem=self.send_sems.at[piece, side, self.dp_size + step],
            recv_sem=self.recv_sems.at[piece, side, self.dp_size + step],
            device_id=self.along(step),
            device_id_type=MESH,
        )

    def block_copy(self, piece, side, held, bit):
        depth = self.fulls[self.pieces[piece][1]].shape[0] // self.dp_size
        owner = self.dp
        for position in range(self.bits):
            if held >> position & 1:
                owner = flipped(owner, position)
        target = self.target(piece, side, owner, depth)
        early = not held and self.kind(piece) == BLOCKS
        return pltpu.make_async_remote_copy(
            src_ref=self.source(piece, side) if early else target,
            dst_ref=target,
            send_sem=self.send_sems.at[piece, side, held | 1 << bit],
            recv_sem=self.recv_sems.at[piece, side, held | 1 << bit],
            device_id=self.across(bit),
            device_id_type=MESH,
        )

    def start(self, copy):
        copy.start()
        self.started.append(copy)

    def begin(self):
        for piece in range(len(self.pieces)):
            for side in self.sides(piece):
                self.local_copy(piece, side).start()

    def send_rows(self, piece):
        if piece in self.begun or piece >= len(self.pieces):
            return
        self.begun.add(piece)
        if self.kind(piece) == BLOCKS:
            return
        for step in range(1, self.seq_size):
            for side in self.sides(piece):
                self.start(self.seq_copy(piece, side, step))

    def advance(self, piece, stage):
        if (piece, stage) in self.done:
            return
        self.done.add((piece, stage))
        self.send_rows(piece)
        kind = self.kind(piece)
        if stage and kind == ROWS:
            return
        for side in self.sides(piece):
            order = self.orders[side] if kind != ROWS else []
            if stage == 0:
                if kind == WHOLE:
                    self.local_copy(piece, side).wait()
                if kind != BLOCKS:
                    for step in range(1, self.seq_size):
                        self.seq_copy(piece, side, step).wait_recv()
                held = [0]
            else:
                reached = [0]
                for bit in order[: stage - 1]:
                    reached += [block | 1 << bit for block in reached]
                held = [block | 1 << order[stage - 1] for block in reached]
                for block in reached:
                    self.block_copy(piece, side, block, order[stage - 1]).wait_recv()
            for bit in order[stage:]:
                for block in held:
                    self.start(self.block_copy(piece, side, block, bit))
        if stage == 0 and not self.hold:
            self.send_rows(piece + self.ahead)

    def events(self, lag):
        for turn in range(len(self.pieces) + lag * self.bits):
            for stage in range(self.bits, -1, -1):
                if 0 <= turn - lag * stage < len(self.pieces):
                    yield (turn - lag * stage, stage)

    def finish(self, lag=1):
        for event in self.events(lag):
            self.advance(*event)
        for piece in range(len(self.pieces)):
            if self.kind(piece) != WHOLE:
                for side in self.sides(piece):
                    self.local_copy(piece, side).wait()
        for copy in self.started:
            copy.wait_send()


def gather_scratch(pieces):
    slots = lax.axis_size("dp") + lax.axis_size("seq")
    return [
        pltpu.SemaphoreType.DMA((pieces, 2)),
        pltpu.SemaphoreType.DMA((pieces, 2, slots)),
        pltpu.SemaphoreType.DMA((pieces, 2, slots)),
    ]


def gather_kernel(kinds, pieces, count, *refs):
    shards, refs = (refs[:count], refs[count:])
    rounded, fulls, sems = (refs[:count], refs[count:-3], refs[-3:])
    for shard, result in zip(shards, rounded):
        result[...] = shard[...].astype(jnp.bfloat16)
    gather = Gather(kinds, pieces, rounded, fulls, *sems)
    greet()
    gather.begin()
    for piece in range(gather.ahead):
        gather.send_rows(piece)
    gather.finish()


def gather_all(kinds, shards, shapes, pieces, collective_id):
    vmem = pl.BlockSpec(memory_space=pltpu.VMEM)
    hbm = pl.BlockSpec(memory_space=pl.ANY)
    count = len(shards)
    out = pl.pallas_call(
        functools.partial(gather_kernel, kinds, pieces, count),
        out_shape=[jax.ShapeDtypeStruct(shard.shape, jnp.bfloat16) for shard in shards]
        + [jax.ShapeDtypeStruct(shape, jnp.bfloat16) for shape in shapes],
        in_specs=[vmem] * count,
        out_specs=[vmem] * count + [hbm] * len(shapes),
        scratch_shapes=gather_scratch(len(pieces)),
        compiler_params=pltpu.CompilerParams(
            collective_id=collective_id, has_side_effects=True, vmem_limit_bytes=60 * 2**20
        ),
        name="gather",
    )(*shards)
    return (out[:count], out[count:])


def token_layout(tokens, lengths, counts, segments):
    seq = lax.axis_index("seq")
    segment = segments[0, seq * tokens]
    start = sum(
        jnp.where(slot < segment, lengths[0, slot], 0) for slot in range(lengths.shape[1])
    )
    valid = (segment < counts[0]).astype(jnp.int32)
    return (start, jnp.where(valid > 0, seq - start // tokens + 1, 1), valid)


def rotated(value, cos, sin):
    first, second = (value[: HD // 2], value[HD // 2 :])
    return jnp.concatenate([first * cos - second * sin, second * cos + first * sin], 0).astype(
        jnp.bfloat16
    )


def attend_kernel(kinds, pieces, lengths, counts, segments, x_ref, gains_ref, w_qkv, *refs):
    count = len(kinds)
    shards = refs[:count]
    q_ref, o_ref, full_ref, lse_ref, kv_all_ref, mid_ref, inner_ref, turned_ref = refs[count : count + 8]
    normed_ref, gain_one, gain_two, cos_ref, sin_ref = refs[count + 8 : count + 13]
    fulls = refs[count + 13 : -11]
    kv_ref, k_rows, slots, kv_send, kv_recv, o_rows, w_buf, w_sems = refs[-11:-3]
    gather = Gather(kinds, pieces, shards, fulls, *refs[-3:])
    seq, seq_size = (gather.seq, gather.seq_size)
    tokens, model = x_ref.shape
    start, reach, valid = token_layout(tokens, lengths, counts, segments)

    def qkv_load(tile, slot):
        return pltpu.make_async_copy(
            w_qkv.at[:, pl.ds(tile * TILE, TILE)], w_buf.at[slot], w_sems.at[slot]
        )

    def qkv_tile(slot):
        return matmul(o_rows[...], w_buf[slot]).T

    def kv_copy(group, step):
        return pltpu.make_async_remote_copy(
            src_ref=kv_ref.at[group],
            dst_ref=slots.at[step, group],
            send_sem=kv_send.at[step, group],
            recv_sem=kv_recv.at[step, group],
            device_id=gather.along(step),
            device_id_type=MESH,
        )

    def send_kv(groups):
        for group in groups:
            for step in range(1, seq_size):

                @pl.when(seq + step < seq_size)
                def _():
                    kv_copy(group, step).start()

    last = w_qkv.shape[1] // TILE - 1
    qkv_load(last, 0).start()
    qkv_load(0, 1).start()
    greet()
    gather.begin()
    gather.send_rows(1)
    gather.send_rows(2)
    gather.hold = True
    gather.advance(0, 0)
    half = lax.broadcasted_iota(jnp.int32, (HD // 2, tokens), 0).astype(jnp.float32)
    inverse = jnp.exp(half * (-2.0 / HD * math.log(ROPE_BASE)))
    place = seq * tokens - start + lax.broadcasted_iota(jnp.int32, (HD // 2, tokens), 1)
    angles = place.astype(jnp.float32) * inverse
    cos, sin = (jnp.cos(angles), jnp.sin(angles))
    cos_ref[...] = cos
    sin_ref[...] = sin
    devices = gather.dp_size * seq_size
    own = model // devices
    for row, gain in enumerate((gain_one, gain_two)):
        for chunk in range(model // 128):
            gain[:, chunk * 128 : (chunk + 1) * 128] = sum(
                pltpu.roll(
                    gains_ref[16 * device + row : 16 * device + row + 1, :].astype(jnp.float32),
                    device * own % 128,
                    1,
                )
                for device in range(chunk * 128 // own, (chunk + 1) * 128 // own)
            )

    @pl.loop(0, tokens // 64)
    def _(chunk):
        part = pl.ds(pl.multiple_of(chunk * 64, 64), 64)
        rows = x_ref[part, :].astype(jnp.float32)
        inverse = lax.rsqrt(jnp.mean(rows * rows, axis=-1, keepdims=True) + NORM_EPS)
        o_rows[part, :] = (rows * inverse * gain_one[...]).astype(jnp.bfloat16)

    qkv_load(last, 0).wait()
    value = qkv_tile(0)
    qkv_load(1, 0).start()
    for group in range(KV_HEADS):
        kv_ref[group, :HD, :] = rotated(value[group * HD : (group + 1) * HD], cos, sin)
        rest = (KV_HEADS + group) * HD
        kv_ref[group, HD:, :] = value[rest : rest + HD].astype(jnp.bfloat16)
    slots[0] = kv_ref[...]
    gather.advance(0, 1)
    for tile in range(last):
        slot = (tile + 1) % 2
        qkv_load(tile, slot).wait()
        value = qkv_tile(slot)
        if tile + 2 < last:
            qkv_load(tile + 2, slot).start()
        for head in range(TILE // HD):
            rows = slice(tile * TILE + head * HD, tile * TILE + (head + 1) * HD)
            q_ref[rows, :] = rotated(value[head * HD : (head + 1) * HD], cos, sin)
        part = slice(tile * TILE, (tile + 1) * TILE)
        normed_ref[part, :] = transposed(o_rows[:, part])
    gather.hold = False
    events = [event for event in gather.events(2) if event not in gather.done]

    def proceed(count):
        for _ in range(min(count, len(events))):
            gather.advance(*events.pop(0))

    for group in range(KV_HEADS):
        proceed(2)
        send_kv([group])
    proceed(2)
    for group in range(KV_HEADS):
        k_rows[0] = transposed(kv_ref[group, :HD, :])
        for step in range(1, seq_size):

            @pl.when(seq >= step)
            def _():
                kv_copy(group, step).wait_recv()
                k_rows[step] = transposed(slots[step, group, :HD, :])

        for part in range(4):

            @pl.loop(group * SHARE + part * SHARE // 4, group * SHARE + (part + 1) * SHARE // 4)
            def _(head):
                attend_head(
                    head, seq + 1, reach, valid, q_ref, slots, group, k_rows, o_ref, full_ref, lse_ref
                )

            proceed(1)
    for step in range(seq_size):

        @pl.when(seq >= step)
        def _():
            kv_all_ref[step] = slots[step]

        @pl.when(seq < step)
        def _():
            kv_all_ref[step] = jnp.zeros_like(kv_ref)

    for group in range(KV_HEADS):
        for step in range(1, seq_size):

            @pl.when(seq + step < seq_size)
            def _():
                kv_copy(group, step).wait_send()

    chunks = model // TILE

    def w_load(chunk):
        return pltpu.make_async_copy(
            fulls[0].at[:, pl.ds(chunk * TILE, TILE)], w_buf.at[chunk % 2], w_sems.at[chunk % 2]
        )

    while (1, gather.bits) not in gather.done:
        proceed(1)
    w_load(0).start()
    for row in range(model // TILE):
        part = slice(row * TILE, (row + 1) * TILE)
        o_rows[:, part] = transposed(o_ref[part, :])
    for chunk in range(chunks):
        w_load(chunk).wait()
        if chunk + 1 < chunks:
            w_load(chunk + 1).start()
        part = slice(chunk * TILE, (chunk + 1) * TILE)
        mid_ref[:, part] = x_ref[:, part].astype(jnp.float32) + matmul(o_rows[...], w_buf[chunk % 2])
        proceed(1)

    @pl.loop(0, tokens // 64)
    def _(chunk):
        part = pl.ds(pl.multiple_of(chunk * 64, 64), 64)
        rows = mid_ref[part, :]
        inverse = lax.rsqrt(jnp.mean(rows * rows, axis=-1, keepdims=True) + NORM_EPS)
        inner_ref[part, :] = (rows * inverse * gain_two[...]).astype(jnp.bfloat16)

    proceed(1)
    for row in range(model // TILE):
        part = slice(row * TILE, (row + 1) * TILE)
        turned_ref[part, :] = transposed(inner_ref[:, part])
    gather.finish(2)


def attend_forward(layout, rows, gains, w_qkv, kinds, shards, shapes, pieces, collective_id):
    tokens, model = rows.shape
    seq_size = lax.axis_size("seq")
    low, wide = (jnp.bfloat16, jnp.float32)
    vmem = pl.BlockSpec(memory_space=pltpu.VMEM)
    smem = pl.BlockSpec(memory_space=pltpu.SMEM)
    hbm = pl.BlockSpec(memory_space=pl.ANY)
    results = [
        ((HEADS * HD, tokens), low),
        ((HEADS * HD, tokens), low),
        ((HEADS * HD, tokens), wide),
        ((HEADS, 1, tokens), wide),
        ((seq_size, KV_HEADS, 2 * HD, tokens), low),
        ((tokens, model), wide),
        ((tokens, model), low),
        ((model, tokens), low),
        ((model, tokens), low),
        ((1, model), wide),
        ((1, model), wide),
        ((HD // 2, tokens), wide),
        ((HD // 2, tokens), wide),
    ]
    out = pl.pallas_call(
        functools.partial(attend_kernel, kinds, pieces),
        out_shape=[jax.ShapeDtypeStruct(*result) for result in results]
        + [jax.ShapeDtypeStruct(shape, low) for shape in shapes],
        in_specs=[smem] * 3 + [vmem] * 2 + [hbm] * (1 + len(shards)),
        out_specs=[vmem] * len(results) + [hbm] * len(shapes),
        scratch_shapes=[
            pltpu.VMEM((KV_HEADS, 2 * HD, tokens), low),
            pltpu.VMEM((seq_size, tokens, HD), low),
            pltpu.VMEM((seq_size, KV_HEADS, 2 * HD, tokens), low),
            pltpu.SemaphoreType.DMA((seq_size, KV_HEADS)),
            pltpu.SemaphoreType.DMA((seq_size, KV_HEADS)),
            pltpu.VMEM((tokens, model), low),
            pltpu.VMEM((2, model, TILE), low),
            pltpu.SemaphoreType.DMA((2,)),
            *gather_scratch(len(pieces)),
        ],
        compiler_params=pltpu.CompilerParams(
            collective_id=collective_id, has_side_effects=True, vmem_limit_bytes=58 * 2**20
        ),
        name="attend_forward",
    )(*layout, rows, gains, w_qkv, *shards)
    return (out[: len(results)], out[len(results) :])


def apart(index, distance, bits):
    return sum(
        lax.rem(index // (1 << bit) + distance // (1 << bit), 2) * (1 << bit) for bit in range(bits)
    )


class Scatter:
    def __init__(self, tiles, shape, refs, deliver):
        self.tiles, (self.size, self.depth, self.columns) = (tiles, shape)
        self.half = self.columns // 2
        self.deliver = deliver
        self.dp, self.seq = (lax.axis_index("dp"), lax.axis_index("seq"))
        self.dp_size, self.seq_size = (lax.axis_size("dp"), lax.axis_size("seq"))
        self.hops = self.size.bit_length() - 1
        refs = list(refs)
        self.own, self.other, self.came = (refs.pop(0), refs.pop(0), refs.pop(0))
        self.sent, self.got, self.kept = ([None], [None], [None])
        for _ in range(self.hops):
            self.sent.append(refs.pop(0))
            self.got.append(refs.pop(0))
            self.kept.append(refs.pop(0))
        self.rows, self.rows_got, self.send_sems, self.recv_sems = refs
        self.steps = tiles + self.hops + 2

    @staticmethod
    def scratch(shape):
        size, depth, columns = shape
        half = columns // 2
        hops = size.bit_length() - 1
        seq_size = lax.axis_size("seq")
        low = jnp.bfloat16
        shapes = [
            pltpu.VMEM((size, depth, columns), low),
            pltpu.VMEM((size, depth, columns), low),
            pltpu.VMEM((2, size, depth, columns), low),
        ]
        for hop in range(1, hops + 1):
            shapes.append(pltpu.VMEM((2, 2, size >> hop, depth, half), low))
            shapes.append(pltpu.VMEM((2, 2, size >> hop, depth, half), low))
            shapes.append(pltpu.VMEM((2, size >> hop, depth, half), low))
        shapes.append(pltpu.VMEM((2, 2, depth, half), low))
        shapes.append(pltpu.VMEM((2, seq_size - 1, 2, depth // seq_size, half), low))
        lanes = max(2, seq_size - 1)
        shapes.append(pltpu.SemaphoreType.DMA((hops + 2, 2, lanes)))
        shapes.append(pltpu.SemaphoreType.DMA((hops + 2, 2, lanes)))
        return shapes

    def bit(self, hop, side):
        return hop if side == 0 else self.hops + 1 - hop

    def copy(self, kind, slot, lane, src, dst, device):
        return pltpu.make_async_remote_copy(
            src_ref=src,
            dst_ref=dst,
            send_sem=self.send_sems.at[kind, slot, lane],
            recv_sem=self.recv_sems.at[kind, slot, lane],
            device_id=device,
            device_id_type=MESH,
        )

    def copies(self, kind, slot):
        if kind == 0:
            return [
                self.copy(0, slot, 0, self.other, self.came.at[slot], {"dp": flipped(self.dp, 0)})
            ]
        if kind <= self.hops:
            return [
                self.copy(
                    kind,
                    slot,
                    side,
                    self.sent[kind].at[slot, side],
                    self.got[kind].at[slot, side],
                    {"dp": flipped(self.dp, self.bit(kind, side))},
                )
                for side in range(2)
            ]
        own = self.depth // self.seq_size
        result = []
        for step in range(1, self.seq_size):
            there = lax.rem(self.seq + step, self.seq_size)
            window = pl.ds(pl.multiple_of(there * own, own), own)
            result.append(
                self.copy(
                    kind,
                    slot,
                    step - 1,
                    self.rows.at[slot, :, window, :],
                    self.rows_got.at[slot, step - 1],
                    {"seq": there},
                )
            )
        return result

    def send(self, kind, tile):
        for copy in self.copies(kind, lax.rem(tile, 2)):
            copy.start()

    def sent_before(self, kind, tile, back):
        @pl.when(tile >= back)
        def _():
            for copy in self.copies(kind, lax.rem(tile + 2 - back, 2)):
                copy.wait_send()

    def plus(self, into, one, two):
        rows = 64 if self.depth % 64 == 0 else 16

        @pl.loop(0, self.depth // rows)
        def _(chunk):
            part = pl.ds(pl.multiple_of(chunk * rows, rows), rows)
            into[part, :] = one[part, :] + two[part, :]

    def stage(self, kind, tile):
        slot = lax.rem(tile, 2)
        for copy in self.copies(kind, slot):
            copy.wait_recv()
        if kind == self.hops + 1:
            own = self.depth // self.seq_size
            window = pl.ds(pl.multiple_of(self.seq * own, own), own)
            for side in range(2):
                total = self.rows[slot, side, window, :].astype(jnp.float32)
                for step in range(self.seq_size - 1):
                    total = total + self.rows_got[slot, step, side].astype(jnp.float32)
                self.deliver(tile, side, total)
            return
        self.sent_before(kind + 1, tile, 2)
        size = self.size >> kind
        for side in range(2):
            columns = pl.ds(side * self.half, self.half)
            for block in range(size):
                if kind == 0:
                    one, two = (self.own.at[block, :, columns], self.came.at[slot, block, :, columns])
                else:
                    one, two = (self.kept[kind].at[side, block], self.got[kind].at[slot, side, block])
                if kind == self.hops:
                    into = self.rows.at[slot, side]
                elif side == 0:
                    place = self.sent if block % 2 else self.kept
                    index = (block // 2,)
                    into = place[kind + 1].at[((slot, 0) if block % 2 else (0,)) + index]
                else:
                    away = block >= size // 2
                    place = self.sent if away else self.kept
                    index = (block - size // 2 if away else block,)
                    into = place[kind + 1].at[((slot, 1) if away else (1,)) + index]
                self.plus(into, one, two)
        self.send(kind + 1, tile)

    def step(self, now, begin):
        for kind in range(self.hops + 1, -1, -1):
            tile = now - kind - 1

            @pl.when((tile >= 0) & (tile < self.tiles))
            def _():
                self.stage(kind, tile)

        @pl.when((now >= 0) & (now < self.tiles))
        def _():
            self.sent_before(0, now, 1)
            begin(now)

    def finish(self):
        for kind in range(self.hops + 2):
            for tile in range(max(0, self.tiles - (1 if kind == 0 else 2)), self.tiles):
                for copy in self.copies(kind, tile % 2):
                    copy.wait_send()


def greet():
    dp, seq = (lax.axis_index("dp"), lax.axis_index("seq"))
    dp_size, seq_size = (lax.axis_size("dp"), lax.axis_size("seq"))
    barrier = pltpu.get_barrier_semaphore()
    others = [{"seq": lax.rem(seq + step, seq_size)} for step in range(1, seq_size)]
    others += [{"dp": flipped(dp, bit)} for bit in range(dp_size.bit_length() - 1)]
    for other in others:
        pl.semaphore_signal(barrier, inc=1, device_id=other, device_id_type=MESH)
    pl.semaphore_wait(barrier, len(others))


TILE = 512


def squares_of(value):
    return sum(
        jnp.sum((part * part).reshape(-1, 8, 128), 0)
        for part in (value[:, c * 128 : (c + 1) * 128] for c in range(value.shape[1] // 128))
    )


def norm_backward_rows(rows_of, gradient, gain_ref, give):
    tokens, model = gradient.shape
    chunk_rows = 64

    def step(chunk, gain_sum):
        part = pl.ds(pl.multiple_of(chunk * chunk_rows, chunk_rows), chunk_rows)
        rows, grad = (rows_of(part), gradient[part, :])
        inverse = lax.rsqrt(jnp.mean(rows * rows, axis=-1, keepdims=True) + NORM_EPS)
        weighted = gain_ref[...] * grad
        scaled = rows * inverse
        mean = jnp.mean(weighted * rows, axis=-1, keepdims=True)
        give(part, inverse * weighted - scaled * (inverse * inverse * mean))
        return gain_sum + jnp.sum(grad * scaled, 0, keepdims=True)

    return lax.fori_loop(
        0, tokens // chunk_rows, step, jnp.zeros((1, model), jnp.float32)
    )


def mlp_kernel(
    rows_ref, turned_ref, gain_ref, grad_hbm, mid_hbm, gu_ref, down_ref, proj_ref,
    down_grad, d_mid_hbm, branch_hbm, block_out_hbm, d_out_hbm, gain_sum, sum_ref, squares,
    grad_ref, mid_ref, gu_buf, down_buf, hidden, d_gu, product, inner_ref, out_ref,
    load_sems, store_sems, out_sems, *scratch
):
    tokens, model = rows_ref.shape
    tiles = FF // TILE
    size, depth, columns = scratch[0].shape

    def deliver(tile, side, total):
        sum_ref[:, pl.ds(pl.multiple_of(side * FF + tile * TILE, TILE), TILE)] = total
        squares[...] += squares_of(total)

    scatter = Scatter(tiles, (size, depth, columns), scratch, deliver)
    bits = scatter.hops + 1

    def loads(tile, slot):
        start = pl.multiple_of(tile * TILE, TILE)
        return [
            pltpu.make_async_copy(
                gu_ref.at[:, pl.ds(start, TILE)], gu_buf.at[slot, 0], load_sems.at[slot, 0]
            ),
            pltpu.make_async_copy(
                gu_ref.at[:, pl.ds(pl.multiple_of(FF + start, TILE), TILE)],
                gu_buf.at[slot, 1],
                load_sems.at[slot, 1],
            ),
            pltpu.make_async_copy(
                down_ref.at[pl.ds(start, TILE), :], down_buf.at[slot], load_sems.at[slot, 2]
            ),
        ]

    def store(tile):
        start = pl.multiple_of(tile * TILE, TILE)
        return pltpu.make_async_copy(
            product, down_grad.at[pl.ds(start, TILE), :], store_sems.at[0]
        )

    grad_load = pltpu.make_async_copy(grad_hbm, grad_ref, store_sems.at[1])
    mid_load = pltpu.make_async_copy(mid_hbm, mid_ref, store_sems.at[2])
    d_mid_store = pltpu.make_async_copy(inner_ref, d_mid_hbm, store_sems.at[3])
    low_stores = []
    for place, result in enumerate((branch_hbm, block_out_hbm)):
        for chunk in range(model // TILE):
            low_stores.append(
                pltpu.make_async_copy(
                    gu_buf.at[0, place, pl.ds(chunk * tokens, tokens), :],
                    result.at[:, pl.ds(chunk * TILE, TILE)],
                    store_sems.at[4 + len(low_stores)],
                )
            )
    chunks = model // TILE

    def proj_load(chunk):
        rows = pl.ds(chunk * TILE, TILE)
        return pltpu.make_async_copy(
            proj_ref.at[rows, :], down_buf.at[chunk % 2], out_sems.at[0, chunk % 2]
        )

    def d_out_store(chunk):
        return pltpu.make_async_copy(
            product.at[:, pl.ds(chunk * tokens, tokens)],
            d_out_hbm.at[pl.ds(chunk * TILE, TILE), :],
            out_sems.at[1, chunk],
        )

    grad_load.start()
    mid_load.start()
    squares[...] = jnp.zeros_like(squares)
    for copy in loads(0, 0):
        copy.start()
    inner_ref[...] = jnp.zeros_like(inner_ref)
    out_ref[...] = jnp.zeros_like(out_ref)
    greet()
    grad_load.wait()

    def begin(tile):
        slot = lax.rem(tile, 2)
        for copy in loads(tile, slot):
            copy.wait()

        @pl.when(tile + 1 < tiles)
        def _():
            for copy in loads(tile + 1, 1 - slot):
                copy.start()

        chunk_rows = min(256, tokens)

        @pl.loop(0, tokens // chunk_rows)
        def _(chunk):
            part = pl.ds(pl.multiple_of(chunk * chunk_rows, chunk_rows), chunk_rows)
            rows = rows_ref[part, :]
            gate = matmul(rows, gu_buf[slot, 0])
            up = matmul(rows, gu_buf[slot, 1])
            d_hidden = contract(grad_ref[part, :], down_buf[slot], 1, 1)
            sigmoid_gate = 1.0 / (1.0 + jnp.exp(-gate))
            silu = gate * sigmoid_gate
            hidden[part, :] = (silu * up).astype(jnp.bfloat16)
            d_gate = d_hidden * up * sigmoid_gate * (1.0 + gate * (1.0 - sigmoid_gate))
            d_gu[part, :TILE] = d_gate.astype(jnp.bfloat16)
            d_gu[part, TILE:] = (d_hidden * silu).astype(jnp.bfloat16)

        def blocks_of(core, into):
            @pl.loop(0, size)
            def _(block):
                owner = apart(scatter.dp, 2 * block + core, bits)
                part = pl.ds(pl.multiple_of(owner * depth, depth), depth)
                into[block] = matmul(turned_ref[part, :], d_gu[...]).astype(jnp.bfloat16)

        blocks_of(1, scatter.other)
        scatter.send(0, tile)
        blocks_of(0, scatter.own)

        @pl.when(tile >= 1)
        def _():
            store(tile - 1).wait()

        hidden_turned = transposed(hidden[...])

        @pl.loop(0, model // TILE)
        def _(chunk):
            part = pl.ds(pl.multiple_of(chunk * TILE, TILE), TILE)
            inner_ref[:, part] += contract(d_gu[:, :TILE], gu_buf[slot, 0, part, :], 1, 1) + contract(
                d_gu[:, TILE:], gu_buf[slot, 1, part, :], 1, 1
            )
            out_ref[:, part] += matmul(hidden[...], down_buf[slot, :, part])
            product[:, part] = matmul(hidden_turned, grad_ref[:, part]).astype(jnp.bfloat16)

        store(tile).start()

    def give(part, back):
        start, count = (part.start, part.size)
        d_mid = grad_ref[part, :].astype(jnp.float32) + back
        inner_ref[part, :] = d_mid
        block_out = mid_ref[part, :] + out_ref[part, :]
        for chunk in range(model // TILE):
            columns = slice(chunk * TILE, (chunk + 1) * TILE)
            rows = pl.ds(pl.multiple_of(chunk * tokens + start, count), count)
            gu_buf[0, 0, rows, :] = d_mid[:, columns].astype(jnp.bfloat16)
            gu_buf[0, 1, rows, :] = block_out[:, columns].astype(jnp.bfloat16)

    @pl.loop(0, scatter.steps)
    def _(now):
        scatter.step(now, begin)

        @pl.when(now == tiles)
        def _():
            mid_load.wait()
            gain_sum[...] = norm_backward_rows(
                lambda part: mid_ref[part, :], inner_ref, gain_ref, give
            )
            d_mid_store.start()
            for copy in low_stores:
                copy.start()
            for chunk in range(2):
                proj_load(chunk).start()

        @pl.when(now == tiles + 1)
        def _():
            store(tiles - 1).wait()
            for chunk in range(chunks):
                proj_load(chunk).wait()
                product[:, chunk * tokens : (chunk + 1) * tokens] = sum(
                    contract(
                        down_buf[chunk % 2, :, part * TILE : (part + 1) * TILE],
                        gu_buf[0, 0, part * tokens : (part + 1) * tokens, :],
                        1,
                        1,
                    )
                    for part in range(chunks)
                ).astype(jnp.bfloat16)
                d_out_store(chunk).start()
                if chunk + 2 < chunks:
                    proj_load(chunk + 2).start()

    d_mid_store.wait()
    for copy in low_stores:
        copy.wait()
    for chunk in range(chunks):
        d_out_store(chunk).wait()
    scatter.finish()


def feed_forward(rows, turned, gain, grad, mid, w_gu, w_down, w_out, collective_id):
    tokens, model = rows.shape
    dp_size, seq_size = (lax.axis_size("dp"), lax.axis_size("seq"))
    shape = (dp_size // 2, model // dp_size, 2 * TILE)
    vmem = pl.BlockSpec(memory_space=pltpu.VMEM)
    hbm = pl.BlockSpec(memory_space=pl.ANY)
    return pl.pallas_call(
        mlp_kernel,
        out_shape=[
            jax.ShapeDtypeStruct((FF, model), jnp.bfloat16),
            jax.ShapeDtypeStruct((tokens, model), jnp.float32),
            jax.ShapeDtypeStruct((tokens, model), jnp.bfloat16),
            jax.ShapeDtypeStruct((tokens, model), jnp.bfloat16),
            jax.ShapeDtypeStruct((model, tokens), jnp.bfloat16),
            jax.ShapeDtypeStruct((1, model), jnp.float32),
            jax.ShapeDtypeStruct((model // (dp_size * seq_size), 2 * FF), jnp.float32),
            jax.ShapeDtypeStruct((8, 128), jnp.float32),
        ],
        in_specs=[vmem, vmem, vmem, hbm, hbm, hbm, hbm, hbm],
        out_specs=[hbm, hbm, hbm, hbm, hbm, vmem, vmem, vmem],
        scratch_shapes=[
            pltpu.VMEM((tokens, model), jnp.bfloat16),
            pltpu.VMEM((tokens, model), jnp.float32),
            pltpu.VMEM((2, 2, model, TILE), jnp.bfloat16),
            pltpu.VMEM((2, TILE, model), jnp.bfloat16),
            pltpu.VMEM((tokens, TILE), jnp.bfloat16),
            pltpu.VMEM((tokens, 2 * TILE), jnp.bfloat16),
            pltpu.VMEM((TILE, model), jnp.bfloat16),
            pltpu.VMEM((tokens, model), jnp.float32),
            pltpu.VMEM((tokens, model), jnp.float32),
            pltpu.SemaphoreType.DMA((2, 3)),
            pltpu.SemaphoreType.DMA((4 + 2 * model // TILE,)),
            pltpu.SemaphoreType.DMA((2, model // TILE)),
            *Scatter.scratch(shape),
        ],
        compiler_params=pltpu.CompilerParams(
            collective_id=collective_id, has_side_effects=True, vmem_limit_bytes=60 * 2**20
        ),
        name="feed_forward",
    )(rows, turned, gain, grad, mid, w_gu, w_down, w_out)


def load_tile(scatter, source, load_sems):
    def copies(tile):
        columns = pl.ds(
            pl.multiple_of(tile * scatter.columns, scatter.columns), scatter.columns
        )
        result = []
        for block in (*range(1, 2 * scatter.size, 2), *range(0, 2 * scatter.size, 2)):
            owner = apart(scatter.dp, block, scatter.hops + 1)
            into = scatter.other if block % 2 else scatter.own
            result.append(
                pltpu.make_async_copy(
                    source.at[owner, :, columns], into.at[block // 2], load_sems.at[block]
                )
            )
        return result

    def begin(tile):
        for copy in copies(tile):
            copy.start()

    def complete(now):
        @pl.when((now >= 0) & (now < scatter.tiles))
        def _():
            for copy in copies(now)[: scatter.size]:
                copy.wait()
            scatter.send(0, now)

    def settle_own(now):
        @pl.when((now >= 0) & (now < scatter.tiles))
        def _():
            for copy in copies(now)[scatter.size :]:
                copy.wait()

    return (begin, complete, settle_own)


def delivered(ref, columns, squares):
    def deliver(tile, side, total):
        start = pl.multiple_of(tile * columns + side * (columns // 2), columns // 2)
        ref[:, pl.ds(start, columns // 2)] = total
        squares[...] += squares_of(total)

    return deliver


def backward_kernel(
    lengths, counts, segments,
    q_ref, kv_ref, full_ref, lse_ref, do_ref, o_ref, branch_ref, cos_ref, sin_ref, squares_in, down_ref,
    d_qkv_ref, down_sum, proj_sum, squares,
    k_rows, v_rows, dk_acc, dv_acc, dkv_ref, turned, parts, parts_got, part_sends, part_recvs, load_sems, *scratch
):
    tokens = q_ref.shape[1]
    _, reach, valid = token_layout(tokens, lengths, counts, segments)
    count = len(scratch) // 2
    down = Scatter(
        down_ref.shape[2] // scratch[0].shape[2],
        scratch[0].shape,
        scratch[:count],
        delivered(down_sum, scratch[0].shape[2], squares),
    )
    proj = Scatter(
        branch_ref.shape[1] // scratch[count].shape[2],
        scratch[count].shape,
        scratch[count:],
        delivered(proj_sum, scratch[count].shape[2], squares),
    )
    seq, seq_size = (down.seq, down.seq_size)
    blocks = seq + 1
    squares[...] = squares_in[...]
    greet()

    def unrotated(value):
        first, second = (value[: HD // 2], value[HD // 2 :])
        cos, sin = (cos_ref[...], sin_ref[...])
        return jnp.concatenate(
            [first * cos + second * sin, second * cos - first * sin], 0
        ).astype(jnp.bfloat16)

    def part_copy(group, dist):
        return pltpu.make_async_remote_copy(
            src_ref=parts.at[dist, group],
            dst_ref=parts_got.at[dist, group],
            send_sem=part_sends.at[dist, group],
            recv_sem=part_recvs.at[dist, group],
            device_id={"seq": lax.rem(seq + seq_size - dist, seq_size)},
            device_id_type=MESH,
        )

    def one_head(head):
        group = head // SHARE
        rows = pl.ds(pl.multiple_of(head * HD, HD), HD)

        @pl.when(lax.rem(head, SHARE) == 0)
        def _():
            dk_acc[...] = jnp.zeros_like(dk_acc)
            dv_acc[...] = jnp.zeros_like(dv_acc)

            @pl.loop(0, blocks)
            def _(dist):
                k_rows[dist] = transposed(kv_ref[dist, group, :HD, :])
                v_rows[dist] = transposed(kv_ref[dist, group, HD:, :])

        query, grad = (q_ref[rows, :], do_ref[rows, :])
        query_rows, grad_rows = (transposed(query), transposed(grad))
        lse = lse_ref[head]
        centre = jnp.sum(grad.astype(jnp.float32) * full_ref[rows, :], 0, keepdims=True)

        def block(dist, mask):
            scores = matmul(k_rows[dist], query) * (SCORE_SCALE * LOG2E)
            prob = jnp.where(mask, jnp.exp2(scores - lse), 0.0)
            d_prob = matmul(v_rows[dist], grad)
            d_score = (prob * (d_prob - centre) * SCORE_SCALE).astype(jnp.bfloat16)
            dv_acc[dist] += matmul(prob.astype(jnp.bfloat16), grad_rows)
            dk_acc[dist] += matmul(d_score, query_rows)
            return matmul(kv_ref[dist, group, :HD, :], d_score)

        d_query = block(0, causal(tokens, valid))
        d_query = lax.fori_loop(
            1, blocks, lambda dist, acc: acc + block(dist, dist < reach), d_query
        )
        turned[rows, :] = unrotated(d_query)

        @pl.when(lax.rem(head, SHARE) == SHARE - 1)
        def _():
            dkv_ref[group, :HD, :] = dk_acc[0].T
            dkv_ref[group, HD:, :] = dv_acc[0].T
            for dist in range(1, seq_size):

                @pl.when(seq >= dist)
                def _():
                    parts[dist, group, :HD, :] = dk_acc[dist].T.astype(jnp.bfloat16)
                    parts[dist, group, HD:, :] = dv_acc[dist].T.astype(jnp.bfloat16)
                    part_copy(group, dist).start()

    def settle():
        for dist in range(1, seq_size):

            @pl.when(seq + dist < seq_size)
            def _():
                for group in range(KV_HEADS):
                    part_copy(group, dist).wait_recv()
                dkv_ref[...] += parts_got[dist].astype(jnp.float32)

            @pl.when(seq >= dist)
            def _():
                for group in range(KV_HEADS):
                    part_copy(group, dist).wait_send()

        for group in range(KV_HEADS):
            place = (HEADS + group) * HD
            turned[place : place + HD, :] = unrotated(dkv_ref[group, :HD, :])
            place += KV_HEADS * HD
            turned[place : place + HD, :] = dkv_ref[group, HD:, :].astype(jnp.bfloat16)
        for chunk in range(turned.shape[0] // TILE):
            part = slice(chunk * TILE, (chunk + 1) * TILE)
            d_qkv_ref[:, part] = transposed(turned[part, :])

    begin_down, complete_down, own_down = load_tile(down, down_ref, load_sems)

    def begin_proj(tile):
        columns = pl.ds(pl.multiple_of(tile * proj.columns, proj.columns), proj.columns)

        def blocks_of(core, into):
            @pl.loop(0, proj.size)
            def _(block):
                owner = apart(proj.dp, 2 * block + core, proj.hops + 1)
                part = pl.ds(pl.multiple_of(owner * proj.depth, proj.depth), proj.depth)
                into[block] = matmul(o_ref[part, :], branch_ref[:, columns]).astype(jnp.bfloat16)

        blocks_of(1, proj.other)
        proj.send(0, tile)
        blocks_of(0, proj.own)

    steps = down.steps
    lag = steps - proj.steps

    @pl.loop(0, steps)
    def _(now):
        down.step(now, begin_down)
        proj.step(now - lag, begin_proj)
        complete_down(now)

        busy, first = (down.tiles, 2)

        def heads_before(step):
            return jnp.minimum(jnp.maximum(step - first, 0), busy) * HEADS // busy

        @pl.loop(heads_before(now), heads_before(now + 1))
        def _(head):
            one_head(head)

        own_down(now)

        @pl.when(now == first + busy)
        def _():
            settle()

    down.finish()
    proj.finish()


def attend_backward(
    layout, query, kv, full, lse, grad, attended, branch, cos, sin, squares, g_down, collective_id
):
    tokens, reach = (query.shape[1], kv.shape[0])
    model = branch.shape[1]
    dp_size, seq_size = (lax.axis_size("dp"), lax.axis_size("seq"))
    width = (HEADS + 2 * KV_HEADS) * HD
    vmem = pl.BlockSpec(memory_space=pltpu.VMEM)
    hbm = pl.BlockSpec(memory_space=pl.ANY)
    down_shape = (dp_size // 2, g_down.shape[1], 256)
    proj_shape = (dp_size // 2, HEADS * HD // dp_size, 256)
    return pl.pallas_call(
        backward_kernel,
        out_shape=[
            jax.ShapeDtypeStruct((tokens, width), jnp.bfloat16),
            jax.ShapeDtypeStruct((g_down.shape[1] // seq_size, model), jnp.float32),
            jax.ShapeDtypeStruct((HEADS * HD // (dp_size * seq_size), model), jnp.float32),
            jax.ShapeDtypeStruct((8, 128), jnp.float32),
        ],
        in_specs=[pl.BlockSpec(memory_space=pltpu.SMEM)] * 3 + [vmem] * 10 + [hbm],
        out_specs=[vmem] * 4,
        scratch_shapes=[
            pltpu.VMEM((reach, tokens, HD), jnp.bfloat16),
            pltpu.VMEM((reach, tokens, HD), jnp.bfloat16),
            pltpu.VMEM((reach, tokens, HD), jnp.float32),
            pltpu.VMEM((reach, tokens, HD), jnp.float32),
            pltpu.VMEM((KV_HEADS, 2 * HD, tokens), jnp.float32),
            pltpu.VMEM((width, tokens), jnp.bfloat16),
            pltpu.VMEM((reach, KV_HEADS, 2 * HD, tokens), jnp.bfloat16),
            pltpu.VMEM((reach, KV_HEADS, 2 * HD, tokens), jnp.bfloat16),
            pltpu.SemaphoreType.DMA((reach, KV_HEADS)),
            pltpu.SemaphoreType.DMA((reach, KV_HEADS)),
            pltpu.SemaphoreType.DMA((dp_size,)),
            *Scatter.scratch(down_shape),
            *Scatter.scratch(proj_shape),
        ],
        compiler_params=pltpu.CompilerParams(
            collective_id=collective_id, has_side_effects=True, vmem_limit_bytes=60 * 2**20
        ),
        name="attend_backward",
    )(*layout, query, kv, full, lse, grad, attended, branch, cos, sin, squares, g_down)


def everyone():
    seq_size = lax.axis_size("seq")
    devices = lax.axis_size("dp") * seq_size
    me = lax.axis_index("dp") * seq_size + lax.axis_index("seq")

    def device(distance):
        other = lax.rem(me + distance, devices)
        return (other, (other // seq_size, lax.rem(other, seq_size)))

    return (me, devices, device)


def last_kernel(
    rows_ref, turned_ref, d_qkv_ref, gain_ref, mlp_gain_ref, squares_ref, w_hbm, d_mid_hbm,
    result, gains_sum, total_ref, input_grad_hbm,
    w_buf, d_normed, d_mid, gains, gains_got, mine, totals_got,
    load_sems, tile_sends, tile_recvs, *scratch
):
    tokens, model = rows_ref.shape
    size, depth, columns = scratch[0].shape
    scatter = Scatter(
        d_qkv_ref.shape[1] // columns, scratch[0].shape, scratch, delivered(result, columns, mine)
    )
    bits = scatter.hops + 1
    me, devices, device = everyone()
    own = model // devices
    chunks = model // TILE

    def w_load(chunk, slot):
        rows = pl.ds(pl.multiple_of(chunk * TILE, TILE), TILE)
        return pltpu.make_async_copy(w_hbm.at[rows, :], w_buf.at[slot], load_sems.at[slot])

    mid_load = pltpu.make_async_copy(d_mid_hbm, d_mid, load_sems.at[2])
    input_store = pltpu.make_async_copy(d_mid, input_grad_hbm, load_sems.at[3])

    def copy(kind, distance):
        other, place = device(distance)
        return pltpu.make_async_remote_copy(
            src_ref=mine if kind else gains.at[other * own // 128],
            dst_ref=(totals_got if kind else gains_got).at[distance],
            send_sem=tile_sends.at[kind, distance],
            recv_sem=tile_recvs.at[kind, distance],
            device_id=place,
            device_id_type=MESH,
        )

    mid_load.start()
    w_load(0, 0).start()
    gains[...] = jnp.zeros_like(gains)
    mine[...] = squares_ref[...]
    barrier = pltpu.get_barrier_semaphore()

    @pl.loop(1, devices)
    def _(distance):
        pl.semaphore_signal(barrier, inc=1, device_id=device(distance)[1], device_id_type=MESH)

    pl.semaphore_wait(barrier, devices - 1)

    def begin(tile):
        part_columns = pl.ds(pl.multiple_of(tile * columns, columns), columns)

        def blocks_of(core, into):
            @pl.loop(0, size)
            def _(block):
                owner = apart(scatter.dp, 2 * block + core, bits)
                part = pl.ds(pl.multiple_of(owner * depth, depth), depth)
                into[block] = matmul(turned_ref[part, :], d_qkv_ref[:, part_columns]).astype(
                    jnp.bfloat16
                )

        blocks_of(1, scatter.other)
        scatter.send(0, tile)
        blocks_of(0, scatter.own)

    def give(part, back):
        d_mid[part, :] += back

    @pl.loop(0, scatter.steps)
    def _(now):
        scatter.step(now, begin)

        @pl.when(now < chunks)
        def _():
            slot = lax.rem(now, 2)
            w_load(now, slot).wait()

            @pl.when(now + 1 < chunks)
            def _():
                w_load(now + 1, 1 - slot).start()

            part = pl.ds(pl.multiple_of(now * TILE, TILE), TILE)
            d_normed[:, part] = contract(d_qkv_ref[...], w_buf[slot], 1, 1)

        @pl.when(now == chunks)
        def _():
            mid_load.wait()
            gain_sum = norm_backward_rows(
                lambda part: rows_ref[part, :].astype(jnp.float32), d_normed, gain_ref, give
            )
            input_store.start()
            for chunk in range(model // 128):
                part = slice(chunk * 128, (chunk + 1) * 128)
                gains[chunk, 0:1, :] = gain_sum[:, part]
                gains[chunk, 1:2, :] = mlp_gain_ref[:, part]

            @pl.loop(1, devices)
            def _(distance):
                copy(0, distance).start()

    @pl.loop(1, devices)
    def _(distance):
        copy(0, distance).wait()

    lane = lax.broadcasted_iota(jnp.int32, (8, 128), 1)
    first = lax.rem(me * own, 128)
    total_gains = gains[me * own // 128] + jnp.sum(gains_got[1:], 0)
    total_gains = jnp.where((lane >= first) & (lane < first + own), total_gains, 0.0)
    gains_sum[...] = total_gains
    mine[...] += total_gains * total_gains

    @pl.loop(1, devices)
    def _(distance):
        copy(1, distance).start()

    @pl.loop(1, devices)
    def _(distance):
        copy(1, distance).wait()

    total = jnp.sum(mine[...] + jnp.sum(totals_got[1:], 0))
    total_ref[...] = jnp.full((8, 128), total, jnp.float32)
    input_store.wait()
    scatter.finish()


def last_sums(
    rows, turned, d_qkv, gain, mlp_gain, squares, weight, d_mid, columns, collective_id
):
    tokens, model = rows.shape
    dp_size, seq_size = (lax.axis_size("dp"), lax.axis_size("seq"))
    devices = dp_size * seq_size
    shape = (dp_size // 2, model // dp_size, columns)
    vmem = pl.BlockSpec(memory_space=pltpu.VMEM)
    hbm = pl.BlockSpec(memory_space=pl.ANY)
    return pl.pallas_call(
        last_kernel,
        out_shape=[
            jax.ShapeDtypeStruct((model // devices, d_qkv.shape[1]), jnp.float32),
            jax.ShapeDtypeStruct((8, 128), jnp.float32),
            jax.ShapeDtypeStruct((8, 128), jnp.float32),
            jax.ShapeDtypeStruct((tokens, model), jnp.float32),
        ],
        in_specs=[vmem] * 6 + [hbm] * 2,
        out_specs=[vmem] * 3 + [hbm],
        scratch_shapes=[
            pltpu.VMEM((2, TILE, d_qkv.shape[1]), jnp.bfloat16),
            pltpu.VMEM((tokens, model), jnp.float32),
            pltpu.VMEM((tokens, model), jnp.float32),
            pltpu.VMEM((model // 128, 8, 128), jnp.float32),
            pltpu.VMEM((devices, 8, 128), jnp.float32),
            pltpu.VMEM((8, 128), jnp.float32),
            pltpu.VMEM((devices, 8, 128), jnp.float32),
            pltpu.SemaphoreType.DMA((4,)),
            pltpu.SemaphoreType.DMA((2, devices)),
            pltpu.SemaphoreType.DMA((2, devices)),
            *Scatter.scratch(shape),
        ],
        compiler_params=pltpu.CompilerParams(
            collective_id=collective_id, has_side_effects=True, vmem_limit_bytes=56 * 2**20
        ),
        name="last_sums",
    )(rows, turned, d_qkv, gain, mlp_gain, squares, weight, d_mid)


def per_device(
    hidden_in,
    out_grad,
    seq_lengths,
    seq_counts,
    segment_ids,
    qkv_weight,
    qkv_m,
    qkv_v,
    out_weight,
    out_m,
    out_v,
    gate_up_weight,
    gate_up_m,
    gate_up_v,
    down_weight,
    down_m,
    down_v,
    norm_gains,
    gain_m,
    gain_v,
):
    tok_dev = hidden_in.shape[0]
    layout = (seq_lengths, seq_counts, segment_ids)
    devices = lax.axis_size("dp") * lax.axis_size("seq")
    own = norm_gains.shape[1]
    gain_rows = jnp.pad(norm_gains, ((0, 14), (0, 128 - own)))
    model = out_weight.shape[1]
    seq_size = lax.axis_size("seq")
    down_depth = down_weight.shape[0]
    spare = -down_depth % 16
    down_shard = jnp.pad(down_weight, ((0, spare), (0, 0))) if spare else down_weight
    early = 3 * TILE
    shards, (w_qkv, gain_rows, gu_block) = gather_all(
        [WHOLE, WHOLE, ROWS],
        [qkv_weight, gain_rows, gate_up_weight, out_weight, down_shard],
        [
            (devices * qkv_weight.shape[0], qkv_weight.shape[1]),
            (devices * 16, 128),
            (seq_size * gate_up_weight.shape[0], 2 * early),
        ],
        [
            (1, 1, ((0, 0, 128),)),
            (0, 0, ((0, 0, 512), (512, 512, 384))),
            (0, 0, ((896, 896, 384), (1280, 1280, 512))),
            (0, 0, ((1792, 1792, 384), (2176, 2176, 384))),
            (2, 2, ((0, 0, early), (FF, early, early))),
        ],
        1,
    )
    shards = [shards[3], shards[4], shards[2], gu_block]
    shapes = [(devices * shard.shape[0], shard.shape[1]) for shard in shards[:3]]
    half, quarter = (model // 2, model // 4)
    pieces = [
        (3, 2, ((0, 0, early), (early, FF, early))),
        (0, 0, ((0, 0, half), (half, half, half))),
        (1, 1, ((0, 0, quarter), (quarter, quarter, quarter))),
        (1, 1, ((half, half, quarter), (half + quarter, half + quarter, quarter))),
    ]
    for low, high in ((3, 6), (6, 9), (9, 10), (10, 11)):
        low, high = (low * TILE, high * TILE)
        pieces.append((2, 2, ((low, low, high - low), (FF + low, FF + low, high - low))))
    forward, (w_out, w_down, w_gu) = attend_forward(
        layout, hidden_in, gain_rows, w_qkv, [WHOLE, WHOLE, WHOLE, BLOCKS], shards, shapes, pieces, 2
    )
    if spare:
        w_down = w_down.reshape(devices, -1, model)[:, :down_depth].reshape(-1, model)
    query, attended, attended_full, lse, kv_all, mid_rows, inner_rows, turned = forward[:8]
    normed, gain_one, gain_two, cos, sin = forward[8:]
    g_down, d_mid, d_branch, block_out, d_attended, g_gain_two, g_gu_own, squares = feed_forward(
        inner_rows, turned, gain_two, out_grad, mid_rows, w_gu, w_down, w_out, 3
    )
    dp_size = lax.axis_size("dp")
    if spare:
        g_down = jnp.pad(
            g_down.reshape(devices, down_depth, model), ((0, 0), (0, spare), (0, 0))
        )
    g_down = g_down.reshape(dp_size, -1, model)
    d_qkv, g_down_own, g_out_own, squares = attend_backward(
        layout, query, kv_all, attended_full, lse, d_attended,
        attended, d_branch, cos, sin, squares, g_down, 4,
    )
    g_down_own = g_down_own[:down_depth]
    g_qkv_own, g_gains_own, total_sq, input_grad = last_sums(
        hidden_in,
        normed,
        d_qkv,
        gain_one,
        g_gain_two,
        squares,
        w_qkv,
        d_mid,
        512,
        5,
    )
    place = (lax.axis_index("dp") * seq_size + lax.axis_index("seq")) * own % 128
    g_gains_own = lax.dynamic_slice(g_gains_own, (0, place), (2, own))
    grad_norm = jnp.sqrt(total_sq[0, 0])
    clip_factor = jnp.minimum(1.0, CLIP_NORM / (grad_norm + 1e-06))
    new_qkv, new_qkv_m, new_qkv_v = adam_update(
        qkv_weight, qkv_m, qkv_v, g_qkv_own, clip_factor, 0.06, WEIGHT_DECAY
    )
    new_out, new_out_m, new_out_v = adam_update(
        out_weight, out_m, out_v, g_out_own, clip_factor, 0.4, WEIGHT_DECAY
    )
    new_gu, new_gu_m, new_gu_v = adam_update(
        gate_up_weight, gate_up_m, gate_up_v, g_gu_own, clip_factor, 0.06, WEIGHT_DECAY
    )
    new_down, new_down_m, new_down_v = adam_update(
        down_weight, down_m, down_v, g_down_own, clip_factor, 0.06, WEIGHT_DECAY
    )
    new_gains, new_gain_m, new_gain_v = adam_update(
        norm_gains, gain_m, gain_v, g_gains_own, clip_factor, 0.6, 0.0
    )
    return (
        block_out,
        input_grad,
        grad_norm,
        new_qkv,
        new_qkv_m,
        new_qkv_v,
        new_out,
        new_out_m,
        new_out_v,
        new_gu,
        new_gu_m,
        new_gu_v,
        new_down,
        new_down_m,
        new_down_v,
        new_gains,
        new_gain_m,
        new_gain_v,
    )


def solution(mesh):
    in_specs = (
        P(("dp", "seq"), None),
        P(("dp", "seq"), None),
        P("dp", None),
        P("dp"),
        P("dp", None),
        P(("dp", "seq"), None),
        P(("dp", "seq"), None),
        P(("dp", "seq"), None),
        P(("dp", "seq"), None),
        P(("dp", "seq"), None),
        P(("dp", "seq"), None),
        P(("dp", "seq"), None),
        P(("dp", "seq"), None),
        P(("dp", "seq"), None),
        P(("dp", "seq"), None),
        P(("dp", "seq"), None),
        P(("dp", "seq"), None),
        P(None, ("dp", "seq")),
        P(None, ("dp", "seq")),
        P(None, ("dp", "seq")),
    )
    out_specs = (
        P(("dp", "seq"), None),
        P(("dp", "seq"), None),
        P(),
        P(("dp", "seq"), None),
        P(("dp", "seq"), None),
        P(("dp", "seq"), None),
        P(("dp", "seq"), None),
        P(("dp", "seq"), None),
        P(("dp", "seq"), None),
        P(("dp", "seq"), None),
        P(("dp", "seq"), None),
        P(("dp", "seq"), None),
        P(("dp", "seq"), None),
        P(("dp", "seq"), None),
        P(("dp", "seq"), None),
        P(None, ("dp", "seq")),
        P(None, ("dp", "seq")),
        P(None, ("dp", "seq")),
    )
    return jax.shard_map(
        per_device, mesh=mesh, in_specs=in_specs, out_specs=out_specs, check_vma=False
    )
```
